32 devices in a mesh: wide: 8 (over y, x, core), narrow: 4 (over z).
Axes of the slice: x: 2, y: 2, z: 4, core: 2. Of those that a mesh axis runs over, the one named last changes fastest.
Arguments:
- tokens: bfloat16 [16384, 768], P('wide'), may hold values from -6 to 6
- lengths: int32 [8], replicated, may hold values from 1 to 4096, 16384 in all
- masked: int32 [16384], P('wide'), may hold values 0 or 1
- attention_in: float32 [768, 2304], P('wide', 'narrow'), may hold values from -0.21875 to 0.21875
- attention_out: float32 [768, 768], P('narrow', 'wide'), may hold values from -0.875 to 0.875
- geglu_in: float32 [768, 2, 1152], P('wide', None, 'narrow'), may hold values from -0.21875 to 0.21875
- geglu_out: float32 [1152, 768], P('narrow', 'wide'), may hold values from -0.1875 to 0.1875
- gain_attention: float32 [768], P('wide'), may hold values from 0.1 to 1.9
- gain_feedforward: float32 [768], P('wide'), may hold values from 0.1 to 1.9
- out_grad: bfloat16 [16384, 768], P('wide'), may hold values from -6 to 6
Outputs:
- output: bfloat16 [16384, 768], P('wide')
- tokens_grad: float32 [16384, 768], P('wide')
- attention_in_grad: float32 [768, 2304], P('wide', 'narrow')
- attention_out_grad: float32 [768, 768], P('narrow', 'wide')
- geglu_in_grad: float32 [768, 2, 1152], P('wide', None, 'narrow')
- geglu_out_grad: float32 [1152, 768], P('narrow', 'wide')
- gain_attention_grad: float32 [768], P('wide')
- gain_feedforward_grad: float32 [768], P('wide')
The draws below stay inside these ranges and needn't reach their ends.
Inputs may be any that keep to these rules, and one draw needn't show every extreme that they name: `lengths`: lengths of the 8 documents packed one after another into the 16384 tokens; they sum to 16384, and one of them is 4096 long.
All inputs are finite; a program needn't handle non-finite values. No bound on the sum of `masked` on one device may be relied on, other than what follows from the above.
Results may differ from the reference program's by a relative error of at most 0.015.
The reference program's roundings to bfloat16 on the way count: a program that leaves them out, or rounds other values in their place, can miss the bound.
Values may be sent and summed in bfloat16 or wider, within the bound.
A program may use at most 128 MiB of HBM per device.

```python
import math
import jax
import jax.numpy as jnp
import numpy as np
from jax import lax

D = 768
HEADS = 12
HEAD_DIM = 64
FF = 1152
WINDOW = 128
TOKENS = 16384
MOST = 4096
DOCS = 8


def plant(drawn, stream_key, smallest, top_value):
    longest = drawn.shape.index(max(drawn.shape))
    spots = []
    for shift in (0, 1):
        where = [jax.random.randint(jax.random.fold_in(stream_key, axis), (), 0, length) for axis, length in enumerate(drawn.shape)]
        where[longest] = (where[longest] + shift) % drawn.shape[longest]
        spots.append(tuple(where))
    return drawn.at[spots[0]].set(smallest).at[spots[1]].set(top_value)


def raised(values, stream_key, source, target, shards_of, factor):
    def block_of(position):
        return (jnp.arange(values.shape[position]) // (values.shape[position] // shards_of)).reshape((-1,) + (1,) * (values.ndim - 1 - position))

    near = jax.random.permutation(stream_key, shards_of)[block_of(target)]
    far = (block_of(target) + shards_of // 2) % shards_of
    return jnp.where((block_of(source) == near) | (block_of(source) == far), factor * values, values)


def steps_of(rng, dims, shards, low, largest):
    def one(dim, blocks):
        steps = jax.random.uniform(jax.random.fold_in(jax.random.fold_in(rng, 6), dim), (blocks,), jnp.float32, low / len(shards), largest / len(shards))
        return jnp.repeat(jnp.exp(steps), dims[dim] // blocks).reshape((-1,) + (1,) * (len(dims) - dim - 1))

    loudness = one(*shards[0])
    for cut in shards[1:]:
        loudness = loudness * one(*cut)
    return loudness


def profile(amount, total, most, lean):
    loads = [(1 << 20) // math.isqrt(rank ** lean) + 1 for rank in range(2, amount + 1)]
    spare, given = total - most - (amount - 1), [1] * (amount - 1)
    while spare > 0:
        free = [i for i in range(amount - 1) if given[i] < most]
        whole, remaining = sum([loads[i] for i in free]), spare
        for i in free:
            addition = min(most - given[i], max(1, remaining * loads[i] // whole), spare)
            given[i] = given[i] + addition
            spare = spare - addition
    return np.array([most] + given)


def ragged_sizes(own_key, amount, total, reach, skew):
    if amount == 2:
        one = jax.random.randint(own_key, (), max(1, total - reach), min(reach, total - 1) + 1)
        return jnp.stack([one, total - one])
    tallies = jnp.asarray(profile(amount, total, reach, skew), jnp.int32)
    couples = (amount - 1) // 2
    source_of, receiver = tallies[1:1 + 2 * couples:2], tallies[2:2 + 2 * couples:2]
    room = jnp.minimum(source_of - 1, reach - receiver)
    shifted = jax.random.randint(jax.random.fold_in(own_key, 1), (couples,), 0, 1 << 20) % (room + 1)
    tallies = tallies.at[1:1 + 2 * couples:2].set(source_of - shifted).at[2:2 + 2 * couples:2].set(receiver + shifted)
    return tallies[jax.random.permutation(jax.random.fold_in(own_key, 2), amount)]


def gaussian(key, shape, deviation, bound, pieces=(), kind=jnp.bfloat16):
    level = steps_of(key, shape, pieces, -0.22, 0.18) if pieces else 1.0
    entries = jax.random.normal(key, shape, jnp.float32) * deviation * level
    return jnp.minimum(jnp.maximum(entries, -bound), bound).astype(kind)


def heavy_noise(stream_key, extent, deviation, reach, shards, heavy, kind=jnp.bfloat16):
    result = deviation * jax.random.normal(stream_key, extent, jnp.float32)
    if shards:
        result = result * steps_of(stream_key, extent, shards, -0.22, 0.18)
    return jnp.clip(raised(result, jax.random.fold_in(stream_key, 3), *heavy), -reach, reach).astype(kind)


def setup_inputs(seed: int = 0) -> dict:
    streams_of = jax.random.split(jax.random.key(seed), 11)
    tokens = gaussian(streams_of[0], (TOKENS, D), 1.0, 6.0, ((0, 8),))
    lengths = ragged_sizes(streams_of[1], DOCS, TOKENS, MOST, 2).astype(jnp.int32)
    masked = plant((jax.random.randint(streams_of[2], (TOKENS,), 0, 5) < 1).astype(jnp.int32), jax.random.fold_in(streams_of[2], 1), 0, 1)
    attention_in = gaussian(streams_of[3], (D, 3 * D), D ** -0.5, 0.21875, ((0, 8), (1, 4)), jnp.float32)
    attention_out = gaussian(streams_of[4], (D, D), (D // 16) ** -0.5, 0.875, ((0, 4), (1, 8)), jnp.float32)
    geglu_in = gaussian(streams_of[5], (D, 2, FF), D ** -0.5, 0.21875, ((0, 8), (2, 4)), jnp.float32)
    geglu_out = gaussian(streams_of[6], (FF, D), FF ** -0.5, 0.1875, ((0, 4), (1, 8)), jnp.float32)
    gain_attention = jnp.clip(1.0 + 0.18 * jax.random.normal(streams_of[7], (D,), jnp.float32), 0.1, 1.9)
    gain_feedforward = jnp.clip(1.0 + 0.18 * jax.random.normal(streams_of[8], (D,), jnp.float32), 0.1, 1.9)
    out_grad = heavy_noise(streams_of[9], (TOKENS, D), 1.0, 6.0, ((0, 8),), (0, 1, 8, 2.0))
    return dict(tokens=tokens, lengths=lengths, masked=masked, attention_in=attention_in, attention_out=attention_out, geglu_in=geglu_in, geglu_out=geglu_out, gain_attention=gain_attention, gain_feedforward=gain_feedforward, out_grad=out_grad)


EPSILON = 1e-05
THETA = 10000.0
NEG_LARGE = -1e+30

@jax.custom_vjp
def low(v):
    return lax.optimization_barrier(v.astype(jnp.bfloat16)).astype(jnp.float32)

@jax.custom_vjp
def low_back(v):
    return v

def low_keep(v):
    return (low(v), None)

def low_pass(kept, grad):
    return (grad,)

def back_keep(v):
    return (v, None)

def back_low(kept, grad):
    return (low(grad),)
low.defvjp(low_keep, low_pass)
low_back.defvjp(back_keep, back_low)

def layer_norm(values, gain):
    row_mean = lax.optimization_barrier(jnp.mean(values, axis=-1, keepdims=True))
    centred = values - row_mean
    row_var = lax.optimization_barrier(jnp.mean(centred * centred, axis=-1, keepdims=True))
    return centred * lax.rsqrt(row_var + EPSILON) * gain

def rotary(values, cosine, sine):
    half_dim = values.shape[-1] // 2
    turned = jnp.concatenate([-values[..., half_dim:], values[..., :half_dim]], axis=-1)
    return values * cosine + turned * sine

def rotary_tables(positions, head_dim):
    freq_index = jnp.arange(head_dim // 2).astype(jnp.float32)
    inverse = jnp.power(jnp.float32(THETA), -2.0 * freq_index / head_dim)
    angles = positions.astype(jnp.float32)[:, None] * inverse[None, :]
    cosine = jnp.cos(angles)
    sine = jnp.sin(angles)
    return (jnp.concatenate([cosine, cosine], axis=-1), jnp.concatenate([sine, sine], axis=-1))

def document_tables(lengths, token_index):
    doc_ends = jnp.cumsum(lengths).astype(jnp.int32)
    finished = doc_ends[None, :] <= token_index[:, None]
    doc_number = lax.optimization_barrier(jnp.sum(finished.astype(jnp.int32), axis=1)).astype(jnp.int32)
    doc_start = lax.optimization_barrier(jnp.sum(jnp.where(finished, lengths[None, :], 0), axis=1)).astype(jnp.int32)
    doc_number = jnp.where(token_index < 0, -1, doc_number).astype(jnp.int32)
    return (doc_number, (token_index - doc_start).astype(jnp.int32))

def attention(queries, keys_low, values_low, doc_number, block_rows):
    tok_count = queries.shape[0]
    half_reach = WINDOW // 2
    zero_rows = jnp.zeros((half_reach,) + keys_low.shape[1:], jnp.float32)
    keys_pad = jnp.concatenate([zero_rows, keys_low, zero_rows], 0)
    values_pad = jnp.concatenate([zero_rows, values_low, zero_rows], 0)
    edge_docs = jnp.full((half_reach,), -1, jnp.int32)
    docs_pad = jnp.concatenate([edge_docs, doc_number.astype(jnp.int32), edge_docs], 0)
    score_scale = 1.0 / math.sqrt(HEAD_DIM)

    def one_block(block_start):
        q_block = lax.dynamic_slice_in_dim(queries, block_start, block_rows, 0)
        k_block = lax.dynamic_slice_in_dim(keys_pad, block_start, block_rows + WINDOW, 0)
        v_block = lax.dynamic_slice_in_dim(values_pad, block_start, block_rows + WINDOW, 0)
        query_docs = lax.dynamic_slice_in_dim(doc_number, block_start, block_rows, 0)
        key_docs = lax.dynamic_slice_in_dim(docs_pad, block_start, block_rows + WINDOW, 0)
        gap = jnp.arange(block_rows, dtype=jnp.int32)[:, None] + half_reach - jnp.arange(block_rows + WINDOW, dtype=jnp.int32)[None, :]
        allowed = (query_docs[:, None] == key_docs[None, :]) & (gap >= -half_reach) & (gap <= half_reach)
        raw_scores = low_back(jnp.einsum('qhd,khd->hqk', q_block, k_block, precision=lax.Precision.HIGHEST)) * score_scale
        scores = jnp.where(allowed[None], raw_scores, NEG_LARGE)
        row_top = lax.optimization_barrier(jnp.max(scores, axis=-1, keepdims=True))
        weights = jnp.exp(scores - row_top)
        totals = lax.optimization_barrier(jnp.sum(weights, axis=-1, keepdims=True))
        probs = low(weights / totals)
        return jnp.einsum('hqk,khd->qhd', probs, v_block, precision=lax.Precision.HIGHEST)
    block_starts = jnp.arange(tok_count // block_rows, dtype=jnp.int32) * block_rows
    blocks_out = lax.map(jax.checkpoint(one_block), block_starts)
    return blocks_out.reshape(tok_count, queries.shape[1], queries.shape[2])

def forward(tokens_f, attention_in, attention_out, geglu_in, geglu_out, gain_attention, gain_feedforward, doc_number, positions):
    tok_count = tokens_f.shape[0]
    block_rows = math.gcd(512, tok_count)
    normed_one = low(layer_norm(tokens_f, low(gain_attention)))
    projected = low_back(jnp.dot(normed_one, low(attention_in), precision=lax.Precision.HIGHEST, preferred_element_type=jnp.float32))
    projected = projected.reshape(tok_count, HEADS, 3, HEAD_DIM)
    cosine, sine = rotary_tables(positions, HEAD_DIM)
    queries = low(rotary(projected[:, :, 0], cosine[:, None], sine[:, None]))
    keys_low = low(rotary(projected[:, :, 1], cosine[:, None], sine[:, None]))
    values_low = low(projected[:, :, 2])
    attended = attention(queries, keys_low, values_low, doc_number, block_rows)
    attended = low_back(low(attended.reshape(tok_count, HEADS * HEAD_DIM)))
    residual = tokens_f + low_back(jnp.dot(attended, low(attention_out), precision=lax.Precision.HIGHEST, preferred_element_type=jnp.float32))
    normed_two = low(layer_norm(residual, low(gain_feedforward)))
    gate_up = jnp.einsum('td,dgf->tgf', normed_two, low(geglu_in), precision=lax.Precision.HIGHEST)
    gate_part = low_back(gate_up[:, 0])
    up_part = low_back(gate_up[:, 1])
    hidden = low(jax.nn.gelu(gate_part) * up_part)
    return residual + low_back(jnp.dot(hidden, low(geglu_out), precision=lax.Precision.HIGHEST, preferred_element_type=jnp.float32))

def reference(tokens, lengths, masked, attention_in, attention_out, geglu_in, geglu_out, gain_attention, gain_feedforward, out_grad):
    tok_count = tokens.shape[0]
    token_index = jnp.arange(tok_count, dtype=jnp.int32)
    doc_number, positions = document_tables(lengths.astype(jnp.int32), token_index)
    tokens_f = tokens.astype(jnp.float32)

    def layer_fn(tok_value, w_one, w_two, w_three, w_four, gain_one, gain_two):
        return forward(tok_value, w_one, w_two, w_three, w_four, gain_one, gain_two, doc_number, positions)
    output_f, pull_back = jax.vjp(layer_fn, tokens_f, attention_in, attention_out, geglu_in, geglu_out, gain_attention, gain_feedforward)
    cotangent = out_grad.astype(jnp.float32) * masked.astype(jnp.float32)[:, None]
    grads = pull_back(cotangent)
    return (output_f.astype(jnp.bfloat16), grads[0], grads[1], grads[2], grads[3], grads[4], grads[5], grads[6])
```

```python
import math

import jax
import jax.numpy as jnp
from jax import lax
from jax.sharding import PartitionSpec as P

HEAD_DIM = 64
WINDOW = 128
HALF = WINDOW // 2
BLOCK = 128

EPSILON = 1e-05
THETA = 10000.0
NEG_LARGE = -1e30
F32 = jnp.float32
BF16 = jnp.bfloat16


def layer_norm(values, gain):
    row_mean = jnp.mean(values, axis=-1, keepdims=True)
    centred = values - row_mean
    row_var = jnp.mean(centred * centred, axis=-1, keepdims=True)
    return centred * lax.rsqrt(row_var + EPSILON) * gain


def rotary(values, cosine, sine):
    half_dim = values.shape[-1] // 2
    turned = jnp.concatenate([-values[..., half_dim:], values[..., :half_dim]], axis=-1)
    return values * cosine + turned * sine


def rotary_back(values, cosine, sine):
    half_dim = values.shape[-1] // 2
    turned = jnp.concatenate([values[..., half_dim:], -values[..., :half_dim]], axis=-1)
    return values * cosine + turned * sine


def rotary_tables(positions, head_dim):
    freq_index = jnp.arange(head_dim // 2).astype(F32)
    inverse = jnp.power(F32(THETA), -2.0 * freq_index / head_dim)
    angles = positions.astype(F32)[:, None] * inverse[None, :]
    cosine = jnp.cos(angles)
    sine = jnp.sin(angles)
    return (jnp.concatenate([cosine, cosine], axis=-1), jnp.concatenate([sine, sine], axis=-1))


def document_tables(lengths, token_index):
    doc_ends = jnp.cumsum(lengths)
    finished = doc_ends[None, :] <= token_index[:, None]
    doc_number = jnp.sum(finished.astype(jnp.int32), axis=1)
    doc_start = jnp.sum(jnp.where(finished, lengths[None, :], 0), axis=1)
    doc_number = jnp.where(token_index < 0, -1, doc_number)
    return (doc_number, token_index - doc_start)


def geglu_act(gate_part, up_part):
    return jax.nn.gelu(gate_part) * up_part


def gathered(shard, wide_axis, narrow_axis):
    whole = lax.all_gather(shard.astype(BF16), "wide", axis=wide_axis, tiled=True)
    return lax.all_gather(whole, "narrow", axis=narrow_axis, tiled=True)


def dot(a, b, dims):
    return lax.dot_general(a, b, (dims, ((), ())), preferred_element_type=F32)


def per_device(tokens, lengths, masked, attention_in, attention_out, geglu_in, geglu_out,
               gain_attention, gain_feedforward, out_grad):
    wide, narrow = lax.axis_size("wide"), lax.axis_size("narrow")
    w, n = lax.axis_index("wide"), lax.axis_index("narrow")
    tok_rows, width = tokens.shape
    rows = tok_rows // narrow
    all_rows = rows + WINDOW
    heads = attention_in.shape[1] * narrow // (3 * HEAD_DIM)
    scale = 1.0 / math.sqrt(HEAD_DIM)

    w_in = gathered(attention_in, 0, 1)
    w_out = gathered(attention_out, 1, 0)
    w_gin = gathered(geglu_in, 0, 2)
    w_gout = gathered(geglu_out, 1, 0)
    gains = lax.all_gather(jnp.stack([gain_attention, gain_feedforward]).astype(BF16), "wide", axis=1, tiled=True).astype(F32)

    up = [(i, i + 1) for i in range(wide - 1)]
    down = [(i + 1, i) for i in range(wide - 1)]
    low = lax.ppermute(tokens[tok_rows - HALF:], "wide", up)
    high = lax.ppermute(tokens[:HALF], "wide", down)
    tokens_ext = jnp.concatenate([low, tokens, high], 0)
    mine_ext = lax.dynamic_slice_in_dim(tokens_ext, n * rows, all_rows, 0)
    token_index = w * tok_rows + n * rows - HALF + jnp.arange(all_rows, dtype=jnp.int32)
    doc_number, positions = document_tables(lengths, token_index)
    cosine, sine = rotary_tables(positions, HEAD_DIM)
    cosine, sine = cosine[:, None], sine[:, None]
    out_cot = (lax.dynamic_slice_in_dim(out_grad, n * rows, rows, 0).astype(F32)
               * lax.dynamic_slice_in_dim(masked, n * rows, rows, 0).astype(F32)[:, None])
    x_all = mine_ext.astype(F32)
    x = x_all[HALF:HALF + rows]

    n1_all = layer_norm(x_all, gains[0]).astype(BF16)
    _, norm_one_pull = jax.vjp(layer_norm, x, gains[0])
    n1 = n1_all[HALF:HALF + rows]
    projected = dot(n1_all, w_in, ((1,), (0,))).reshape(all_rows, heads, 3, HEAD_DIM)
    queries = rotary(projected[HALF:HALF + rows, :, 0], cosine[HALF:HALF + rows], sine[HALF:HALF + rows]).astype(BF16)
    keys = rotary(projected[:, :, 1], cosine, sine).astype(BF16)
    values = projected[:, :, 2].astype(BF16)

    blocks = rows // BLOCK
    q = queries.reshape(blocks, BLOCK, heads, HEAD_DIM)

    def windows(a):
        return jnp.stack([a[i * BLOCK:i * BLOCK + BLOCK + WINDOW] for i in range(blocks)])

    k, v, kd = windows(keys), windows(values), windows(doc_number)
    qd = doc_number[HALF:HALF + rows].reshape(blocks, BLOCK)
    gap = (jnp.arange(BLOCK, dtype=jnp.int32)[:, None] + HALF
           - jnp.arange(BLOCK + WINDOW, dtype=jnp.int32)[None, :])
    allowed = (qd[:, :, None] == kd[:, None, :]) & (jnp.abs(gap) <= HALF)
    scores = jnp.einsum("bqhd,bkhd->bhqk", q, k, preferred_element_type=F32) * scale
    scores = jnp.where(allowed[:, None], scores, NEG_LARGE)
    top = jnp.max(scores, axis=-1, keepdims=True)
    weights = jnp.exp(scores - top)
    probs = weights / jnp.sum(weights, axis=-1, keepdims=True)
    probs_low = probs.astype(BF16)
    attended = jnp.einsum("bhqk,bkhd->bqhd", probs_low, v, preferred_element_type=F32).reshape(rows, heads * HEAD_DIM).astype(BF16)
    residual = x + dot(attended, w_out, ((1,), (0,)))
    n2_f, norm_two_pull = jax.vjp(layer_norm, residual, gains[1])
    n2 = n2_f.astype(BF16)
    gate = dot(n2, w_gin[:, 0], ((1,), (0,)))
    up_part = dot(n2, w_gin[:, 1], ((1,), (0,)))
    hidden_f, geglu_pull = jax.vjp(geglu_act, gate, up_part)
    hidden = hidden_f.astype(BF16)
    output = (residual + dot(hidden, w_gout, ((1,), (0,)))).astype(BF16)
    output = lax.all_gather(output, "narrow", axis=0, tiled=True)

    cot_low = out_cot.astype(BF16)
    geglu_out_grad = dot(hidden, cot_low, ((0,), (0,)))
    hidden_grad = dot(cot_low, w_gout, ((1,), (1,)))
    gate_grad, up_grad = geglu_pull(hidden_grad)
    gate_grad, up_grad = gate_grad.astype(BF16), up_grad.astype(BF16)
    geglu_in_grad = jnp.stack([dot(n2, gate_grad, ((0,), (0,))), dot(n2, up_grad, ((0,), (0,)))], axis=1)
    n2_grad = dot(gate_grad, w_gin[:, 0], ((1,), (1,))) + dot(up_grad, w_gin[:, 1], ((1,), (1,)))
    residual_norm_grad, gain_two_grad = norm_two_pull(n2_grad)
    residual_grad = out_cot + residual_norm_grad
    residual_low = residual_grad.astype(BF16)
    attention_out_grad = dot(attended, residual_low, ((0,), (0,)))
    attended_grad = dot(residual_low, w_out, ((1,), (1,))).astype(BF16).reshape(blocks, BLOCK, heads, HEAD_DIM)

    v_grad = jnp.einsum("bhqk,bqhd->bkhd", probs_low, attended_grad, preferred_element_type=F32)
    p_grad = jnp.einsum("bqhd,bkhd->bhqk", attended_grad, v, preferred_element_type=F32)
    row_dot = jnp.sum(probs * p_grad, axis=-1, keepdims=True)
    s_grad = (probs * (p_grad - row_dot) * scale).astype(BF16)
    q_grad = jnp.einsum("bhqk,bkhd->bqhd", s_grad, k, preferred_element_type=F32).reshape(rows, heads, HEAD_DIM)
    k_grad = jnp.einsum("bhqk,bqhd->bkhd", s_grad, q, preferred_element_type=F32)

    def overlapped(a):
        total = jnp.zeros((all_rows, heads, HEAD_DIM), F32)
        for i in range(blocks):
            total = total + jnp.pad(a[i], ((i * BLOCK, all_rows - i * BLOCK - BLOCK - WINDOW), (0, 0), (0, 0)))
        return total

    pair = jnp.stack([overlapped(k_grad), overlapped(v_grad)], axis=1)
    devices = wide * narrow
    up_all = [(i, i + 1) for i in range(devices - 1)]
    down_all = [(i + 1, i) for i in range(devices - 1)]
    from_low = lax.ppermute(pair[all_rows - HALF:].astype(BF16), ("wide", "narrow"), up_all).astype(F32)
    from_high = lax.ppermute(pair[:HALF].astype(BF16), ("wide", "narrow"), down_all).astype(F32)
    own = pair[HALF:HALF + rows]
    own = own + jnp.concatenate([from_low, jnp.zeros((rows - WINDOW,) + own.shape[1:], F32), from_high], 0)
    c_own, s_own = cosine[HALF:HALF + rows], sine[HALF:HALF + rows]
    projected_grad = jnp.stack([rotary_back(q_grad, c_own, s_own), rotary_back(own[:, 0], c_own, s_own), own[:, 1]], axis=2)
    projected_grad = projected_grad.reshape(rows, 3 * heads * HEAD_DIM).astype(BF16)
    attention_in_grad = dot(n1, projected_grad, ((0,), (0,)))
    n1_grad = dot(projected_grad, w_in, ((1,), (1,)))
    tokens_norm_grad, gain_one_grad = norm_one_pull(n1_grad)
    tokens_grad = (residual_grad + tokens_norm_grad).astype(BF16)
    tokens_grad = lax.all_gather(tokens_grad, "narrow", axis=0, tiled=True).astype(F32)

    def scattered(grad, wide_axis, narrow_axis):
        part = lax.psum_scatter(grad.astype(BF16), "narrow", scatter_dimension=narrow_axis, tiled=True)
        return lax.psum_scatter(part, "wide", scatter_dimension=wide_axis, tiled=True).astype(F32)

    gain_sums = lax.psum_scatter(lax.psum(jnp.stack([gain_one_grad, gain_two_grad]), "narrow"), "wide", scatter_dimension=1, tiled=True)
    return (output, tokens_grad,
            scattered(attention_in_grad, 0, 1), scattered(attention_out_grad, 1, 0),
            scattered(geglu_in_grad, 0, 2), scattered(geglu_out_grad, 1, 0),
            gain_sums[0], gain_sums[1])


def solution(mesh):
    return jax.shard_map(
        per_device,
        mesh=mesh,
        in_specs=(P("wide", None), P(), P("wide"), P("wide", "narrow"), P("narrow", "wide"),
                  P("wide", None, "narrow"), P("narrow", "wide"), P("wide"), P("wide"), P("wide", None)),
        out_specs=(P("wide", None), P("wide", None), P("wide", "narrow"), P("narrow", "wide"),
                   P("wide", None, "narrow"), P("narrow", "wide"), P("wide"), P("wide")),
        check_vma=False,
    )
```

```python
import functools
import itertools
import math

import jax
import jax.numpy as jnp
import numpy as np
from jax import lax
from jax.experimental import pallas as pl
from jax.experimental.pallas import tpu as pltpu
from jax.sharding import PartitionSpec as P

MESH = pl.DeviceIdType.MESH
HEAD_DIM = 64
WINDOW = 128
HALF = WINDOW // 2
BLOCK = 128
SPAN = BLOCK + WINDOW
GAIN_LANES = 32
EPSILON = 1e-05
THETA = 10000.0
NEG_LARGE = -1e30
F32 = jnp.float32
BF16 = jnp.bfloat16
GELU_A = math.sqrt(2.0 / math.pi)
GELU_B = 0.044715


def round_up(value, unit):
    return -(-value // unit) * unit


def dot(a, b, ca, cb):
    return lax.dot_general(a, b, (((ca,), (cb,)), ((), ())), preferred_element_type=F32)


class Sizes:
    def __init__(self, wide, narrow, tok_rows, width, heads_width, hidden, docs):
        self.W, self.N, self.T, self.D, self.F, self.docs = wide, narrow, tok_rows, width, hidden, docs
        self.R = tok_rows // narrow
        self.E = self.R + WINDOW
        self.NB = self.R // BLOCK
        self.pairs = width // 128
        self.SH = width // wide
        self.RS = round_up(self.SH, 16)
        self.QN, self.FN = heads_width // narrow, hidden // narrow
        self.bits = (wide // 2).bit_length() - 1
        first = GAIN_LANES + 3 * self.QN
        self.real = first + self.QN + 3 * self.FN
        self.LA = round_up(first, 128)
        self.lanes = round_up(self.real, 128)
        self.O0 = self.LA - first
        cut_a = (self.LA // 256) * 128
        mid = self.LA + ((self.lanes - self.LA) // 256) * 128
        self.cuts = [(0, cut_a), (cut_a, self.LA), (self.LA, mid), (mid, self.lanes)]
        self.C = len(self.cuts)
        self.CA = 2
        self.MB = min(self.R, 256)
        self.blocks = self.R // self.MB
        self.FC = 384 if hidden % 384 == 0 else hidden
        self.HT = max(1, 192 // (2 * self.SH))
        self.TM = self.HT * 2 * self.SH


def combos(bit_list):
    out = []
    for mask in range(1 << len(bit_list)):
        out.append([b for i, b in enumerate(bit_list) if mask >> i & 1])
    return out


def layer_kernel(z, names, lengths, tokens, cot, freq, pk, out, tg, gp, *scratch):
    s = dict(zip(names, scratch))
    W, N, T, D, F, R, E, NB = z.W, z.N, z.T, z.D, z.F, z.R, z.E, z.NB
    C, SH, RS, N2 = z.C, z.SH, z.RS, z.N // 2
    wb = [s[f"wb{c}"] for c in range(C)]
    r0 = [s[f"r0{c}"] for c in range(C)]
    r1 = [s[f"r1{c}"] for c in range(C)]
    rz = [s[f"rz{c}"] for c in range(C)]
    w, n = lax.axis_index("wide"), lax.axis_index("narrow")
    core, hi = lax.rem(w, 2), lax.div(w, 2)
    place = n + core * (N - 1 - 2 * n)
    ahead = 1 - 2 * core
    first, last = place == 0, place == N - 1
    has_prev = jnp.logical_or(place > 0, w > 0)
    has_next = jnp.logical_or(place < N - 1, w < W - 1)
    prev_dev = (jnp.where(first, w - 1, w), jnp.where(first, n, n - ahead))
    next_dev = (jnp.where(last, w + 1, w), jnp.where(last, n, n + ahead))
    sib_dev = (w + 1 - 2 * core, n)

    def around(k):
        return lax.rem(n + k + N, N)

    def flip(value, bit_list):
        for b in bit_list:
            value = value + (1 - 2 * lax.rem(lax.div(hi, 1 << b), 2)) * (1 << b)
        return value

    def bit_dev(b):
        return (2 * flip(hi, [b]) + core, n)

    pending = []

    def copy_to(src, dst, send, recv, dev):
        return pltpu.make_async_remote_copy(src_ref=src, dst_ref=dst, send_sem=send, recv_sem=recv, device_id=dev, device_id_type=MESH)

    def send(src, dst, send_sem, recv_sem, dev):
        c = copy_to(src, dst, send_sem, recv_sem, dev)
        c.start()
        pending.append(c)

    def arrived(dst, send_sem, recv_sem, dev):
        copy_to(dst, dst, send_sem, recv_sem, dev).wait_recv()

    barrier = pltpu.get_barrier_semaphore()
    partners = [(w, around(k)) for k in range(1, N)] + [bit_dev(b) for b in range(z.bits)] + [sib_dev]
    for dev in partners:
        pl.semaphore_signal(barrier, inc=1, device_id=dev, device_id_type=MESH)

    @pl.when(has_prev)
    def _():
        pl.semaphore_signal(barrier, inc=1, device_id=prev_dev, device_id_type=MESH)

    @pl.when(has_next)
    def _():
        pl.semaphore_signal(barrier, inc=1, device_id=next_dev, device_id_type=MESH)

    pl.semaphore_wait(barrier, len(partners) + has_prev.astype(jnp.int32) + has_next.astype(jnp.int32))

    half_refs = [pl.ds(h * N2, N2) for h in range(2)]
    gather_order = [list(range(z.bits))[::-1], list(range(z.bits))]

    def z_start(c):
        lo, up = z.cuts[c]
        src = pk.at[:, lo:up]
        pltpu.make_async_copy(src, wb[c].at[n, hi, core], s["l_own"].at[c]).start()
        for k in range(1, N):
            send(src, wb[c].at[n, hi, core], s["zs"].at[c, k - 1], s["zr"].at[c, k - 1], (w, around(k)))

    def z_wait(c):
        lo, up = z.cuts[c]
        pltpu.make_async_copy(pk.at[:, lo:up], wb[c].at[n, hi, core], s["l_own"].at[c]).wait()
        for k in range(1, N):
            arrived(wb[c].at[around(-k), hi, core], s["zs"].at[c, k - 1], s["zr"].at[c, k - 1], (w, around(-k)))

    def s_start(c, t):
        for h in range(2):
            b = gather_order[h][t]
            for i, combo in enumerate(combos(gather_order[h][:t])):
                ref = wb[c].at[half_refs[h], flip(hi, combo), core]
                slot = (1 << t) - 1 + i
                send(ref, ref, s["ss"].at[c, h, slot], s["sr"].at[c, h, slot], bit_dev(b))

    def s_wait(c, t):
        for h in range(2):
            b = gather_order[h][t]
            for i, combo in enumerate(combos(gather_order[h][:t])):
                ref = wb[c].at[half_refs[h], flip(hi, combo + [b]), core]
                slot = (1 << t) - 1 + i
                arrived(ref, s["ss"].at[c, h, slot], s["sr"].at[c, h, slot], bit_dev(b))

    def d_start(c):
        for h in range(2):
            ref = wb[c].at[half_refs[h], :, core]
            send(ref, ref, s["ds"].at[c, h], s["dr"].at[c, h], sib_dev)

    def d_wait(c):
        for h in range(2):
            arrived(wb[c].at[half_refs[h], :, 1 - core], s["ds"].at[c, h], s["dr"].at[c, h], sib_dev)

    stages = z.bits + 2

    def gather_step(t):
        for st in reversed(range(stages)):
            c = t - st
            if not 0 <= c < C:
                continue
            if st == 0:
                z_wait(c)
            elif st <= z.bits:
                s_wait(c, st - 1)
            else:
                d_wait(c)
            if st < z.bits:
                s_start(c, st)
            elif st == z.bits:
                d_start(c)

    for c in range(C):
        z_start(c)

    xin = s["xin"]
    own = pltpu.make_async_copy(tokens.at[pl.ds(pl.multiple_of(place * R, 16), R)], xin.at[pl.ds(HALF, R)], s["l_tok"].at[0])
    own.start()

    def low_copy():
        return pltpu.make_async_copy(tokens.at[pl.ds(pl.multiple_of(place * R - HALF, 16), HALF)], xin.at[pl.ds(0, HALF)], s["l_tok"].at[1])

    def high_copy():
        return pltpu.make_async_copy(tokens.at[pl.ds(pl.multiple_of(place * R + R, 16), HALF)], xin.at[pl.ds(HALF + R, HALF)], s["l_tok"].at[2])

    def halo_to_next():
        return copy_to(tokens.at[pl.ds(T - HALF, HALF)], xin.at[pl.ds(0, HALF)], s["hs"].at[0], s["hr"].at[0], (w + 1, n))

    def halo_to_prev():
        return copy_to(tokens.at[pl.ds(0, HALF)], xin.at[pl.ds(HALF + R, HALF)], s["hs"].at[1], s["hr"].at[1], (w - 1, n))

    zeros_halo = jnp.zeros((HALF, D), BF16)

    @pl.when(place > 0)
    def _():
        low_copy().start()

    @pl.when(place < N - 1)
    def _():
        high_copy().start()

    @pl.when(jnp.logical_and(last, w < W - 1))
    def _():
        halo_to_next().start()

    @pl.when(jnp.logical_and(first, w > 0))
    def _():
        halo_to_prev().start()

    @pl.when(jnp.logical_and(first, w == 0))
    def _():
        xin[0:HALF, :] = zeros_halo

    @pl.when(jnp.logical_and(last, w == W - 1))
    def _():
        xin[HALF + R:, :] = zeros_halo

    base = w * T + place * R
    ends, total = [], jnp.int32(0)
    for d in range(z.docs):
        total = total + lengths[d]
        ends.append(total)
    cos_t, sin_t, bias_t = s["cos"], s["sin"], s["bias"]
    lane = lax.broadcasted_iota(jnp.int32, (BLOCK, 128), 1)
    low_half = lax.rem(lane, HEAD_DIM) < HEAD_DIM // 2

    def table_rows(i, carry):
        r = pl.multiple_of(i * BLOCK, BLOCK)
        t = base - HALF + r + lax.broadcasted_iota(jnp.int32, (BLOCK, 128), 0)
        start = jnp.zeros((BLOCK, 128), jnp.int32)
        for d in range(z.docs):
            start = start + jnp.where(t >= ends[d], lengths[d], 0)
        angle = (t - start).astype(F32) * freq[0:1, :]
        cos_t[pl.ds(r, BLOCK), :] = jnp.cos(angle)
        sine = jnp.sin(angle)
        sin_t[pl.ds(r, BLOCK), :] = jnp.where(low_half, -sine, sine)
        return carry

    lax.fori_loop(0, E // BLOCK, table_rows, 0)

    def bias_rows(b, carry):
        tk = base - HALF + b * BLOCK + lax.broadcasted_iota(jnp.int32, (SPAN, BLOCK), 0)
        tq = base + b * BLOCK + lax.broadcasted_iota(jnp.int32, (SPAN, BLOCK), 1)
        dk = jnp.where(tk < 0, -1, 0)
        dq = jnp.zeros((SPAN, BLOCK), jnp.int32)
        for d in range(z.docs):
            dk = dk + jnp.where(tk >= ends[d], 1, 0)
            dq = dq + jnp.where(tq >= ends[d], 1, 0)
        near = jnp.abs(tk - tq) <= HALF
        bias_t[b] = jnp.where(jnp.logical_and(dk == dq, near), 0.0, NEG_LARGE).astype(F32)
        return carry

    lax.fori_loop(0, NB, bias_rows, 0)

    own.wait()

    @pl.when(place > 0)
    def _():
        low_copy().wait()

    @pl.when(place < N - 1)
    def _():
        high_copy().wait()

    @pl.when(jnp.logical_and(first, w > 0))
    def _():
        halo_to_next().wait_recv()

    @pl.when(jnp.logical_and(last, w < W - 1))
    def _():
        halo_to_prev().wait_recv()

    @pl.when(jnp.logical_and(last, w < W - 1))
    def _():
        halo_to_next().wait_send()

    @pl.when(jnp.logical_and(first, w > 0))
    def _():
        halo_to_prev().wait_send()

    a_ready = z.CA - 1 + stages - 1
    for t in range(a_ready + 1):
        gather_step(t)

    wqkv, wot, wg, wu, wgo = s["wqkv"], s["wot"], s["wg"], s["wu"], s["wgo"]
    gcol, grow, gsum = s["gcol"], s["grow"], s["gsum"]

    def shard_pair(c, nn, i):
        a, b = wb[c][nn, i, 0], wb[c][nn, i, 1]
        if SH % 16 == 0:
            return jnp.concatenate([a[:SH], b[:SH]], axis=0)
        return jnp.concatenate([a.astype(F32)[:SH], b.astype(F32)[:SH]], axis=0).astype(BF16)

    def part(lo, up, nn, i):
        return jnp.concatenate([shard_pair(c, nn, i) for c in range(lo, up)], axis=1)

    QN, FN = z.QN, z.FN

    def unpack_a(i, carry):
        r = pl.multiple_of(i * 2 * SH, 16)
        a = [part(0, z.CA, nn, i) for nn in range(N)]
        for k in range(3):
            at = GAIN_LANES + k * QN
            wqkv[pl.ds(r, 2 * SH), k * D:(k + 1) * D] = jnp.concatenate([v[:, at:at + QN] for v in a], axis=1)
        gcol[pl.ds(r, 2 * SH), :] = a[0][:, 0:128].astype(F32)
        return carry

    lax.fori_loop(0, W // 2, unpack_a, 0)
    grow[...] = gcol[...].T[0:8, :]
    gsum[...] = jnp.zeros((8, D), F32)

    def normed(x):
        centred = x - jnp.mean(x, axis=-1, keepdims=True)
        rstd = lax.rsqrt(jnp.mean(centred * centred, axis=-1, keepdims=True) + EPSILON)
        return centred * rstd, rstd

    n1, qkv = s["n1"], s["qkv"]

    def norm_rows(i, carry):
        r = pl.multiple_of(i * BLOCK, BLOCK)
        hat, _ = normed(xin[pl.ds(r, BLOCK), :].astype(F32))
        n1[pl.ds(r, BLOCK), :] = (hat * grow[0:1, :]).astype(BF16)
        return carry

    lax.fori_loop(0, E // BLOCK, norm_rows, 0)

    def partner_lanes(x):
        lanes = lax.broadcasted_iota(jnp.int32, x.shape, 1)
        return jnp.where(lax.rem(lanes, HEAD_DIM) < HEAD_DIM // 2, pltpu.roll(x, 128 - HEAD_DIM // 2, 1), pltpu.roll(x, HEAD_DIM // 2, 1))

    def project_turned(ct, carry):
        at = pl.multiple_of(ct * 128, 128)
        y = dot(n1[...], wqkv[:, pl.ds(at, 128)], 1, 0)
        y = y * cos_t[...] + partner_lanes(y) * sin_t[...]
        y = y * jnp.where(ct < D // 128, F32(1.0 / math.sqrt(HEAD_DIM)), F32(1.0))
        qkv[:, pl.ds(at, 128)] = y.astype(BF16)
        return carry

    lax.fori_loop(0, 2 * D // 128, project_turned, 0)

    def project(ct, carry):
        at = pl.multiple_of(2 * D + ct * 256, 128)
        qkv[:, pl.ds(at, 256)] = dot(n1[...], wqkv[:, pl.ds(at, 256)], 1, 0).astype(BF16)
        return carry

    lax.fori_loop(0, D // 256, project, 0)
    gather_step(a_ready + 1)

    att, stat = s["att"], s["stat"]
    lane_row = lax.broadcasted_iota(jnp.int32, (BLOCK, 128), 1)
    keep_one = jnp.where(lane_row < HEAD_DIM, 1.0, 0.0).astype(BF16)
    keep_two = jnp.where(lane_row < HEAD_DIM, 0.0, 1.0).astype(BF16)

    def stacked(x):
        return jnp.concatenate([x * keep_one, x * keep_two], axis=0)

    def unstacked(x):
        return jnp.concatenate([x[:HEAD_DIM, :BLOCK], x[HEAD_DIM:, BLOCK:]], axis=0).T

    def unit_refs(j, b):
        lanes = [pl.ds(pl.multiple_of(k * D + j * 128, 128), 128) for k in range(3)]
        return lanes, pl.ds(pl.multiple_of(b * BLOCK, BLOCK), SPAN), pl.ds(pl.multiple_of(b * BLOCK + HALF, 16), BLOCK)

    def unit_scores(j, b):
        (lq, lk, lv), keys, queries = unit_refs(j, b)
        qs = stacked(qkv[queries, lq])
        kp, vp = qkv[keys, lk], qkv[keys, lv]
        pen = bias_t[b]
        return qs, kp, vp, dot(kp, qs, 1, 1) + jnp.concatenate([pen, pen], axis=1)

    def attend(u, carry):
        j, b = lax.div(u, NB), lax.rem(u, NB)
        _, _, vp, scores = unit_scores(j, b)
        top = jnp.max(scores, axis=0, keepdims=True)
        weights = jnp.exp(scores - top)
        inv = 1.0 / jnp.sum(weights, axis=0, keepdims=True)
        stat[u, 0:1, :] = top
        stat[u, 1:2, :] = inv
        got = unstacked(dot(vp, (weights * inv).astype(BF16), 0, 0))
        att[pl.ds(pl.multiple_of(b * BLOCK, BLOCK), BLOCK), pl.ds(pl.multiple_of(j * 128, 128), 128)] = got.astype(BF16)
        return carry

    lax.fori_loop(0, z.pairs * NB, attend, 0)
    for t in range(a_ready + 2, C + stages - 1):
        gather_step(t)

    def unpack_b(i, carry):
        r = pl.multiple_of(i * 2 * SH, 16)
        a = [shard_pair(z.CA - 1, nn, i)[:, z.LA - z.O0 - z.cuts[z.CA - 1][0]:] for nn in range(N)] if z.O0 else None
        bs = [part(z.CA, C, nn, i) for nn in range(N)]
        o_rest = QN - z.O0
        wot[pl.ds(r, 2 * SH), :] = jnp.concatenate(
            [x for nn in range(N) for x in (([a[nn]] if z.O0 else []) + [bs[nn][:, :o_rest]])], axis=1)
        for k, ref in enumerate((wg, wu, wgo)):
            at = o_rest + k * FN
            ref[pl.ds(r, 2 * SH), :] = jnp.concatenate([v[:, at:at + FN] for v in bs], axis=1)
        return carry

    lax.fori_loop(0, W // 2, unpack_b, 0)

    ost, n2, res, resg = s["ost"], s["n2"], s["resr"], s["resg"]
    hid, dgate, dup, datt = s["hid"], s["dgate"], s["dup"], s["datt"]
    MB, FC = z.MB, z.FC

    def norm_back(hat, rstd, e, gain):
        eg = e * gain
        return rstd * (eg - jnp.mean(eg, axis=-1, keepdims=True) - hat * jnp.mean(eg * hat, axis=-1, keepdims=True))

    def token_copies(stage, dest, rb, key):
        src = stage.at[pl.ds(pl.multiple_of(rb * MB, 16), MB)]
        dst = dest.at[pl.ds(pl.multiple_of(place * R + rb * MB, 16), MB)]
        local = pltpu.make_async_copy(src, dst, s[key + "l"].at[rb])
        remote = [copy_to(src, dst, s[key + "s"].at[rb, k - 1], s[key + "r"].at[rb, k - 1], (w, around(k))) for k in range(1, N)]
        return local, remote

    def token_arrivals(dest, rb, key):
        for k in range(1, N):
            source = around(-k)
            theirs = source + core * (N - 1 - 2 * source)
            ref = dest.at[pl.ds(pl.multiple_of(theirs * R + rb * MB, 16), MB)]
            arrived(ref, s[key + "s"].at[rb, k - 1], s[key + "r"].at[rb, k - 1], (w, source))

    def feed(rb, carry):
        r = pl.multiple_of(rb * MB, 16)
        rows = pl.ds(r, MB)
        x = xin[pl.ds(pl.multiple_of(rb * MB + HALF, 16), MB), :].astype(F32)
        residual = x + dot(att[rows, :], wot[...], 1, 1)
        hat, rstd = normed(residual)
        gain = grow[1:2, :]
        n2v = (hat * gain).astype(BF16)
        n2[rows, :] = n2v
        cotv = cot[rows, :]
        total_out, e = residual, None
        for f in range(0, F, FC):
            gate = dot(n2v, wg[:, f:f + FC], 1, 0)
            upv = dot(n2v, wu[:, f:f + FC], 1, 0)
            dh = dot(cotv, wgo[:, f:f + FC], 1, 0)
            sq = gate * gate
            th = jnp.tanh(GELU_A * (gate * (1.0 + GELU_B * sq)))
            half = 0.5 * (1.0 + th)
            act = gate * half
            slope = half + (0.5 * GELU_A) * gate * (1.0 - th * th) * (1.0 + (3.0 * GELU_B) * sq)
            hv = (act * upv).astype(BF16)
            dgv = (dh * upv * slope).astype(BF16)
            duv = (dh * act).astype(BF16)
            hid[rows, f:f + FC] = hv
            dgate[rows, f:f + FC] = dgv
            dup[rows, f:f + FC] = duv
            total_out = total_out + dot(hv, wgo[:, f:f + FC], 1, 1)
            more = dot(dgv, wg[:, f:f + FC], 1, 1) + dot(duv, wu[:, f:f + FC], 1, 1)
            e = more if e is None else e + more
        ost[rows, :] = total_out.astype(BF16)
        local, remote = token_copies(ost, out, rb, "o")
        local.start()
        for c in remote:
            c.start()
        gsum[1:2, :] = gsum[1:2, :] + jnp.sum(e * hat, axis=0, keepdims=True)
        grad = cotv.astype(F32) + norm_back(hat, rstd, e, gain)
        resg[rows, :] = grad
        low = grad.astype(BF16)
        res[rows, :] = low
        datt[rows, :] = dot(low, wot[...], 1, 0).astype(BF16)
        return carry

    lax.fori_loop(0, z.blocks, feed, 0)

    for c in pending:
        c.wait_send()
    pending.clear()

    def store_rows(c, nn, i, k, value):
        if RS > SH:
            value = jnp.concatenate([value, jnp.zeros((RS - SH, value.shape[1]), F32)], axis=0)
        wb[c][nn, i, k] = value.astype(BF16)

    HT, TM = z.HT, z.TM
    owx = s["owx"]

    def store_part(chunks, nn, t, value):
        lo = z.cuts[chunks[0]][0]
        for c in chunks:
            a, b = z.cuts[c]
            for i in range(HT):
                for k in range(2):
                    at = (2 * i + k) * SH
                    store_rows(c, nn, t * HT + i, k, value[at:at + SH, a - lo:b - lo])

    def grads_b(t, carry):
        r = pl.multiple_of(t * TM, 16)
        cols = pl.ds(pl.multiple_of(t * TM, 128), TM) if TM % 128 == 0 else None
        gg = dot(s["n2t"][pl.ds(r, TM), :], dgate[...], 1, 0)
        gu = dot(s["n2t"][pl.ds(r, TM), :], dup[...], 1, 0)
        go = dot(s["ct"][pl.ds(r, TM), :], hid[...], 1, 0)
        gw = dot(s["rt"][pl.ds(r, TM), :], att[...], 1, 0)
        if z.O0:
            firsts = [gw[:, nn * QN:nn * QN + z.O0] for nn in range(N)]
            spare = owx.shape[1] - N * z.O0
            if spare:
                firsts.append(jnp.zeros((TM, spare), F32))
            owx[pl.ds(r, TM), :] = jnp.concatenate(firsts, axis=1)
        for nn in range(N):
            pieces = [gw[:, nn * QN + z.O0:(nn + 1) * QN]] + [v[:, nn * FN:(nn + 1) * FN] for v in (gg, gu, go)]
            if z.lanes > z.real:
                pieces.append(jnp.zeros((TM, z.lanes - z.real), F32))
            store_part(list(range(z.CA, C)), nn, t, jnp.concatenate(pieces, axis=1))
        return carry

    def transposed(dst, src, row0):
        def body(i, carry):
            at = pl.multiple_of(i * 128, 128)
            dst[pl.ds(at, 128), :] = src[row0:row0 + R, pl.ds(at, 128)].astype(F32).T.astype(BF16)
            return carry

        lax.fori_loop(0, D // 128, body, 0)

    transposed(s["n2t"], n2, 0)
    transposed(s["ct"], cot, 0)
    transposed(s["rt"], res, 0)
    lax.fori_loop(0, D // TM, grads_b, 0)

    scatter_order = [list(range(z.bits)), list(range(z.bits))[::-1]]

    def slot_base(t):
        return sum(1 << (z.bits - 1 - u) for u in range(t))

    def r0_start(c):
        send(wb[c].at[:, :, 1 - core], r0[c], s["g0s"].at[c], s["g0r"].at[c], sib_dev)

    def r0_finish(c):
        arrived(r0[c], s["g0s"].at[c], s["g0r"].at[c], sib_dev)

        def body(i, carry):
            for nn in range(N):
                wb[c][nn, i, core] = (wb[c][nn, i, core].astype(F32) + r0[c][nn, i].astype(F32)).astype(BF16)
            return carry

        lax.fori_loop(0, W // 2, body, 0)

    def r1_start(c, t):
        for h in range(2):
            b = scatter_order[h][t]
            for i, combo in enumerate(combos(scatter_order[h][t + 1:])):
                slot = slot_base(t) + i
                send(wb[c].at[half_refs[h], flip(hi, combo + [b]), core], r1[c].at[h, slot], s["g1s"].at[c, h, slot], s["g1r"].at[c, h, slot], bit_dev(b))

    def r1_finish(c, t):
        for h in range(2):
            b = scatter_order[h][t]
            for i, combo in enumerate(combos(scatter_order[h][t + 1:])):
                slot = slot_base(t) + i
                arrived(r1[c].at[h, slot], s["g1s"].at[c, h, slot], s["g1r"].at[c, h, slot], bit_dev(b))
                hv = flip(hi, combo)
                for nn in range(N2):
                    at = h * N2 + nn
                    wb[c][at, hv, core] = (wb[c][at, hv, core].astype(F32) + r1[c][h, slot, nn].astype(F32)).astype(BF16)

    def rz_start(c):
        for k in range(1, N):
            send(wb[c].at[around(k), hi, core], rz[c].at[k - 1], s["g2s"].at[c, k - 1], s["g2r"].at[c, k - 1], (w, around(k)))

    def rz_finish(c):
        total_g = wb[c][n, hi, core].astype(F32)
        for k in range(1, N):
            arrived(rz[c].at[k - 1], s["g2s"].at[c, k - 1], s["g2r"].at[c, k - 1], (w, around(-k)))
            total_g = total_g + rz[c][k - 1].astype(F32)
        lo, up = z.cuts[c]
        gp[:, lo:up] = total_g

    def scatter_advance(chunks, st):
        for c in chunks:
            if st == 0:
                r0_start(c)
            elif st == 1:
                r0_finish(c)
                if z.bits:
                    r1_start(c, 0)
                else:
                    rz_start(c)
            elif st <= z.bits + 1:
                r1_finish(c, st - 2)
                if st - 1 < z.bits:
                    r1_start(c, st - 1)
                else:
                    rz_start(c)
            else:
                rz_finish(c)

    part_a, part_b = list(range(z.CA)), list(range(z.CA, C))
    scatter_advance(part_b, 0)

    dkv, edge, rim, rimr = s["dkv"], s["edge"], s["rim"], s["rimr"]
    dk_ref, dv_ref = dkv.at[0], dkv.at[1]

    def attend_back(j, carry):
        dkv[...] = jnp.zeros((2, E, 128), F32)

        def one(b, inner):
            u = j * NB + b
            (lq, lk, lv), keys, queries = unit_refs(j, b)
            qs, kp, vp, scores = unit_scores(j, b)
            probs = jnp.exp(scores - stat[u, 0:1, :]) * stat[u, 1:2, :]
            gs = stacked(datt[pl.ds(pl.multiple_of(b * BLOCK, BLOCK), BLOCK), pl.ds(pl.multiple_of(j * 128, 128), 128)])
            prob_grad = dot(vp, gs, 1, 1)
            row_dot = jnp.sum(probs * prob_grad, axis=0, keepdims=True)
            score_grad = (probs * (prob_grad - row_dot)).astype(BF16)
            dv_ref[keys, :] = dv_ref[keys, :] + dot(probs.astype(BF16), gs, 1, 0)
            dk_ref[keys, :] = dk_ref[keys, :] + dot(score_grad, qs, 1, 0)
            dq = unstacked(dot(kp, score_grad, 0, 0)) * F32(1.0 / math.sqrt(HEAD_DIM))
            dq = dq * cos_t[queries, :] - partner_lanes(dq) * sin_t[queries, :]
            qkv[queries, lq] = dq.astype(BF16)
            return inner

        lax.fori_loop(0, NB, one, 0)
        (_, lk, lv), _, _ = unit_refs(j, 0)
        lj = pl.ds(pl.multiple_of(j * 128, 128), 128)
        for k, ref in enumerate((dk_ref, dv_ref)):
            wide_lanes = pl.ds(pl.multiple_of(k * D + j * 128, 128), 128)
            rim[0, :, wide_lanes] = ref[0:HALF, :].astype(BF16)
            rim[1, :, wide_lanes] = ref[E - HALF:, :].astype(BF16)
            edge[0, :, wide_lanes] = ref[HALF:WINDOW, :]
            edge[1, :, wide_lanes] = ref[R:R + HALF, :]
        mid = slice(HALF, HALF + R)
        dk = dk_ref[mid, :]
        qkv[mid, lk] = (dk * cos_t[mid, :] - partner_lanes(dk) * sin_t[mid, :]).astype(BF16)
        qkv[mid, lv] = dv_ref[mid, :].astype(BF16)
        return carry

    half_pairs = z.pairs // 2
    lax.fori_loop(0, half_pairs, attend_back, 0)
    scatter_advance(part_b, 1)
    lax.fori_loop(half_pairs, z.pairs, attend_back, 0)

    def rim_to_prev():
        return copy_to(rim.at[0], rimr.at[1], s["rs"].at[0], s["rr"].at[1], prev_dev)

    def rim_to_next():
        return copy_to(rim.at[1], rimr.at[0], s["rs"].at[1], s["rr"].at[0], next_dev)

    @pl.when(has_prev)
    def _():
        rim_to_prev().start()

    @pl.when(has_next)
    def _():
        rim_to_next().start()

    @pl.when(jnp.logical_not(has_prev))
    def _():
        rimr[0] = jnp.zeros((HALF, 2 * D), BF16)

    @pl.when(jnp.logical_not(has_next))
    def _():
        rimr[1] = jnp.zeros((HALF, 2 * D), BF16)

    for st in range(2, z.bits + 2):
        scatter_advance(part_b, st)

    @pl.when(has_prev)
    def _():
        rim_to_next().wait_recv()

    @pl.when(has_next)
    def _():
        rim_to_prev().wait_recv()

    @pl.when(has_prev)
    def _():
        rim_to_prev().wait_send()

    @pl.when(has_next)
    def _():
        rim_to_next().wait_send()

    for side, row in ((0, HALF), (1, R)):
        rows = slice(row, row + HALF)
        for j in range(z.pairs):
            lk = slice(j * 128, (j + 1) * 128)
            lv = slice(D + j * 128, D + (j + 1) * 128)
            dk = edge[side, :, lk] + rimr[side, :, lk].astype(F32)
            dv = edge[side, :, lv] + rimr[side, :, lv].astype(F32)
            dk = dk * cos_t[rows, :] - partner_lanes(dk) * sin_t[rows, :]
            qkv[rows, D + j * 128:D + (j + 1) * 128] = dk.astype(BF16)
            qkv[rows, 2 * D + j * 128:2 * D + (j + 1) * 128] = dv.astype(BF16)

    tst = n2

    def input_grad(rb, carry):
        rows = pl.ds(pl.multiple_of(rb * MB, 16), MB)
        ext = pl.ds(pl.multiple_of(rb * MB + HALF, 16), MB)
        e = dot(qkv[ext, :], wqkv[...], 1, 1)
        hat, rstd = normed(xin[ext, :].astype(F32))
        gsum[0:1, :] = gsum[0:1, :] + jnp.sum(e * hat, axis=0, keepdims=True)
        tst[rows, :] = (resg[rows, :] + norm_back(hat, rstd, e, grow[0:1, :])).astype(BF16)
        local, remote = token_copies(tst, tg, rb, "t")
        local.start()
        for c in remote:
            c.start()
        return carry

    lax.fori_loop(0, z.blocks, input_grad, 0)

    gcol[...] = jnp.concatenate([gsum[...], jnp.zeros((120, D), F32)], axis=0).T
    transposed(s["n2t"], n1, HALF)

    def grads_a(t, carry):
        r = pl.multiple_of(t * TM, 16)
        g = [dot(s["n2t"][pl.ds(r, TM), :], qkv[HALF:HALF + R, k * D:(k + 1) * D], 1, 0) for k in range(3)]
        gains = gcol[pl.ds(r, TM), 0:GAIN_LANES]
        for nn in range(N):
            pieces = [gains] + [v[:, nn * QN:(nn + 1) * QN] for v in g]
            if z.O0:
                pieces.append(owx[pl.ds(r, TM), nn * z.O0:(nn + 1) * z.O0])
            store_part(part_a, nn, t, jnp.concatenate(pieces, axis=1))
        return carry

    lax.fori_loop(0, D // TM, grads_a, 0)
    scatter_advance(part_a, 0)
    scatter_advance(part_b, z.bits + 2)
    for st in range(1, z.bits + 3):
        scatter_advance(part_a, st)

    def token_end(stage, dest, key):
        def body(rb, carry):
            local, remote = token_copies(stage, dest, rb, key)
            local.wait()
            for c in remote:
                c.wait_send()
            token_arrivals(dest, rb, key)
            return carry

        lax.fori_loop(0, z.blocks, body, 0)

    for c in pending:
        c.wait_send()
    token_end(ost, out, "o")
    token_end(tst, tg, "t")


def run_layer(z, lengths, tokens, cot, freq, pk):
    shapes, names = [], []

    def vmem(name, shape, dtype):
        names.append(name)
        shapes.append(pltpu.VMEM(shape, dtype))

    def sems(name, *shape):
        names.append(name)
        shapes.append(pltpu.SemaphoreType.DMA(shape))

    W, N, D, F, R, E, C = z.W, z.N, z.D, z.F, z.R, z.E, z.C
    for c, (lo, up) in enumerate(z.cuts):
        vmem(f"wb{c}", (N, W // 2, 2, z.RS, up - lo), BF16)
        vmem(f"r0{c}", (N, W // 2, z.RS, up - lo), BF16)
        vmem(f"r1{c}", (2, W // 2 - 1, N // 2, z.RS, up - lo), BF16)
        vmem(f"rz{c}", (N - 1, z.RS, up - lo), BF16)
    vmem("xin", (E, D), BF16)
    vmem("n1", (E, D), BF16)
    vmem("qkv", (E, 3 * D), BF16)
    vmem("wqkv", (D, 3 * D), BF16)
    vmem("wot", (D, D), BF16)
    for name in ("wg", "wu", "wgo"):
        vmem(name, (D, F), BF16)
    vmem("gcol", (D, 128), F32)
    vmem("grow", (8, D), F32)
    vmem("gsum", (8, D), F32)
    vmem("owx", (D, round_up(max(N * z.O0, 1), 128)), F32)
    vmem("cos", (E, 128), F32)
    vmem("sin", (E, 128), F32)
    vmem("bias", (z.NB, SPAN, BLOCK), F32)
    vmem("stat", (z.pairs * z.NB, 8, 2 * BLOCK), F32)
    for name in ("att", "ost", "n2", "resr", "datt"):
        vmem(name, (R, D), BF16)
    for name in ("n2t", "ct", "rt"):
        vmem(name, (D, R), BF16)
    vmem("resg", (R, D), F32)
    for name in ("hid", "dgate", "dup"):
        vmem(name, (R, F), BF16)
    vmem("dkv", (2, E, 128), F32)
    vmem("edge", (2, HALF, 2 * D), F32)
    vmem("rim", (2, HALF, 2 * D), BF16)
    vmem("rimr", (2, HALF, 2 * D), BF16)
    sems("l_own", C)
    sems("l_tok", 3)
    for name in ("zs", "zr", "g2s", "g2r"):
        sems(name, C, N - 1)
    for name in ("ss", "sr", "g1s", "g1r"):
        sems(name, C, 2, W // 2 - 1)
    for name in ("ds", "dr"):
        sems(name, C, 2)
    for name in ("g0s", "g0r"):
        sems(name, C)
    for name in ("hs", "hr", "rs", "rr"):
        sems(name, 2)
    for name in ("ol", "tl"):
        sems(name, z.blocks)
    for name in ("os", "or", "ts", "tr"):
        sems(name, z.blocks, N - 1)
    hbm = pl.BlockSpec(memory_space=pl.ANY)
    vm = pl.BlockSpec(memory_space=pltpu.VMEM)
    return pl.pallas_call(
        functools.partial(layer_kernel, z, names),
        out_shape=(
            jax.ShapeDtypeStruct((z.T, D), BF16),
            jax.ShapeDtypeStruct((z.T, D), BF16),
            jax.ShapeDtypeStruct((z.RS, z.lanes), F32),
        ),
        in_specs=[pl.BlockSpec(memory_space=pltpu.SMEM), hbm, vm, vm, vm],
        out_specs=(hbm, hbm, vm),
        scratch_shapes=shapes,
        compiler_params=pltpu.CompilerParams(collective_id=0, has_side_effects=True, vmem_limit_bytes=VMEM_BYTES),
    )(lengths, tokens, cot, freq, pk)


VMEM_BYTES = 64 * 1024 * 1024 - 1024 * 64


def per_device(tokens, lengths, masked, attention_in, attention_out, geglu_in, geglu_out, gain_attention, gain_feedforward, out_grad):
    wide, narrow = lax.axis_size("wide"), lax.axis_size("narrow")
    w, n = lax.axis_index("wide"), lax.axis_index("narrow")
    z = Sizes(wide, narrow, tokens.shape[0], tokens.shape[1], attention_out.shape[0] * narrow, geglu_out.shape[0] * narrow, lengths.shape[0])
    place = jnp.where(lax.rem(w, 2) == 0, n, narrow - 1 - n)
    cot = lax.dynamic_slice_in_dim(out_grad, place * z.R, z.R, 0)
    mask = lax.dynamic_slice_in_dim(masked, place * z.R, z.R, 0)
    cot = jnp.where((mask == 1)[:, None], cot, jnp.zeros((), BF16))
    heads = z.QN // HEAD_DIM
    w_in = attention_in.astype(BF16).reshape(z.SH, heads, 3, HEAD_DIM)
    gains = jnp.stack([gain_attention, gain_feedforward], axis=1).astype(BF16)
    pk = jnp.concatenate(
        [jnp.pad(gains, ((0, 0), (0, GAIN_LANES - 2)))]
        + [w_in[:, :, k].reshape(z.SH, z.QN) for k in range(3)]
        + [attention_out.astype(BF16).T, geglu_in[:, 0].astype(BF16), geglu_in[:, 1].astype(BF16), geglu_out.astype(BF16).T],
        axis=1,
    )
    pk = jnp.pad(pk, ((0, z.RS - z.SH), (0, z.lanes - z.real)))
    j = np.arange(128) % (HEAD_DIM // 2)
    freq = jnp.asarray(np.broadcast_to((THETA ** (-2.0 * j / HEAD_DIM)).astype(np.float32)[None], (8, 128)))
    out, tg, gp = run_layer(z, lengths, tokens, cot, freq, pk)
    gp = gp[: z.SH]
    at = GAIN_LANES

    def take(count):
        nonlocal at
        value = gp[:, at:at + count]
        at += count
        return value

    in_grad = jnp.stack([take(z.QN).reshape(z.SH, heads, HEAD_DIM) for _ in range(3)], axis=2).reshape(z.SH, 3 * z.QN)
    out_w_grad = take(z.QN).T
    gate_up = jnp.stack([take(z.FN), take(z.FN)], axis=1)
    down = take(z.FN).T
    return (out, tg.astype(F32), in_grad, out_w_grad, gate_up, down, gp[:, 0], gp[:, 1])


def solution(mesh):
    return jax.shard_map(
        per_device,
        mesh=mesh,
        in_specs=(P("wide", None), P(), P("wide"), P("wide", "narrow"), P("narrow", "wide"), P("wide", None, "narrow"),
                  P("narrow", "wide"), P("wide"), P("wide"), P("wide", None)),
        out_specs=(P("wide", None), P("wide", None), P("wide", "narrow"), P("narrow", "wide"), P("wide", None, "narrow"),
                   P("narrow", "wide"), P("wide"), P("wide")),
        check_vma=False,
    )
```

```python
import functools
import itertools
import math

import jax
import jax.numpy as jnp
from jax import lax
from jax.experimental import pallas as pl
from jax.experimental.pallas import tpu as pltpu
from jax.sharding import PartitionSpec as P

MESH = pl.DeviceIdType.MESH
HEAD_DIM = 64
WINDOW = 128
HALF = WINDOW // 2
BLOCK = 128
SPAN = BLOCK + WINDOW
GAIN_LANES = 32
EPSILON = 1e-05
THETA = 10000.0
NEG_LARGE = -1e30
F32 = jnp.float32
BF16 = jnp.bfloat16
GELU_A = math.sqrt(2.0 / math.pi)
GELU_B = 0.044715


def round_up(value, unit):
    return -(-value // unit) * unit


def dot(a, b, ca, cb):
    return lax.dot_general(a, b, (((ca,), (cb,)), ((), ())), preferred_element_type=F32)


class Sizes:
    def __init__(self, wide, narrow, tok_rows, width, heads_width, hidden, docs):
        self.W, self.N, self.T, self.D, self.F, self.docs = wide, narrow, tok_rows, width, hidden, docs
        self.R = tok_rows // narrow
        self.E = self.R + WINDOW
        self.NB = self.R // BLOCK
        self.pairs = width // 128
        self.G = 4 if self.NB % 4 == 0 else 1
        self.SH = width // wide
        self.RS = round_up(self.SH, 16)
        self.QN, self.FN = heads_width // narrow, hidden // narrow
        self.bits = (wide // 2).bit_length() - 1
        first = GAIN_LANES + 3 * self.QN
        self.real = first + self.QN + 3 * self.FN
        self.LA = round_up(first, 128)
        self.lanes = round_up(self.real, 128)
        self.O0 = self.LA - first
        cut_a = (self.LA // 256) * 128
        mid = self.LA + ((self.lanes - self.LA) // 256) * 128
        self.cuts = [(0, cut_a), (cut_a, self.LA), (self.LA, mid), (mid, self.lanes)]
        self.C = len(self.cuts)
        self.CA = 2
        self.MB = min(self.R, 256)
        self.blocks = self.R // self.MB
        self.FC = 384 if hidden % 384 == 0 else hidden
        self.HT = max(1, 192 // (2 * self.SH))
        self.TM = self.HT * 2 * self.SH


def combos(bit_list):
    out = []
    for mask in range(1 << len(bit_list)):
        out.append([b for i, b in enumerate(bit_list) if mask >> i & 1])
    return out


def layer_kernel(z, names, lengths, tokens, grads_in, masked, w_in, w_out, w_gu, w_down, gains, out, tg, gp, *scratch):
    s = dict(zip(names, scratch))
    W, N, T, D, F, R, E, NB = z.W, z.N, z.T, z.D, z.F, z.R, z.E, z.NB
    C, SH, RS, N2 = z.C, z.SH, z.RS, z.N // 2
    wb = [s[f"wb{c}"] for c in range(C)]
    pk, cot = s["pk"], s["cot"]
    r0 = [s[f"r0{c}"] for c in range(C)]
    r1 = [s[f"r1{c}"] for c in range(C)]
    rz = [s[f"rz{c}"] for c in range(C)]
    w, n = lax.axis_index("wide"), lax.axis_index("narrow")
    core, hi = lax.rem(w, 2), lax.div(w, 2)
    place = n + core * (N - 1 - 2 * n)
    ahead = 1 - 2 * core
    first, last = place == 0, place == N - 1
    has_prev = jnp.logical_or(place > 0, w > 0)
    has_next = jnp.logical_or(place < N - 1, w < W - 1)
    prev_dev = (jnp.where(first, w - 1, w), jnp.where(first, n, n - ahead))
    next_dev = (jnp.where(last, w + 1, w), jnp.where(last, n, n + ahead))
    sib_dev = (w + 1 - 2 * core, n)

    def around(k):
        return lax.rem(n + k + N, N)

    def flip(value, bit_list):
        for b in bit_list:
            value = value + (1 - 2 * lax.rem(lax.div(hi, 1 << b), 2)) * (1 << b)
        return value

    def bit_dev(b):
        return (2 * flip(hi, [b]) + core, n)

    pending = []

    def copy_to(src, dst, send, recv, dev):
        return pltpu.make_async_remote_copy(src_ref=src, dst_ref=dst, send_sem=send, recv_sem=recv, device_id=dev, device_id_type=MESH)

    def send(src, dst, send_sem, recv_sem, dev):
        c = copy_to(src, dst, send_sem, recv_sem, dev)
        c.start()
        pending.append(c)

    def arrived(dst, send_sem, recv_sem, dev):
        copy_to(dst, dst, send_sem, recv_sem, dev).wait_recv()

    barrier = pltpu.get_barrier_semaphore()
    partners = [(w, around(k)) for k in range(1, N)] + [bit_dev(b) for b in range(z.bits)] + [sib_dev]
    for dev in partners:
        pl.semaphore_signal(barrier, inc=1, device_id=dev, device_id_type=MESH)

    @pl.when(has_prev)
    def _():
        pl.semaphore_signal(barrier, inc=1, device_id=prev_dev, device_id_type=MESH)

    @pl.when(has_next)
    def _():
        pl.semaphore_signal(barrier, inc=1, device_id=next_dev, device_id_type=MESH)

    pl.semaphore_wait(barrier, len(partners) + has_prev.astype(jnp.int32) + has_next.astype(jnp.int32))

    half_refs = [pl.ds(h * N2, N2) for h in range(2)]
    gather_order = [list(range(z.bits))[::-1], list(range(z.bits))]

    def z_start(c):
        lo, up = z.cuts[c]
        src = pk.at[:, lo:up]
        pltpu.make_async_copy(src, wb[c].at[n, hi, core], s["l_own"].at[c]).start()
        for k in range(1, N):
            send(src, wb[c].at[n, hi, core], s["zs"].at[c, k - 1], s["zr"].at[c, k - 1], (w, around(k)))

    def z_wait(c):
        lo, up = z.cuts[c]
        pltpu.make_async_copy(pk.at[:, lo:up], wb[c].at[n, hi, core], s["l_own"].at[c]).wait()
        for k in range(1, N):
            arrived(wb[c].at[around(-k), hi, core], s["zs"].at[c, k - 1], s["zr"].at[c, k - 1], (w, around(-k)))

    def s_start(c, t):
        for h in range(2):
            b = gather_order[h][t]
            for i, combo in enumerate(combos(gather_order[h][:t])):
                ref = wb[c].at[half_refs[h], flip(hi, combo), core]
                slot = (1 << t) - 1 + i
                send(ref, ref, s["ss"].at[c, h, slot], s["sr"].at[c, h, slot], bit_dev(b))

    def s_wait(c, t):
        for h in range(2):
            b = gather_order[h][t]
            for i, combo in enumerate(combos(gather_order[h][:t])):
                ref = wb[c].at[half_refs[h], flip(hi, combo + [b]), core]
                slot = (1 << t) - 1 + i
                arrived(ref, s["ss"].at[c, h, slot], s["sr"].at[c, h, slot], bit_dev(b))

    def d_start(c):
        for h in range(2):
            ref = wb[c].at[half_refs[h], :, core]
            send(ref, ref, s["ds"].at[c, h], s["dr"].at[c, h], sib_dev)

    def d_wait(c):
        for h in range(2):
            arrived(wb[c].at[half_refs[h], :, 1 - core], s["ds"].at[c, h], s["dr"].at[c, h], sib_dev)

    stages = z.bits + 2

    def gather_step(t):
        for st in reversed(range(stages)):
            c = t - st
            if not 0 <= c < C:
                continue
            if st == 0:
                z_wait(c)
            elif st <= z.bits:
                s_wait(c, st - 1)
            else:
                d_wait(c)
            if st < z.bits:
                s_start(c, st)
            elif st == z.bits:
                d_start(c)

    def flipped(x):
        a, b = x.shape
        a2, b2 = round_up(a, 128), round_up(b, 128)
        if b2 > b:
            x = jnp.concatenate([x, jnp.zeros((a, b2 - b), F32)], axis=1)
        if a2 > a:
            x = jnp.concatenate([x, jnp.zeros((a2 - a, b2), F32)], axis=0)
        return x.T[:b, :a]

    def pack(lo, up, pieces):
        have = sum(p.shape[1] for p in pieces)
        if up - lo > have:
            pieces = pieces + [jnp.zeros((SH, up - lo - have), F32)]
        value = jnp.concatenate(pieces, axis=1)
        if RS > SH:
            value = jnp.concatenate([value, jnp.zeros((RS - SH, up - lo), F32)], axis=0)
        pk[:, lo:up] = value.astype(BF16)

    QN, FN = z.QN, z.FN
    heads = QN // HEAD_DIM
    raw_in, out_t = w_in[...], flipped(w_out[...])
    gain_cols = jnp.concatenate([flipped(gains[...]), jnp.zeros((SH, GAIN_LANES - 2), F32)], axis=1)
    pack(0, z.LA, [gain_cols] + [raw_in[:, (3 * a + k) * HEAD_DIM:(3 * a + k + 1) * HEAD_DIM] for k in range(3) for a in range(heads)] + [out_t[:, :z.O0]])
    for c in range(z.CA):
        z_start(c)
    pack(z.LA, z.lanes, [out_t[:, z.O0:], w_gu[...].astype(F32), flipped(w_down[...])])
    for c in range(z.CA, C):
        z_start(c)

    xin = s["xin"]
    own = pltpu.make_async_copy(tokens.at[pl.ds(pl.multiple_of(place * R, 16), R)], xin.at[pl.ds(HALF, R)], s["l_tok"].at[0])
    own.start()
    own_cot = pltpu.make_async_copy(grads_in.at[pl.ds(pl.multiple_of(place * R, 16), R)], cot, s["l_tok"].at[3])
    own_cot.start()

    def low_copy():
        return pltpu.make_async_copy(tokens.at[pl.ds(pl.multiple_of(place * R - HALF, 16), HALF)], xin.at[pl.ds(0, HALF)], s["l_tok"].at[1])

    def high_copy():
        return pltpu.make_async_copy(tokens.at[pl.ds(pl.multiple_of(place * R + R, 16), HALF)], xin.at[pl.ds(HALF + R, HALF)], s["l_tok"].at[2])

    def halo_to_next():
        return copy_to(tokens.at[pl.ds(T - HALF, HALF)], xin.at[pl.ds(0, HALF)], s["hs"].at[0], s["hr"].at[0], (w + 1, n))

    def halo_to_prev():
        return copy_to(tokens.at[pl.ds(0, HALF)], xin.at[pl.ds(HALF + R, HALF)], s["hs"].at[1], s["hr"].at[1], (w - 1, n))

    zeros_halo = jnp.zeros((HALF, D), BF16)

    @pl.when(place > 0)
    def _():
        low_copy().start()

    @pl.when(place < N - 1)
    def _():
        high_copy().start()

    @pl.when(jnp.logical_and(last, w < W - 1))
    def _():
        halo_to_next().start()

    @pl.when(jnp.logical_and(first, w > 0))
    def _():
        halo_to_prev().start()

    @pl.when(jnp.logical_and(first, w == 0))
    def _():
        xin[0:HALF, :] = zeros_halo

    @pl.when(jnp.logical_and(last, w == W - 1))
    def _():
        xin[HALF + R:, :] = zeros_halo

    base = w * T + place * R
    ends, total = [], jnp.int32(0)
    for d in range(z.docs):
        total = total + lengths[d]
        ends.append(total)
    cos_t, sin_t, bias_t = s["cos"], s["sin"], s["bias"]
    lane = lax.broadcasted_iota(jnp.int32, (BLOCK, 128), 1)
    low_half = lax.rem(lane, HEAD_DIM) < HEAD_DIM // 2

    freq_lane = lax.rem(lax.broadcasted_iota(jnp.int32, (1, 128), 1), HEAD_DIM // 2)
    freq = jnp.zeros((1, 128), F32)
    for d in range(HEAD_DIM // 2):
        freq = jnp.where(freq_lane == d, F32(THETA ** (-2.0 * d / HEAD_DIM)), freq)

    def table_rows(i, carry):
        r = pl.multiple_of(i * BLOCK, BLOCK)
        t = base - HALF + r + lax.broadcasted_iota(jnp.int32, (BLOCK, 128), 0)
        start = jnp.zeros((BLOCK, 128), jnp.int32)
        for d in range(z.docs):
            start = start + jnp.where(t >= ends[d], lengths[d], 0)
        angle = (t - start).astype(F32) * freq
        cos_t[pl.ds(r, BLOCK), :] = jnp.cos(angle)
        sine = jnp.sin(angle)
        sin_t[pl.ds(r, BLOCK), :] = jnp.where(low_half, -sine, sine)
        return carry

    lax.fori_loop(0, E // BLOCK, table_rows, 0)

    def bias_rows(b, carry):
        tk = base - HALF + b * BLOCK + lax.broadcasted_iota(jnp.int32, (SPAN, BLOCK), 0)
        tq = base + b * BLOCK + lax.broadcasted_iota(jnp.int32, (SPAN, BLOCK), 1)
        dk = jnp.where(tk < 0, -1, 0)
        dq = jnp.zeros((SPAN, BLOCK), jnp.int32)
        for d in range(z.docs):
            dk = dk + jnp.where(tk >= ends[d], 1, 0)
            dq = dq + jnp.where(tq >= ends[d], 1, 0)
        near = jnp.abs(tk - tq) <= HALF
        bias_t[b] = jnp.where(jnp.logical_and(dk == dq, near), 0.0, NEG_LARGE).astype(F32)
        return carry

    lax.fori_loop(0, NB, bias_rows, 0)

    own.wait()

    @pl.when(place > 0)
    def _():
        low_copy().wait()

    @pl.when(place < N - 1)
    def _():
        high_copy().wait()

    @pl.when(jnp.logical_and(first, w > 0))
    def _():
        halo_to_next().wait_recv()

    @pl.when(jnp.logical_and(last, w < W - 1))
    def _():
        halo_to_prev().wait_recv()

    @pl.when(jnp.logical_and(last, w < W - 1))
    def _():
        halo_to_next().wait_send()

    @pl.when(jnp.logical_and(first, w > 0))
    def _():
        halo_to_prev().wait_send()

    own_cot.wait()

    def mask_rows(b, carry):
        rows = pl.ds(pl.multiple_of(b * BLOCK, BLOCK), BLOCK)
        keep = jnp.where(masked[pl.ds(place * NB + b, 1), :] == 1, 1.0, 0.0).astype(F32)
        keep = jnp.broadcast_to(keep, (BLOCK, BLOCK)).T.astype(BF16)
        cot[rows, :] = cot[rows, :] * jnp.concatenate([keep] * (D // BLOCK), axis=1)
        return carry

    lax.fori_loop(0, NB, mask_rows, 0)

    def transposed(dst, src, row0):
        def body(i, carry):
            at = pl.multiple_of(i * 128, 128)
            dst[pl.ds(at, 128), :] = src[row0:row0 + R, pl.ds(at, 128)].astype(F32).T.astype(BF16)
            return carry

        lax.fori_loop(0, D // 128, body, 0)

    transposed(s["ct"], cot, 0)

    a_ready = z.CA - 1 + stages - 1
    for t in range(a_ready + 1):
        gather_step(t)

    wqkv, wot, wg, wu, wgo = s["wqkv"], s["wot"], s["wg"], s["wu"], s["wgo"]
    gcol, grow, gsum = s["gcol"], s["grow"], s["gsum"]

    def shard_pair(c, nn, i):
        a, b = wb[c][nn, i, 0], wb[c][nn, i, 1]
        if SH % 16 == 0:
            return jnp.concatenate([a[:SH], b[:SH]], axis=0)
        return jnp.concatenate([a.astype(F32)[:SH], b.astype(F32)[:SH]], axis=0).astype(BF16)

    def part(lo, up, nn, i):
        return jnp.concatenate([shard_pair(c, nn, i) for c in range(lo, up)], axis=1)

    def unpack_a(i, carry):
        r = pl.multiple_of(i * 2 * SH, 16)
        a = [part(0, z.CA, nn, i) for nn in range(N)]
        for k in range(3):
            at = GAIN_LANES + k * QN
            wqkv[pl.ds(r, 2 * SH), k * D:(k + 1) * D] = jnp.concatenate([v[:, at:at + QN] for v in a], axis=1)
        gcol[pl.ds(r, 2 * SH), :] = a[0][:, 0:128].astype(F32)
        return carry

    lax.fori_loop(0, W // 2, unpack_a, 0)
    grow[...] = gcol[...].T[0:8, :]
    gsum[...] = jnp.zeros((8, D), F32)

    def normed(x):
        centred = x - jnp.mean(x, axis=-1, keepdims=True)
        rstd = lax.rsqrt(jnp.mean(centred * centred, axis=-1, keepdims=True) + EPSILON)
        return centred * rstd, rstd

    n1, qkv = s["n1"], s["qkv"]

    def norm_rows(i, carry):
        r = pl.multiple_of(i * BLOCK, BLOCK)
        hat, _ = normed(xin[pl.ds(r, BLOCK), :].astype(F32))
        n1[pl.ds(r, BLOCK), :] = (hat * grow[0:1, :]).astype(BF16)
        return carry

    lax.fori_loop(0, E // BLOCK, norm_rows, 0)

    def partner_lanes(x):
        lanes = lax.broadcasted_iota(jnp.int32, x.shape, 1)
        return jnp.where(lax.rem(lanes, HEAD_DIM) < HEAD_DIM // 2, pltpu.roll(x, 128 - HEAD_DIM // 2, 1), pltpu.roll(x, HEAD_DIM // 2, 1))

    def project_turned(ct, carry):
        at = pl.multiple_of(ct * 256, 128)
        y = dot(n1[...], wqkv[:, pl.ds(at, 256)], 1, 0)
        scale = jnp.where(ct < D // 256, F32(1.0 / math.sqrt(HEAD_DIM)), F32(1.0))
        for k in range(2):
            part_y = y[:, k * 128:(k + 1) * 128]
            part_y = (part_y * cos_t[...] + partner_lanes(part_y) * sin_t[...]) * scale
            qkv[:, pl.ds(pl.multiple_of(at + k * 128, 128), 128)] = part_y.astype(BF16)
        return carry

    lax.fori_loop(0, 2 * D // 256, project_turned, 0)

    def project(ct, carry):
        at = pl.multiple_of(2 * D + ct * 256, 128)
        qkv[:, pl.ds(at, 256)] = dot(n1[...], wqkv[:, pl.ds(at, 256)], 1, 0).astype(BF16)
        return carry

    lax.fori_loop(0, D // 256, project, 0)
    gather_step(a_ready + 1)

    att, stat = s["att"], s["stat"]
    lane_row = lax.broadcasted_iota(jnp.int32, (BLOCK, 128), 1)
    keep_one = jnp.where(lane_row < HEAD_DIM, 1.0, 0.0).astype(BF16)
    keep_two = jnp.where(lane_row < HEAD_DIM, 0.0, 1.0).astype(BF16)

    def stacked(x):
        return jnp.concatenate([x * keep_one, x * keep_two], axis=0)

    def unstacked(x):
        return jnp.concatenate([x[:HEAD_DIM, :BLOCK], x[HEAD_DIM:, BLOCK:]], axis=0).T

    def unit_refs(j, b):
        lanes = [pl.ds(pl.multiple_of(k * D + j * 128, 128), 128) for k in range(3)]
        return lanes, pl.ds(pl.multiple_of(b * BLOCK, BLOCK), SPAN), pl.ds(pl.multiple_of(b * BLOCK + HALF, 16), BLOCK)

    def unit_scores(j, b):
        (lq, lk, lv), keys, queries = unit_refs(j, b)
        qs = stacked(qkv[queries, lq])
        kp, vp = qkv[keys, lk], qkv[keys, lv]
        pen = bias_t[b]
        return qs, kp, vp, dot(kp, qs, 1, 1) + jnp.concatenate([pen, pen], axis=1)

    G = z.G

    def attend(v, carry):
        j, g = lax.div(v, NB // G), lax.rem(v, NB // G)
        for i in range(G):
            b = g * G + i
            u = j * NB + b
            _, _, vp, scores = unit_scores(j, b)
            top = jnp.max(scores, axis=0, keepdims=True)
            weights = jnp.exp(scores - top)
            inv = 1.0 / jnp.sum(weights, axis=0, keepdims=True)
            stat[u, 0:1, :] = top
            stat[u, 1:2, :] = inv
            got = unstacked(dot(vp, (weights * inv).astype(BF16), 0, 0))
            att[pl.ds(pl.multiple_of(b * BLOCK, BLOCK), BLOCK), pl.ds(pl.multiple_of(j * 128, 128), 128)] = got.astype(BF16)
        return carry

    lax.fori_loop(0, z.pairs * (NB // G), attend, 0)
    for t in range(a_ready + 2, C + stages - 1):
        gather_step(t)

    def unpack_b(i, carry):
        r = pl.multiple_of(i * 2 * SH, 16)
        a = [shard_pair(z.CA - 1, nn, i)[:, z.LA - z.O0 - z.cuts[z.CA - 1][0]:] for nn in range(N)] if z.O0 else None
        bs = [part(z.CA, C, nn, i) for nn in range(N)]
        o_rest = QN - z.O0
        wot[pl.ds(r, 2 * SH), :] = jnp.concatenate(
            [x for nn in range(N) for x in (([a[nn]] if z.O0 else []) + [bs[nn][:, :o_rest]])], axis=1)
        for k, ref in enumerate((wg, wu, wgo)):
            at = o_rest + k * FN
            ref[pl.ds(r, 2 * SH), :] = jnp.concatenate([v[:, at:at + FN] for v in bs], axis=1)
        return carry

    lax.fori_loop(0, W // 2, unpack_b, 0)

    ost, n2, res, resg = s["ost"], s["n2"], s["resr"], s["resg"]
    hid, dgate, dup, datt = s["hid"], s["dgate"], s["dup"], s["datt"]
    MB, FC = z.MB, z.FC

    def norm_back(hat, rstd, e, gain):
        eg = e * gain
        return rstd * (eg - jnp.mean(eg, axis=-1, keepdims=True) - hat * jnp.mean(eg * hat, axis=-1, keepdims=True))

    def line_rows(dest, m, rb):
        theirs = m + core * (N - 1 - 2 * m)
        return dest.at[pl.ds(pl.multiple_of(theirs * R + rb * MB, 16), MB)]

    def behind(side):
        return n if side == 0 else N - 1 - n

    def line_copy(dest, rb, key, side, k, stage=None):
        step = 1 - 2 * side
        ref = line_rows(dest, n - step * k, rb)
        src = ref if stage is None else stage.at[pl.ds(pl.multiple_of(rb * MB, 16), MB)]
        return copy_to(src, ref, s[key + "s"].at[rb, side, k], s[key + "r"].at[rb, side, k], (w, n + step))

    def own_copy(stage, dest, rb, key):
        return pltpu.make_async_copy(stage.at[pl.ds(pl.multiple_of(rb * MB, 16), MB)], line_rows(dest, n, rb), s[key + "l"].at[rb])

    def token_send(stage, dest, rb, key):
        own_copy(stage, dest, rb, key).start()
        for side in range(2):
            @pl.when(behind(side) < N - 1)
            def _():
                line_copy(dest, rb, key, side, 0, stage).start()

    def token_forward(dest, key, k):
        def body(rb, carry):
            for side in range(2):
                step = 1 - 2 * side

                @pl.when(behind(side) >= k)
                def _():
                    arrived(line_rows(dest, n - step * k, rb), s[key + "s"].at[rb, side, k - 1], s[key + "r"].at[rb, side, k - 1], (w, n - step))

                if k < N - 1:
                    @pl.when(jnp.logical_and(behind(side) >= k, behind(side) < N - 1))
                    def _():
                        line_copy(dest, rb, key, side, k).start()
            return carry

        lax.fori_loop(0, z.blocks, body, 0)

    def token_end(stage, dest, key):
        def body(rb, carry):
            own_copy(stage, dest, rb, key).wait()
            for side in range(2):
                for k in range(N - 1):
                    @pl.when(jnp.logical_and(behind(side) >= k, behind(side) < N - 1))
                    def _():
                        line_copy(dest, rb, key, side, k).wait_send()
            return carry

        lax.fori_loop(0, z.blocks, body, 0)

    def feed(rb, carry):
        r = pl.multiple_of(rb * MB, 16)
        rows = pl.ds(r, MB)
        x = xin[pl.ds(pl.multiple_of(rb * MB + HALF, 16), MB), :].astype(F32)
        residual = x + dot(att[rows, :], wot[...], 1, 1)
        hat, rstd = normed(residual)
        gain = grow[1:2, :]
        n2v = (hat * gain).astype(BF16)
        n2[rows, :] = n2v
        cotv = cot[rows, :]
        total_out, e = residual, None
        for f in range(0, F, FC):
            gate = dot(n2v, wg[:, f:f + FC], 1, 0)
            upv = dot(n2v, wu[:, f:f + FC], 1, 0)
            dh = dot(cotv, wgo[:, f:f + FC], 1, 0)
            sq = gate * gate
            th = jnp.tanh(GELU_A * (gate * (1.0 + GELU_B * sq)))
            half = 0.5 * (1.0 + th)
            act = gate * half
            slope = half + (0.5 * GELU_A) * gate * (1.0 - th * th) * (1.0 + (3.0 * GELU_B) * sq)
            hv = (act * upv).astype(BF16)
            dgv = (dh * upv * slope).astype(BF16)
            duv = (dh * act).astype(BF16)
            hid[rows, f:f + FC] = hv
            dgate[rows, f:f + FC] = dgv
            dup[rows, f:f + FC] = duv
            total_out = total_out + dot(hv, wgo[:, f:f + FC], 1, 1)
            more = dot(dgv, wg[:, f:f + FC], 1, 1) + dot(duv, wu[:, f:f + FC], 1, 1)
            e = more if e is None else e + more
        ost[rows, :] = total_out.astype(BF16)
        token_send(ost, out, rb, "o")
        gsum[1:2, :] = gsum[1:2, :] + jnp.sum(e * hat, axis=0, keepdims=True)
        grad = cotv.astype(F32) + norm_back(hat, rstd, e, gain)
        resg[rows, :] = grad
        low = grad.astype(BF16)
        res[rows, :] = low
        datt[rows, :] = dot(low, wot[...], 1, 0).astype(BF16)
        return carry

    lax.fori_loop(0, z.blocks, feed, 0)

    for c in pending:
        c.wait_send()
    pending.clear()

    def store_rows(c, nn, i, k, value):
        if RS > SH:
            value = jnp.concatenate([value, jnp.zeros((RS - SH, value.shape[1]), F32)], axis=0)
        wb[c][nn, i, k] = value.astype(BF16)

    HT, TM = z.HT, z.TM
    owx = s["owx"]

    def store_part(chunks, nn, t, value):
        lo = z.cuts[chunks[0]][0]
        for c in chunks:
            a, b = z.cuts[c]
            for i in range(HT):
                for k in range(2):
                    at = (2 * i + k) * SH
                    store_rows(c, nn, t * HT + i, k, value[at:at + SH, a - lo:b - lo])

    def grads_b(t, carry):
        r = pl.multiple_of(t * TM, 16)
        cols = pl.ds(pl.multiple_of(t * TM, 128), TM) if TM % 128 == 0 else None
        gg = dot(s["n2t"][pl.ds(r, TM), :], dgate[...], 1, 0)
        gu = dot(s["n2t"][pl.ds(r, TM), :], dup[...], 1, 0)
        go = dot(s["ct"][pl.ds(r, TM), :], hid[...], 1, 0)
        gw = dot(s["rt"][pl.ds(r, TM), :], att[...], 1, 0)
        if z.O0:
            firsts = [gw[:, nn * QN:nn * QN + z.O0] for nn in range(N)]
            spare = owx.shape[1] - N * z.O0
            if spare:
                firsts.append(jnp.zeros((TM, spare), F32))
            owx[pl.ds(r, TM), :] = jnp.concatenate(firsts, axis=1)
        for nn in range(N):
            pieces = [gw[:, nn * QN + z.O0:(nn + 1) * QN]] + [v[:, nn * FN:(nn + 1) * FN] for v in (gg, gu, go)]
            if z.lanes > z.real:
                pieces.append(jnp.zeros((TM, z.lanes - z.real), F32))
            store_part(list(range(z.CA, C)), nn, t, jnp.concatenate(pieces, axis=1))
        return carry

    transposed(s["n2t"], n2, 0)
    transposed(s["rt"], res, 0)
    lax.fori_loop(0, D // TM, grads_b, 0)

    scatter_order = [list(range(z.bits)), list(range(z.bits))[::-1]]

    def slot_base(t):
        return sum(1 << (z.bits - 1 - u) for u in range(t))

    def r0_start(c):
        send(wb[c].at[:, :, 1 - core], r0[c], s["g0s"].at[c], s["g0r"].at[c], sib_dev)

    def r0_finish(c):
        arrived(r0[c], s["g0s"].at[c], s["g0r"].at[c], sib_dev)

        def body(i, carry):
            for nn in range(N):
                wb[c][nn, i, core] = (wb[c][nn, i, core].astype(F32) + r0[c][nn, i].astype(F32)).astype(BF16)
            return carry

        lax.fori_loop(0, W // 2, body, 0)

    def r1_start(c, t):
        for h in range(2):
            b = scatter_order[h][t]
            for i, combo in enumerate(combos(scatter_order[h][t + 1:])):
                slot = slot_base(t) + i
                send(wb[c].at[half_refs[h], flip(hi, combo + [b]), core], r1[c].at[h, slot], s["g1s"].at[c, h, slot], s["g1r"].at[c, h, slot], bit_dev(b))

    def r1_finish(c, t):
        for h in range(2):
            b = scatter_order[h][t]
            for i, combo in enumerate(combos(scatter_order[h][t + 1:])):
                slot = slot_base(t) + i
                arrived(r1[c].at[h, slot], s["g1s"].at[c, h, slot], s["g1r"].at[c, h, slot], bit_dev(b))
                hv = flip(hi, combo)
                for nn in range(N2):
                    at = h * N2 + nn
                    wb[c][at, hv, core] = (wb[c][at, hv, core].astype(F32) + r1[c][h, slot, nn].astype(F32)).astype(BF16)

    def rz_copy(c, side, d):
        step = 1 - 2 * side
        return copy_to(wb[c].at[n + step * (1 + d), hi, core], rz[c].at[side, d], s["g2s"].at[c, side, d], s["g2r"].at[c, side, d], (w, n + step))

    def rz_round(c, r):
        for side in range(2):
            step = 1 - 2 * side

            @pl.when(behind(side) == r)
            def _():
                if r > 0:
                    for d in range(N - r):
                        arrived(rz[c].at[side, d], s["g2s"].at[c, side, d], s["g2r"].at[c, side, d], (w, n - step))
                    for d in range(1, N - r):
                        m = n + step * d
                        wb[c][m, hi, core] = (wb[c][m, hi, core].astype(F32) + rz[c][side, d].astype(F32)).astype(BF16)
                for d in range(N - 1 - r):
                    rz_copy(c, side, d).start()

    def rz_sent(c):
        for side in range(2):
            for r in range(N - 1):
                @pl.when(behind(side) == r)
                def _():
                    for d in range(N - 1 - r):
                        rz_copy(c, side, d).wait_send()

    def rz_finish(c):
        lo, up = z.cuts[c]
        gp[:, lo:up] = wb[c][n, hi, core].astype(F32)
        for side in range(2):
            @pl.when(behind(side) > 0)
            def _():
                gp[:, lo:up] = gp[:, lo:up] + rz[c][side, 0].astype(F32)

    last_stage = z.bits + 1 + N

    def scatter_advance(chunks, st):
        for c in chunks:
            if st == 0:
                r0_start(c)
            elif st <= z.bits + 1:
                if st == 1:
                    r0_finish(c)
                else:
                    r1_finish(c, st - 2)
                if st <= z.bits:
                    r1_start(c, st - 1)
                else:
                    rz_round(c, 0)
            else:
                rz_round(c, st - z.bits - 1)
                if st == last_stage - 1:
                    rz_finish(c)

    part_a, part_b = list(range(z.CA)), list(range(z.CA, C))
    scatter_advance(part_b, 0)
    token_forward(out, "o", 1)

    dkv, edge, rim, rimr = s["dkv"], s["edge"], s["rim"], s["rimr"]
    dk_ref, dv_ref = dkv.at[0], dkv.at[1]

    def attend_back(j, carry):
        dkv[:, 0:BLOCK, :] = jnp.zeros((2, BLOCK, 128), F32)

        def group(g, inner):
            tails = None
            for i in range(G):
                b = g * G + i
                u = j * NB + b
                (lq, lk, lv), keys, queries = unit_refs(j, b)
                qs, kp, vp, scores = unit_scores(j, b)
                probs = jnp.exp(scores - stat[u, 0:1, :]) * stat[u, 1:2, :]
                gs = stacked(datt[pl.ds(pl.multiple_of(b * BLOCK, BLOCK), BLOCK), pl.ds(pl.multiple_of(j * 128, 128), 128)])
                prob_grad = dot(vp, gs, 1, 1)
                row_dot = jnp.sum(probs * prob_grad, axis=0, keepdims=True)
                score_grad = (probs * (prob_grad - row_dot)).astype(BF16)
                parts = (dot(score_grad, qs, 1, 0), dot(probs.astype(BF16), gs, 1, 0))
                dq = unstacked(dot(kp, score_grad, 0, 0)) * F32(1.0 / math.sqrt(HEAD_DIM))
                dq = dq * cos_t[queries, :] - partner_lanes(dq) * sin_t[queries, :]
                qkv[queries, lq] = dq.astype(BF16)
                here = pl.ds(pl.multiple_of(b * BLOCK, BLOCK), BLOCK)
                for k in range(2):
                    before = dkv[k, here, :] if tails is None else tails[k]
                    dkv[k, here, :] = before + parts[k][:BLOCK]
                tails = [x[BLOCK:] for x in parts]
            after = pl.ds(pl.multiple_of(g * G * BLOCK + G * BLOCK, BLOCK), BLOCK)
            for k in range(2):
                dkv[k, after, :] = tails[k]
            return inner

        lax.fori_loop(0, NB // G, group, 0)
        (_, lk, lv), _, _ = unit_refs(j, 0)
        lj = pl.ds(pl.multiple_of(j * 128, 128), 128)
        for k, ref in enumerate((dk_ref, dv_ref)):
            wide_lanes = pl.ds(pl.multiple_of(k * D + j * 128, 128), 128)
            rim[0, :, wide_lanes] = ref[0:HALF, :].astype(BF16)
            rim[1, :, wide_lanes] = ref[E - HALF:, :].astype(BF16)
            edge[0, :, wide_lanes] = ref[HALF:WINDOW, :]
            edge[1, :, wide_lanes] = ref[R:R + HALF, :]
        mid = slice(HALF, HALF + R)
        dk = dk_ref[mid, :]
        qkv[mid, lk] = (dk * cos_t[mid, :] - partner_lanes(dk) * sin_t[mid, :]).astype(BF16)
        qkv[mid, lv] = dv_ref[mid, :].astype(BF16)
        return carry

    half_pairs = z.pairs // 2
    lax.fori_loop(0, half_pairs, attend_back, 0)
    scatter_advance(part_b, 1)
    if N > 2:
        token_forward(out, "o", 2)
    lax.fori_loop(half_pairs, z.pairs, attend_back, 0)

    def rim_to_prev():
        return copy_to(rim.at[0], rimr.at[1], s["rs"].at[0], s["rr"].at[1], prev_dev)

    def rim_to_next():
        return copy_to(rim.at[1], rimr.at[0], s["rs"].at[1], s["rr"].at[0], next_dev)

    @pl.when(has_prev)
    def _():
        rim_to_prev().start()

    @pl.when(has_next)
    def _():
        rim_to_next().start()

    @pl.when(jnp.logical_not(has_prev))
    def _():
        rimr[0] = jnp.zeros((HALF, 2 * D), BF16)

    @pl.when(jnp.logical_not(has_next))
    def _():
        rimr[1] = jnp.zeros((HALF, 2 * D), BF16)

    for k in range(3, N):
        token_forward(out, "o", k)
    for st in range(2, z.bits + 2):
        scatter_advance(part_b, st)

    @pl.when(has_prev)
    def _():
        rim_to_next().wait_recv()

    @pl.when(has_next)
    def _():
        rim_to_prev().wait_recv()

    @pl.when(has_prev)
    def _():
        rim_to_prev().wait_send()

    @pl.when(has_next)
    def _():
        rim_to_next().wait_send()

    for side, row in ((0, HALF), (1, R)):
        rows = slice(row, row + HALF)
        for j in range(z.pairs):
            lk = slice(j * 128, (j + 1) * 128)
            lv = slice(D + j * 128, D + (j + 1) * 128)
            dk = edge[side, :, lk] + rimr[side, :, lk].astype(F32)
            dv = edge[side, :, lv] + rimr[side, :, lv].astype(F32)
            dk = dk * cos_t[rows, :] - partner_lanes(dk) * sin_t[rows, :]
            qkv[rows, D + j * 128:D + (j + 1) * 128] = dk.astype(BF16)
            qkv[rows, 2 * D + j * 128:2 * D + (j + 1) * 128] = dv.astype(BF16)

    tst = n2

    def input_grad(rb, carry):
        rows = pl.ds(pl.multiple_of(rb * MB, 16), MB)
        ext = pl.ds(pl.multiple_of(rb * MB + HALF, 16), MB)
        e = dot(qkv[ext, :], wqkv[...], 1, 1)
        hat, rstd = normed(xin[ext, :].astype(F32))
        gsum[0:1, :] = gsum[0:1, :] + jnp.sum(e * hat, axis=0, keepdims=True)
        tst[rows, :] = (resg[rows, :] + norm_back(hat, rstd, e, grow[0:1, :])).astype(BF16)
        token_send(tst, tg, rb, "t")
        return carry

    lax.fori_loop(0, z.blocks, input_grad, 0)

    gcol[...] = jnp.concatenate([gsum[...], jnp.zeros((120, D), F32)], axis=0).T
    transposed(s["n2t"], n1, HALF)

    def grads_a(t, carry):
        r = pl.multiple_of(t * TM, 16)
        g = [dot(s["n2t"][pl.ds(r, TM), :], qkv[HALF:HALF + R, k * D:(k + 1) * D], 1, 0) for k in range(3)]
        gains = gcol[pl.ds(r, TM), 0:GAIN_LANES]
        for nn in range(N):
            pieces = [gains] + [v[:, nn * QN:(nn + 1) * QN] for v in g]
            if z.O0:
                pieces.append(owx[pl.ds(r, TM), nn * z.O0:(nn + 1) * z.O0])
            store_part(part_a, nn, t, jnp.concatenate(pieces, axis=1))
        return carry

    lax.fori_loop(0, D // TM, grads_a, 0)
    scatter_advance(part_a, 0)
    for st in range(z.bits + 2, last_stage):
        scatter_advance(part_b, st)
    for st in range(1, z.bits + 1):
        scatter_advance(part_a, st)
    token_forward(tg, "t", 1)
    scatter_advance(part_a, z.bits + 1)
    for k in range(2, N):
        token_forward(tg, "t", k)
    for st in range(z.bits + 2, last_stage):
        scatter_advance(part_a, st)

    for c in pending:
        c.wait_send()
    for c in range(C):
        rz_sent(c)
    token_end(ost, out, "o")
    token_end(tst, tg, "t")


def run_layer(z, *args):
    shapes, names = [], []

    def vmem(name, shape, dtype):
        names.append(name)
        shapes.append(pltpu.VMEM(shape, dtype))

    def sems(name, *shape):
        names.append(name)
        shapes.append(pltpu.SemaphoreType.DMA(shape))

    W, N, D, F, R, E, C = z.W, z.N, z.D, z.F, z.R, z.E, z.C
    for c, (lo, up) in enumerate(z.cuts):
        vmem(f"wb{c}", (N, W // 2, 2, z.RS, up - lo), BF16)
        vmem(f"r0{c}", (N, W // 2, z.RS, up - lo), BF16)
        vmem(f"r1{c}", (2, W // 2 - 1, N // 2, z.RS, up - lo), BF16)
        vmem(f"rz{c}", (2, N - 1, z.RS, up - lo), BF16)
    vmem("xin", (E, D), BF16)
    vmem("n1", (E, D), BF16)
    vmem("qkv", (E, 3 * D), BF16)
    vmem("wqkv", (D, 3 * D), BF16)
    vmem("wot", (D, D), BF16)
    for name in ("wg", "wu", "wgo"):
        vmem(name, (D, F), BF16)
    vmem("gcol", (D, 128), F32)
    vmem("grow", (8, D), F32)
    vmem("gsum", (8, D), F32)
    vmem("owx", (D, round_up(max(N * z.O0, 1), 128)), F32)
    vmem("cos", (E, 128), F32)
    vmem("sin", (E, 128), F32)
    vmem("bias", (z.NB, SPAN, BLOCK), F32)
    vmem("stat", (z.pairs * z.NB, 8, 2 * BLOCK), F32)
    vmem("pk", (z.RS, z.lanes), BF16)
    for name in ("att", "ost", "n2", "resr", "datt", "cot"):
        vmem(name, (R, D), BF16)
    for name in ("n2t", "ct", "rt"):
        vmem(name, (D, R), BF16)
    vmem("resg", (R, D), F32)
    for name in ("hid", "dgate", "dup"):
        vmem(name, (R, F), BF16)
    vmem("dkv", (2, E, 128), F32)
    vmem("edge", (2, HALF, 2 * D), F32)
    vmem("rim", (2, HALF, 2 * D), BF16)
    vmem("rimr", (2, HALF, 2 * D), BF16)
    sems("l_own", C)
    sems("l_tok", 4)
    for name in ("zs", "zr"):
        sems(name, C, N - 1)
    for name in ("g2s", "g2r"):
        sems(name, C, 2, N - 1)
    for name in ("ss", "sr", "g1s", "g1r"):
        sems(name, C, 2, W // 2 - 1)
    for name in ("ds", "dr"):
        sems(name, C, 2)
    for name in ("g0s", "g0r"):
        sems(name, C)
    for name in ("hs", "hr", "rs", "rr"):
        sems(name, 2)
    for name in ("ol", "tl"):
        sems(name, z.blocks)
    for name in ("os", "or", "ts", "tr"):
        sems(name, z.blocks, 2, N - 1)
    hbm = pl.BlockSpec(memory_space=pl.ANY)
    vm = pl.BlockSpec(memory_space=pltpu.VMEM)
    return pl.pallas_call(
        functools.partial(layer_kernel, z, names),
        out_shape=(
            jax.ShapeDtypeStruct((z.T, D), BF16),
            jax.ShapeDtypeStruct((z.T, D), BF16),
            jax.ShapeDtypeStruct((z.RS, z.lanes), F32),
        ),
        in_specs=[pl.BlockSpec(memory_space=pltpu.SMEM), hbm, hbm] + [vm] * 6,
        out_specs=(hbm, hbm, vm),
        scratch_shapes=shapes,
        compiler_params=pltpu.CompilerParams(collective_id=0, has_side_effects=True, vmem_limit_bytes=VMEM_BYTES),
    )(*args)


VMEM_BYTES = 64 * 1024 * 1024 - 1024 * 64


def finish_kernel(z, tg, out, gp, o_out, o_tg, o_in, o_ow, o_gu, o_dn, o_gains, low, full, s_in, s_out, s_copy):
    rows = low.shape[1]
    steps = z.T // rows
    whole = pltpu.make_async_copy(out, o_out, s_copy)
    whole.start()

    def load(i):
        return pltpu.make_async_copy(tg.at[pl.ds(i * rows, rows)], low.at[i % 2], s_in.at[i % 2])

    def store(i):
        return pltpu.make_async_copy(full.at[i % 2], o_tg.at[pl.ds(i * rows, rows)], s_out.at[i % 2])

    load(0).start()
    for i in range(steps):
        if i + 1 < steps:
            load(i + 1).start()
        load(i).wait()
        if i >= 2:
            store(i - 2).wait()
        full[i % 2] = low[i % 2].astype(F32)
        store(i).start()
        if i == 0:
            unpack_grads(z, gp, o_in, o_ow, o_gu, o_dn, o_gains)
    for i in range(max(0, steps - 2), steps):
        store(i).wait()
    whole.wait()


def unpack_grads(z, gp, o_in, o_ow, o_gu, o_dn, o_gains):
    SH, QN, FN = z.SH, z.QN, z.FN
    heads = QN // HEAD_DIM
    value = gp[...][:SH]

    def flipped(x):
        a, b = x.shape
        a2, b2 = round_up(a, 128), round_up(b, 128)
        if b2 > b:
            x = jnp.concatenate([x, jnp.zeros((a, b2 - b), F32)], axis=1)
        if a2 > a:
            x = jnp.concatenate([x, jnp.zeros((a2 - a, b2), F32)], axis=0)
        return x.T[:b, :a]

    at = GAIN_LANES
    o_in[...] = jnp.concatenate(
        [value[:, at + k * QN + a * HEAD_DIM:at + k * QN + (a + 1) * HEAD_DIM] for a in range(heads) for k in range(3)], axis=1)
    at += 3 * QN
    o_ow[...] = flipped(value[:, at:at + QN])
    at += QN
    for k in range(2):
        o_gu[:, k, :] = value[:, at + k * FN:at + (k + 1) * FN]
    at += 2 * FN
    o_dn[...] = flipped(value[:, at:at + FN])
    o_gains[...] = flipped(value[:, :128])[0:8, :]


def finish(z, tg, out, gp):
    rows = 256
    hbm = pl.BlockSpec(memory_space=pl.ANY)
    vm = pl.BlockSpec(memory_space=pltpu.VMEM)
    return pl.pallas_call(
        functools.partial(finish_kernel, z),
        out_shape=(
            jax.ShapeDtypeStruct((z.T, z.D), BF16),
            jax.ShapeDtypeStruct((z.T, z.D), F32),
            jax.ShapeDtypeStruct((z.SH, 3 * z.QN), F32),
            jax.ShapeDtypeStruct((z.QN, z.SH), F32),
            jax.ShapeDtypeStruct((z.SH, 2, z.FN), F32),
            jax.ShapeDtypeStruct((z.FN, z.SH), F32),
            jax.ShapeDtypeStruct((8, z.SH), F32),
        ),
        in_specs=[hbm, hbm, vm],
        out_specs=(hbm, hbm, vm, vm, vm, vm, vm),
        scratch_shapes=[
            pltpu.VMEM((2, rows, z.D), BF16),
            pltpu.VMEM((2, rows, z.D), F32),
            pltpu.SemaphoreType.DMA((2,)),
            pltpu.SemaphoreType.DMA((2,)),
            pltpu.SemaphoreType.DMA,
        ],
        compiler_params=pltpu.CompilerParams(vmem_limit_bytes=32 * 1024 * 1024),
    )(tg, out, gp)


def per_device(tokens, lengths, masked, attention_in, attention_out, geglu_in, geglu_out, gain_attention, gain_feedforward, out_grad):
    wide, narrow = lax.axis_size("wide"), lax.axis_size("narrow")
    z = Sizes(wide, narrow, tokens.shape[0], tokens.shape[1], attention_out.shape[0] * narrow, geglu_out.shape[0] * narrow, lengths.shape[0])
    gate_up = geglu_in.astype(BF16).reshape(z.SH, 2 * z.FN)
    gains = jnp.stack([gain_attention, gain_feedforward])
    out, tg, gp = run_layer(
        z, lengths, tokens, out_grad, masked.reshape(-1, 128), attention_in, attention_out, gate_up, geglu_out, gains)
    out, tg, g_in, g_out, g_gu, g_down, g_gains = finish(z, tg, out, gp)
    return (out, tg, g_in, g_out, g_gu, g_down, g_gains[0], g_gains[1])


def solution(mesh):
    return jax.shard_map(
        per_device,
        mesh=mesh,
        in_specs=(P("wide", None), P(), P("wide"), P("wide", "narrow"), P("narrow", "wide"), P("wide", None, "narrow"),
                  P("narrow", "wide"), P("wide"), P("wide"), P("wide", None)),
        out_specs=(P("wide", None), P("wide", None), P("wide", "narrow"), P("narrow", "wide"), P("wide", None, "narrow"),
                   P("narrow", "wide"), P("wide"), P("wide")),
        check_vma=False,
    )
```

```python
import functools
import itertools
import math

import jax
import jax.numpy as jnp
from jax import lax
from jax.experimental import pallas as pl
from jax.experimental.pallas import tpu as pltpu
from jax.sharding import PartitionSpec as P

MESH = pl.DeviceIdType.MESH
HEAD_DIM = 64
WINDOW = 128
HALF = WINDOW // 2
BLOCK = 128
FINISH_ROWS = 256
SPAN = BLOCK + WINDOW
GAIN_LANES = 32
EPSILON = 1e-05
THETA = 10000.0
NEG_LARGE = -1e30
F32 = jnp.float32
BF16 = jnp.bfloat16
GELU_A = math.sqrt(2.0 / math.pi)
GELU_B = 0.044715


def round_up(value, unit):
    return -(-value // unit) * unit


def dot(a, b, ca, cb):
    return lax.dot_general(a, b, (((ca,), (cb,)), ((), ())), preferred_element_type=F32)


class Sizes:
    def __init__(self, wide, narrow, tok_rows, width, heads_width, hidden, docs):
        self.W, self.N, self.T, self.D, self.F, self.docs = wide, narrow, tok_rows, width, hidden, docs
        self.R = tok_rows // narrow
        self.E = self.R + WINDOW
        self.NB = self.R // BLOCK
        self.pairs = width // 128
        self.G = 4 if self.NB % 4 == 0 else 1
        self.SH = width // wide
        self.RS = round_up(self.SH, 16)
        self.QN, self.FN = heads_width // narrow, hidden // narrow
        self.bits = (wide // 2).bit_length() - 1
        first = GAIN_LANES + 3 * self.QN
        self.real = first + self.QN + 3 * self.FN
        self.LA = round_up(first, 128)
        self.lanes = round_up(self.real, 128)
        self.O0 = self.LA - first
        cut_a = (self.LA // 256) * 128
        mid = self.LA + ((self.lanes - self.LA) // 256) * 128
        self.cuts = [(0, cut_a), (cut_a, self.LA), (self.LA, mid), (mid, self.lanes)]
        self.C = len(self.cuts)
        self.CA = 2
        self.MB = min(self.R, 256)
        self.blocks = self.R // self.MB
        self.FC = 384 if hidden % 384 == 0 else hidden
        self.HT = max(1, 192 // (2 * self.SH))
        self.TM = self.HT * 2 * self.SH


def combos(bit_list):
    out = []
    for mask in range(1 << len(bit_list)):
        out.append([b for i, b in enumerate(bit_list) if mask >> i & 1])
    return out


def layer_kernel(z, names, lengths, tokens, grads_in, masked, w_in, w_out, w_gu, w_down, gain_one, gain_two, out, tg, gp, *scratch):
    s = dict(zip(names, scratch))
    W, N, T, D, F, R, E, NB = z.W, z.N, z.T, z.D, z.F, z.R, z.E, z.NB
    C, SH, RS, N2 = z.C, z.SH, z.RS, z.N // 2
    wb = [s[f"wb{c}"] for c in range(C)]
    pk, cot = s["pk"], s["cot"]
    r0 = [s[f"r0{c}"] for c in range(C)]
    r1 = [s[f"r1{c}"] for c in range(C)]
    rz = [s[f"rz{c}"] for c in range(C)]
    w, n = lax.axis_index("wide"), lax.axis_index("narrow")
    core, hi = lax.rem(w, 2), lax.div(w, 2)
    place = n + core * (N - 1 - 2 * n)
    ahead = 1 - 2 * core
    first, last = place == 0, place == N - 1
    has_prev = jnp.logical_or(place > 0, w > 0)
    has_next = jnp.logical_or(place < N - 1, w < W - 1)
    prev_dev = (jnp.where(first, w - 1, w), jnp.where(first, n, n - ahead))
    next_dev = (jnp.where(last, w + 1, w), jnp.where(last, n, n + ahead))
    at_end = jnp.logical_or(first, last)
    low_block = jnp.logical_and(at_end, w > 0)
    high_block = jnp.logical_and(at_end, w < W - 1)
    sib_dev = (w + 1 - 2 * core, n)

    def around(k):
        return lax.rem(n + k + N, N)

    def flip(value, bit_list):
        for b in bit_list:
            value = value + (1 - 2 * lax.rem(lax.div(hi, 1 << b), 2)) * (1 << b)
        return value

    def bit_dev(b):
        return (2 * flip(hi, [b]) + core, n)

    pending = []

    def copy_to(src, dst, send, recv, dev):
        return pltpu.make_async_remote_copy(src_ref=src, dst_ref=dst, send_sem=send, recv_sem=recv, device_id=dev, device_id_type=MESH)

    def send(src, dst, send_sem, recv_sem, dev):
        c = copy_to(src, dst, send_sem, recv_sem, dev)
        c.start()
        pending.append(c)

    def arrived(dst, send_sem, recv_sem, dev):
        copy_to(dst, dst, send_sem, recv_sem, dev).wait_recv()

    barrier = pltpu.get_barrier_semaphore()
    partners = [(w, around(k)) for k in range(1, N)] + [bit_dev(b) for b in range(z.bits)] + [sib_dev]
    for dev in partners:
        pl.semaphore_signal(barrier, inc=1, device_id=dev, device_id_type=MESH)

    @pl.when(low_block)
    def _():
        pl.semaphore_signal(barrier, inc=1, device_id=(w - 1, n), device_id_type=MESH)

    @pl.when(high_block)
    def _():
        pl.semaphore_signal(barrier, inc=1, device_id=(w + 1, n), device_id_type=MESH)


    def flipped(x):
        a, b = x.shape
        a2, b2 = round_up(a, 128), round_up(b, 128)
        if b2 > b:
            x = jnp.concatenate([x, jnp.zeros((a, b2 - b), F32)], axis=1)
        if a2 > a:
            x = jnp.concatenate([x, jnp.zeros((a2 - a, b2), F32)], axis=0)
        return x.T[:b, :a]

    def pack(lo, up, pieces):
        have = sum(p.shape[1] for p in pieces)
        if up - lo > have:
            pieces = pieces + [jnp.zeros((SH, up - lo - have), F32)]
        value = jnp.concatenate(pieces, axis=1)
        if RS > SH:
            value = jnp.concatenate([value, jnp.zeros((RS - SH, up - lo), F32)], axis=0)
        pk[:, lo:up] = value.astype(BF16)

    QN, FN = z.QN, z.FN
    heads = QN // HEAD_DIM
    raw_in, out_t = w_in[...], flipped(w_out[...])
    gain_rows = jnp.concatenate([gain_one[...], gain_two[...], jnp.zeros((6, SH), F32)], axis=0)
    gain_cols = jnp.concatenate([flipped(gain_rows), jnp.zeros((SH, GAIN_LANES - 8), F32)], axis=1)
    pack(0, z.LA, [gain_cols] + [raw_in[:, (3 * a + k) * HEAD_DIM:(3 * a + k + 1) * HEAD_DIM] for k in range(3) for a in range(heads)] + [out_t[:, :z.O0]])
    pl.semaphore_wait(barrier, len(partners) + low_block.astype(jnp.int32) + high_block.astype(jnp.int32))

    half_refs = [pl.ds(h * N2, N2) for h in range(2)]
    gather_order = [list(range(z.bits))[::-1], list(range(z.bits))]

    def z_start(c):
        lo, up = z.cuts[c]
        src = pk.at[:, lo:up]
        pltpu.make_async_copy(src, wb[c].at[n, hi, core], s["l_own"].at[c]).start()
        for k in range(1, N):
            send(src, wb[c].at[n, hi, core], s["zs"].at[c, k - 1], s["zr"].at[c, k - 1], (w, around(k)))

    def z_wait(c):
        lo, up = z.cuts[c]
        pltpu.make_async_copy(pk.at[:, lo:up], wb[c].at[n, hi, core], s["l_own"].at[c]).wait()
        for k in range(1, N):
            arrived(wb[c].at[around(-k), hi, core], s["zs"].at[c, k - 1], s["zr"].at[c, k - 1], (w, around(-k)))

    def s_start(c, t):
        for h in range(2):
            b = gather_order[h][t]
            for i, combo in enumerate(combos(gather_order[h][:t])):
                ref = wb[c].at[half_refs[h], flip(hi, combo), core]
                slot = (1 << t) - 1 + i
                send(ref, ref, s["ss"].at[c, h, slot], s["sr"].at[c, h, slot], bit_dev(b))

    def s_wait(c, t):
        for h in range(2):
            b = gather_order[h][t]
            for i, combo in enumerate(combos(gather_order[h][:t])):
                ref = wb[c].at[half_refs[h], flip(hi, combo + [b]), core]
                slot = (1 << t) - 1 + i
                arrived(ref, s["ss"].at[c, h, slot], s["sr"].at[c, h, slot], bit_dev(b))

    def d_start(c, late):
        for h in range(2):
            everyone = combos(gather_order[h])
            for i, combo in enumerate(everyone):
                if (i >= len(everyone) // 2) == late:
                    ref = wb[c].at[half_refs[h], flip(hi, combo), core]
                    send(ref, ref, s["ds"].at[c, h, i], s["dr"].at[c, h, i], sib_dev)

    def d_wait(c):
        for h in range(2):
            for i, combo in enumerate(combos(gather_order[h])):
                arrived(wb[c].at[half_refs[h], flip(hi, combo), 1 - core], s["ds"].at[c, h, i], s["dr"].at[c, h, i], sib_dev)

    stages = z.bits + 2

    def gather_event(c, st):
        if st == 0:
            z_wait(c)
            if c + 1 < C:
                z_start(c + 1)
        elif st <= z.bits:
            s_wait(c, st - 1)
        else:
            d_wait(c)
        if st < z.bits:
            s_start(c, st)
        if st == z.bits - 1:
            d_start(c, False)
        if st == z.bits:
            d_start(c, True)

    steps = [[(t - st, st) for st in reversed(range(stages)) if 0 <= t - st < C] for t in range(C + stages - 1)]
    a_step = z.CA - 1 + stages - 1
    a_at = steps[a_step].index((z.CA - 1, stages - 1)) + 1

    def gather_events(events):
        for c, st in events:
            gather_event(c, st)

    z_start(0)
    raw_gate, raw_up, raw_down = w_gu[:, 0, :], w_gu[:, 1, :], flipped(w_down[...])
    pack(z.LA, z.lanes, [out_t[:, z.O0:]] + [raw_gate, raw_up, raw_down])

    xin = s["xin"]
    own = pltpu.make_async_copy(tokens.at[pl.ds(pl.multiple_of(place * R, 16), R)], xin.at[pl.ds(HALF, R)], s["l_tok"].at[0])
    own.start()
    own_cot = pltpu.make_async_copy(grads_in.at[pl.ds(pl.multiple_of(place * R, 16), R)], cot, s["l_tok"].at[3])
    own_cot.start()

    def low_copy():
        return pltpu.make_async_copy(tokens.at[pl.ds(pl.multiple_of(place * R - HALF, 16), HALF)], xin.at[pl.ds(0, HALF)], s["l_tok"].at[1])

    def high_copy():
        return pltpu.make_async_copy(tokens.at[pl.ds(pl.multiple_of(place * R + R, 16), HALF)], xin.at[pl.ds(HALF + R, HALF)], s["l_tok"].at[2])

    halo = s["halo"]

    def halo_to_next():
        return copy_to(tokens.at[pl.ds(T - HALF, HALF)], halo.at[0], s["hs"].at[0], s["hr"].at[0], (w + 1, n))

    def halo_to_prev():
        return copy_to(tokens.at[pl.ds(0, HALF)], halo.at[1], s["hs"].at[1], s["hr"].at[1], (w - 1, n))

    @pl.when(place > 0)
    def _():
        low_copy().start()

    @pl.when(place < N - 1)
    def _():
        high_copy().start()

    @pl.when(high_block)
    def _():
        halo_to_next().start()

    @pl.when(low_block)
    def _():
        halo_to_prev().start()

    @pl.when(w == 0)
    def _():
        halo[0] = jnp.zeros((HALF, D), BF16)

    @pl.when(w == W - 1)
    def _():
        halo[1] = jnp.zeros((HALF, D), BF16)

    ends, total = [], jnp.int32(0)
    for d in range(z.docs):
        total = total + lengths[d]
        ends.append(total)
    cos_t, sin_t, bias_t = s["cos"], s["sin"], s["bias"]
    lane = lax.broadcasted_iota(jnp.int32, (BLOCK, 128), 1)
    low_half = lax.rem(lane, HEAD_DIM) < HEAD_DIM // 2

    freq_lane = lax.rem(lax.broadcasted_iota(jnp.int32, (1, 128), 1), HEAD_DIM // 2)
    freq = jnp.zeros((1, 128), F32)
    for d in range(HEAD_DIM // 2):
        freq = jnp.where(freq_lane == d, F32(THETA ** (-2.0 * d / HEAD_DIM)), freq)

    def tables(spot):
        base = w * T + spot * R
        lax.fori_loop(0, E // BLOCK, functools.partial(table_rows, base), 0)
        lax.fori_loop(0, NB, functools.partial(bias_rows, base), 0)

    def table_rows(base, i, carry):
        r = pl.multiple_of(i * BLOCK, BLOCK)
        t = base - HALF + r + lax.broadcasted_iota(jnp.int32, (BLOCK, 128), 0)
        start = jnp.zeros((BLOCK, 128), jnp.int32)
        for d in range(z.docs):
            start = start + jnp.where(t >= ends[d], lengths[d], 0)
        angle = (t - start).astype(F32) * freq
        cos_t[pl.ds(r, BLOCK), :] = jnp.cos(angle)
        sine = jnp.sin(angle)
        sin_t[pl.ds(r, BLOCK), :] = jnp.where(low_half, -sine, sine)
        return carry

    def bias_rows(base, b, carry):
        tk = base - HALF + b * BLOCK + lax.broadcasted_iota(jnp.int32, (SPAN, BLOCK), 0)
        tq = base + b * BLOCK + lax.broadcasted_iota(jnp.int32, (SPAN, BLOCK), 1)
        dk = jnp.where(tk < 0, -1, 0)
        dq = jnp.zeros((SPAN, BLOCK), jnp.int32)
        for d in range(z.docs):
            dk = dk + jnp.where(tk >= ends[d], 1, 0)
            dq = dq + jnp.where(tq >= ends[d], 1, 0)
        near = jnp.abs(tk - tq) <= HALF
        bias_t[b] = jnp.where(jnp.logical_and(dk == dq, near), 0.0, NEG_LARGE).astype(F32)
        return carry

    gather_events(steps[0])
    tables(place)
    gather_events(steps[1])

    own.wait()

    @pl.when(place > 0)
    def _():
        low_copy().wait()

    @pl.when(place < N - 1)
    def _():
        high_copy().wait()

    @pl.when(low_block)
    def _():
        halo_to_next().wait_recv()
        halo_to_prev().wait_send()

    @pl.when(high_block)
    def _():
        halo_to_prev().wait_recv()
        halo_to_next().wait_send()

    @pl.when(first)
    def _():
        xin[0:HALF, :] = halo[0]

    @pl.when(last)
    def _():
        xin[HALF + R:, :] = halo[1]

    gather_events(steps[2])
    own_cot.wait()

    def mask_rows(b, carry):
        rows = pl.ds(pl.multiple_of(b * BLOCK, BLOCK), BLOCK)
        keep = jnp.where(masked[pl.ds(place * NB + b, 1), :] == 1, 1.0, 0.0).astype(F32)
        keep = jnp.broadcast_to(keep, (BLOCK, BLOCK)).T.astype(BF16)
        cot[rows, :] = cot[rows, :] * jnp.concatenate([keep] * (D // BLOCK), axis=1)
        return carry

    lax.fori_loop(0, NB, mask_rows, 0)

    def transposed(dst, src, row0):
        def body(i, carry):
            at = pl.multiple_of(i * 128, 128)
            dst[pl.ds(at, 128), :] = src[row0:row0 + R, pl.ds(at, 128)].astype(F32).T.astype(BF16)
            return carry

        lax.fori_loop(0, D // 128, body, 0)

    transposed(s["ct"], cot, 0)

    for t in range(3, a_step):
        gather_events(steps[t])
    gather_events(steps[a_step][:a_at])

    wqkv, wot, wg, wu, wgo = s["wqkv"], s["wot"], s["wg"], s["wu"], s["wgo"]
    gcol, grow, gsum = s["gcol"], s["grow"], s["gsum"]

    def section(nn, i, lo, up):
        found = []
        for c, (a, b) in enumerate(z.cuts):
            x, y = max(lo, a), min(up, b)
            if x >= y:
                continue
            x0, y0 = (x - a) // 128 * 128, round_up(y - a, 128)
            both = [wb[c][nn, i, k, :, x0:y0] for k in range(2)]
            if SH % 16 == 0:
                v = jnp.concatenate([q[:SH] for q in both], axis=0)
            else:
                v = jnp.concatenate([q.astype(F32)[:SH] for q in both], axis=0).astype(BF16)
            found.append(v[:, x - a - x0:y - a - x0])
        return found[0] if len(found) == 1 else jnp.concatenate(found, axis=1)

    def place_columns(ref, r, at, sections):
        width = sum(v.shape[1] for v in sections)
        ref[pl.ds(r, 2 * SH), at:at + width] = jnp.concatenate(sections, axis=1)

    def unpack_a(i, carry):
        r = pl.multiple_of(i * 2 * SH, 16)
        parts = [section(nn, i, 0, z.LA) for nn in range(N)]
        for k in range(3):
            at = GAIN_LANES + k * QN
            place_columns(wqkv, r, k * D, [v[:, at:at + QN] for v in parts])
        gcol[pl.ds(r, 2 * SH), :] = parts[0][:, 0:128].astype(F32)
        return carry

    lax.fori_loop(0, W // 2, unpack_a, 0)
    grow[...] = gcol[...].T[0:8, :]
    gsum[...] = jnp.zeros((8, D), F32)

    def normed(x):
        centred = x - jnp.mean(x, axis=-1, keepdims=True)
        rstd = lax.rsqrt(jnp.mean(centred * centred, axis=-1, keepdims=True) + EPSILON)
        return centred * rstd, rstd

    n1, qkv = s["n1"], s["qkv"]

    def norm_rows(i, carry):
        r = pl.multiple_of(i * BLOCK, BLOCK)
        hat, _ = normed(xin[pl.ds(r, BLOCK), :].astype(F32))
        n1[pl.ds(r, BLOCK), :] = (hat * grow[0:1, :]).astype(BF16)
        return carry

    def partner_lanes(x):
        lanes = lax.broadcasted_iota(jnp.int32, x.shape, 1)
        return jnp.where(lax.rem(lanes, HEAD_DIM) < HEAD_DIM // 2, pltpu.roll(x, 128 - HEAD_DIM // 2, 1), pltpu.roll(x, HEAD_DIM // 2, 1))

    def project_turned(ct, carry):
        at = pl.multiple_of(ct * 256, 128)
        y = dot(n1[...], wqkv[:, pl.ds(at, 256)], 1, 0)
        scale = jnp.where(ct < D // 256, F32(1.0 / math.sqrt(HEAD_DIM)), F32(1.0))
        for k in range(2):
            part_y = y[:, k * 128:(k + 1) * 128]
            part_y = (part_y * cos_t[...] + partner_lanes(part_y) * sin_t[...]) * scale
            qkv[:, pl.ds(pl.multiple_of(at + k * 128, 128), 128)] = part_y.astype(BF16)
        return carry

    def project(ct, carry):
        at = pl.multiple_of(2 * D + ct * 256, 128)
        qkv[:, pl.ds(at, 256)] = dot(n1[...], wqkv[:, pl.ds(at, 256)], 1, 0).astype(BF16)
        return carry

    def make_qkv():
        lax.fori_loop(0, E // BLOCK, norm_rows, 0)
        lax.fori_loop(0, 2 * D // 256, project_turned, 0)
        lax.fori_loop(0, D // 256, project, 0)

    gather_events(steps[a_step][a_at:])
    make_qkv()

    att, stat = s["att"], s["stat"]
    lane_row = lax.broadcasted_iota(jnp.int32, (BLOCK, 128), 1)
    keep_one = jnp.where(lane_row < HEAD_DIM, 1.0, 0.0).astype(BF16)
    keep_two = jnp.where(lane_row < HEAD_DIM, 0.0, 1.0).astype(BF16)

    def stacked(x):
        return jnp.concatenate([x * keep_one, x * keep_two], axis=0)

    def unstacked(x):
        return jnp.concatenate([x[:HEAD_DIM, :BLOCK], x[HEAD_DIM:, BLOCK:]], axis=0).T

    def unit_refs(j, b):
        lanes = [pl.ds(pl.multiple_of(k * D + j * 128, 128), 128) for k in range(3)]
        return lanes, pl.ds(pl.multiple_of(b * BLOCK, BLOCK), SPAN), pl.ds(pl.multiple_of(b * BLOCK + HALF, 16), BLOCK)

    def unit_scores(j, b):
        (lq, lk, lv), keys, queries = unit_refs(j, b)
        qs = stacked(qkv[queries, lq])
        kp, vp = qkv[keys, lk], qkv[keys, lv]
        pen = bias_t[b]
        return qs, kp, vp, dot(kp, qs, 1, 1) + jnp.concatenate([pen, pen], axis=1)

    G = z.G

    def attend(v, carry):
        j, g = lax.div(v, NB // G), lax.rem(v, NB // G)
        for i in range(G):
            b = g * G + i
            u = j * NB + b
            _, _, vp, scores = unit_scores(j, b)
            top = jnp.max(scores, axis=0, keepdims=True)
            weights = jnp.exp(scores - top)
            inv = 1.0 / jnp.sum(weights, axis=0, keepdims=True)
            stat[u, 0:1, :] = top
            stat[u, 1:2, :] = inv
            got = unstacked(dot(vp, (weights * inv).astype(BF16), 0, 0))
            att[pl.ds(pl.multiple_of(b * BLOCK, BLOCK), BLOCK), pl.ds(pl.multiple_of(j * 128, 128), 128)] = got.astype(BF16)
        return carry

    def attend_part(lo, up):
        lax.fori_loop(lo * (NB // G), up * (NB // G), attend, 0)

    half_pairs = z.pairs // 2
    attend_part(0, half_pairs)
    gather_events(steps[a_step + 1])
    attend_part(half_pairs, z.pairs)
    for t in range(a_step + 2, len(steps)):
        gather_events(steps[t])

    slices_at = GAIN_LANES + 4 * QN

    def unpack_out(i, carry):
        r = pl.multiple_of(i * 2 * SH, 16)
        place_columns(wot, r, 0, [section(nn, i, GAIN_LANES + 3 * QN, slices_at) for nn in range(N)])
        return carry

    def unpack_feed(i, carry):
        r = pl.multiple_of(i * 2 * SH, 16)
        parts = [section(nn, i, slices_at, slices_at + 3 * FN) for nn in range(N)]
        for a, ref in enumerate((wg, wu, wgo)):
            place_columns(ref, r, 0, [v[:, a * FN:(a + 1) * FN] for v in parts])
        return carry

    lax.fori_loop(0, W // 2, unpack_out, 0)
    lax.fori_loop(0, W // 2, unpack_feed, 0)

    ost, n2, res, resg = s["ost"], s["n2"], s["resr"], s["resg"]
    hid, dgate, dup, datt = s["hid"], s["dgate"], s["dup"], s["datt"]
    MB, FC = z.MB, z.FC

    def norm_back(hat, rstd, e, gain):
        eg = e * gain
        return rstd * (eg - jnp.mean(eg, axis=-1, keepdims=True) - hat * jnp.mean(eg * hat, axis=-1, keepdims=True))

    def line_rows(dest, m, rb):
        theirs = m + core * (N - 1 - 2 * m)
        return dest.at[pl.ds(pl.multiple_of(theirs * R + rb * MB, 16), MB)]

    def behind(side):
        return n if side == 0 else N - 1 - n

    def line_copy(dest, rb, key, side, k, stage=None):
        step = 1 - 2 * side
        ref = line_rows(dest, n - step * k, rb)
        src = ref if stage is None else stage.at[pl.ds(pl.multiple_of(rb * MB, 16), MB)]
        return copy_to(src, ref, s[key + "s"].at[rb, side, k], s[key + "r"].at[rb, side, k], (w, n + step))

    def own_copy(stage, dest, rb, key):
        return pltpu.make_async_copy(stage.at[pl.ds(pl.multiple_of(rb * MB, 16), MB)], line_rows(dest, n, rb), s[key + "l"].at[rb])

    def token_send(stage, dest, rb, key):
        own_copy(stage, dest, rb, key).start()
        for side in range(2):
            @pl.when(behind(side) < N - 1)
            def _():
                line_copy(dest, rb, key, side, 0, stage).start()

    hops = {"o": N - 2 if N > 2 else N - 1, "t": N - 1}

    def token_forward(dest, key, k):
        if k > hops[key]:
            return

        def body(rb, carry):
            for side in range(2):
                step = 1 - 2 * side

                @pl.when(behind(side) >= k)
                def _():
                    arrived(line_rows(dest, n - step * k, rb), s[key + "s"].at[rb, side, k - 1], s[key + "r"].at[rb, side, k - 1], (w, n - step))

                if k < hops[key]:
                    @pl.when(jnp.logical_and(behind(side) >= k, behind(side) < N - 1))
                    def _():
                        line_copy(dest, rb, key, side, k).start()
            return carry

        lax.fori_loop(0, z.blocks, body, 0)

    def token_end(stage, dest, key):
        def body(rb, carry):
            own_copy(stage, dest, rb, key).wait()
            for side in range(2):
                for k in range(hops[key]):
                    @pl.when(jnp.logical_and(behind(side) >= k, behind(side) < N - 1))
                    def _():
                        line_copy(dest, rb, key, side, k).wait_send()
            return carry

        lax.fori_loop(0, z.blocks, body, 0)

    def feed(rb, carry):
        r = pl.multiple_of(rb * MB, 16)
        rows = pl.ds(r, MB)
        x = xin[pl.ds(pl.multiple_of(rb * MB + HALF, 16), MB), :].astype(F32)
        residual = x + dot(att[rows, :], wot[...], 1, 1)
        hat, rstd = normed(residual)
        gain = grow[1:2, :]
        n2v = (hat * gain).astype(BF16)
        n2[rows, :] = n2v
        cotv = cot[rows, :]
        total_out, e = residual, None
        for f in range(0, F, FC):
            gate = dot(n2v, wg[:, f:f + FC], 1, 0)
            upv = dot(n2v, wu[:, f:f + FC], 1, 0)
            dh = dot(cotv, wgo[:, f:f + FC], 1, 0)
            sq = gate * gate
            th = jnp.tanh(GELU_A * (gate * (1.0 + GELU_B * sq)))
            half = 0.5 * (1.0 + th)
            act = gate * half
            slope = half + (0.5 * GELU_A) * gate * (1.0 - th * th) * (1.0 + (3.0 * GELU_B) * sq)
            hv = (act * upv).astype(BF16)
            dgv = (dh * upv * slope).astype(BF16)
            duv = (dh * act).astype(BF16)
            hid[rows, f:f + FC] = hv
            dgate[rows, f:f + FC] = dgv
            dup[rows, f:f + FC] = duv
            total_out = total_out + dot(hv, wgo[:, f:f + FC], 1, 1)
            more = dot(dgv, wg[:, f:f + FC], 1, 1) + dot(duv, wu[:, f:f + FC], 1, 1)
            e = more if e is None else e + more
        ost[rows, :] = total_out.astype(BF16)
        token_send(ost, out, rb, "o")
        gsum[1:2, :] = gsum[1:2, :] + jnp.sum(e * hat, axis=0, keepdims=True)
        grad = cotv.astype(F32) + norm_back(hat, rstd, e, gain)
        resg[rows, :] = grad
        low = grad.astype(BF16)
        res[rows, :] = low
        datt[rows, :] = dot(low, wot[...], 1, 0).astype(BF16)
        return carry

    lax.fori_loop(0, z.blocks, feed, 0)

    for c in pending:
        c.wait_send()
    pending.clear()

    def store_rows(c, nn, i, k, value):
        if RS > SH:
            value = jnp.concatenate([value, jnp.zeros((RS - SH, value.shape[1]), F32)], axis=0)
        wb[c][nn, i, k] = value.astype(BF16)

    HT, TM = z.HT, z.TM
    owx = s["owx"]

    def store_part(chunks, nn, t, value):
        lo = z.cuts[chunks[0]][0]
        for c in chunks:
            a, b = z.cuts[c]
            for i in range(HT):
                for k in range(2):
                    at = (2 * i + k) * SH
                    store_rows(c, nn, t * HT + i, k, value[at:at + SH, a - lo:b - lo])

    def grads_b(t, carry):
        r = pl.multiple_of(t * TM, 16)
        cols = pl.ds(pl.multiple_of(t * TM, 128), TM) if TM % 128 == 0 else None
        gg = dot(s["n2t"][pl.ds(r, TM), :], dgate[...], 1, 0)
        gu = dot(s["n2t"][pl.ds(r, TM), :], dup[...], 1, 0)
        go = dot(s["ct"][pl.ds(r, TM), :], hid[...], 1, 0)
        gw = dot(s["rt"][pl.ds(r, TM), :], att[...], 1, 0)
        if z.O0:
            firsts = [gw[:, nn * QN:nn * QN + z.O0] for nn in range(N)]
            spare = owx.shape[1] - N * z.O0
            if spare:
                firsts.append(jnp.zeros((TM, spare), F32))
            owx[pl.ds(r, TM), :] = jnp.concatenate(firsts, axis=1)
        for nn in range(N):
            pieces = [gw[:, nn * QN + z.O0:(nn + 1) * QN]] + [v[:, nn * FN:(nn + 1) * FN] for v in (gg, gu, go)]
            if z.lanes > z.real:
                pieces.append(jnp.zeros((TM, z.lanes - z.real), F32))
            store_part(list(range(z.CA, C)), nn, t, jnp.concatenate(pieces, axis=1))
        return carry

    scatter_order = [list(range(z.bits)), list(range(z.bits))[::-1]]

    def slot_base(t):
        return sum(1 << (z.bits - 1 - u) for u in range(t))

    def r0_start(c):
        send(wb[c].at[:, :, 1 - core], r0[c], s["g0s"].at[c], s["g0r"].at[c], sib_dev)

    def r0_finish(c):
        arrived(r0[c], s["g0s"].at[c], s["g0r"].at[c], sib_dev)

        def body(i, carry):
            for nn in range(N):
                wb[c][nn, i, core] = (wb[c][nn, i, core].astype(F32) + r0[c][nn, i].astype(F32)).astype(BF16)
            return carry

        lax.fori_loop(0, W // 2, body, 0)

    def r1_start(c, t):
        for h in range(2):
            b = scatter_order[h][t]
            for i, combo in enumerate(combos(scatter_order[h][t + 1:])):
                slot = slot_base(t) + i
                send(wb[c].at[half_refs[h], flip(hi, combo + [b]), core], r1[c].at[h, slot], s["g1s"].at[c, h, slot], s["g1r"].at[c, h, slot], bit_dev(b))

    def r1_finish(c, t):
        for h in range(2):
            b = scatter_order[h][t]
            for i, combo in enumerate(combos(scatter_order[h][t + 1:])):
                slot = slot_base(t) + i
                arrived(r1[c].at[h, slot], s["g1s"].at[c, h, slot], s["g1r"].at[c, h, slot], bit_dev(b))
                hv = flip(hi, combo)
                for nn in range(N2):
                    at = h * N2 + nn
                    wb[c][at, hv, core] = (wb[c][at, hv, core].astype(F32) + r1[c][h, slot, nn].astype(F32)).astype(BF16)

    def rz_copy(c, side, d):
        step = 1 - 2 * side
        return copy_to(wb[c].at[n + step * (1 + d), hi, core], rz[c].at[side, d], s["g2s"].at[c, side, d], s["g2r"].at[c, side, d], (w, n + step))

    def rz_round(c, r):
        for side in range(2):
            step = 1 - 2 * side

            @pl.when(behind(side) == r)
            def _():
                if r > 0:
                    for d in range(N - r):
                        arrived(rz[c].at[side, d], s["g2s"].at[c, side, d], s["g2r"].at[c, side, d], (w, n - step))
                    for d in range(1, N - r):
                        m = n + step * d
                        wb[c][m, hi, core] = (wb[c][m, hi, core].astype(F32) + rz[c][side, d].astype(F32)).astype(BF16)
                for d in range(N - 1 - r):
                    rz_copy(c, side, d).start()

    def rz_sent(c):
        for side in range(2):
            for r in range(N - 1):
                @pl.when(behind(side) == r)
                def _():
                    for d in range(N - 1 - r):
                        rz_copy(c, side, d).wait_send()

    def rz_finish(c):
        lo, up = z.cuts[c]
        gp[:, lo:up] = wb[c][n, hi, core].astype(F32)
        for side in range(2):
            @pl.when(behind(side) > 0)
            def _():
                gp[:, lo:up] = gp[:, lo:up] + rz[c][side, 0].astype(F32)

    last_stage = z.bits + 1 + N

    def scatter_advance(chunks, st):
        for c in chunks:
            if st == 0:
                r0_start(c)
            elif st <= z.bits + 1:
                if st == 1:
                    r0_finish(c)
                else:
                    r1_finish(c, st - 2)
                if st <= z.bits:
                    r1_start(c, st - 1)
                else:
                    rz_round(c, 0)
            else:
                rz_round(c, st - z.bits - 1)
                if st == last_stage - 1:
                    rz_finish(c)

    part_a, part_b = list(range(z.CA)), list(range(z.CA, C))
    transposed(s["n2t"], n2, 0)
    transposed(s["rt"], res, 0)
    lax.fori_loop(0, D // TM, grads_b, 0)

    scatter_advance(part_b, 0)

    dkv, edge, rim, rimr = s["dkv"], s["edge"], s["rim"], s["rimr"]
    dk_ref, dv_ref = dkv.at[0], dkv.at[1]

    def attend_back(j, carry):
        dkv[:, 0:BLOCK, :] = jnp.zeros((2, BLOCK, 128), F32)

        def group(g, inner):
            tails = None
            for i in range(G):
                b = g * G + i
                u = j * NB + b
                (lq, lk, lv), keys, queries = unit_refs(j, b)
                qs, kp, vp, scores = unit_scores(j, b)
                probs = jnp.exp(scores - stat[u, 0:1, :]) * stat[u, 1:2, :]
                gs = stacked(datt[pl.ds(pl.multiple_of(b * BLOCK, BLOCK), BLOCK), pl.ds(pl.multiple_of(j * 128, 128), 128)])
                prob_grad = dot(vp, gs, 1, 1)
                row_dot = jnp.sum(probs * prob_grad, axis=0, keepdims=True)
                score_grad = (probs * (prob_grad - row_dot)).astype(BF16)
                parts = (dot(score_grad, qs, 1, 0), dot(probs.astype(BF16), gs, 1, 0))
                dq = unstacked(dot(kp, score_grad, 0, 0)) * F32(1.0 / math.sqrt(HEAD_DIM))
                dq = dq * cos_t[queries, :] - partner_lanes(dq) * sin_t[queries, :]
                qkv[queries, lq] = dq.astype(BF16)
                here = pl.ds(pl.multiple_of(b * BLOCK, BLOCK), BLOCK)
                for k in range(2):
                    before = dkv[k, here, :] if tails is None else tails[k]
                    dkv[k, here, :] = before + parts[k][:BLOCK]
                tails = [x[BLOCK:] for x in parts]
            after = pl.ds(pl.multiple_of(g * G * BLOCK + G * BLOCK, BLOCK), BLOCK)
            for k in range(2):
                dkv[k, after, :] = tails[k]
            return inner

        lax.fori_loop(0, NB // G, group, 0)
        (_, lk, lv), _, _ = unit_refs(j, 0)
        lj = pl.ds(pl.multiple_of(j * 128, 128), 128)
        for k, ref in enumerate((dk_ref, dv_ref)):
            wide_lanes = pl.ds(pl.multiple_of(k * D + j * 128, 128), 128)
            rim[0, :, wide_lanes] = ref[0:HALF, :].astype(BF16)
            rim[1, :, wide_lanes] = ref[E - HALF:, :].astype(BF16)
            edge[0, :, wide_lanes] = ref[HALF:WINDOW, :]
            edge[1, :, wide_lanes] = ref[R:R + HALF, :]
        mid = slice(HALF, HALF + R)
        dk = dk_ref[mid, :]
        qkv[mid, lk] = (dk * cos_t[mid, :] - partner_lanes(dk) * sin_t[mid, :]).astype(BF16)
        qkv[mid, lv] = dv_ref[mid, :].astype(BF16)
        return carry

    lax.fori_loop(0, half_pairs, attend_back, 0)
    token_forward(out, "o", 1)
    lax.fori_loop(half_pairs, z.pairs, attend_back, 0)

    def rim_to_prev():
        return copy_to(rim.at[0], rimr.at[1], s["rs"].at[0], s["rr"].at[1], prev_dev)

    def rim_to_next():
        return copy_to(rim.at[1], rimr.at[0], s["rs"].at[1], s["rr"].at[0], next_dev)

    @pl.when(has_prev)
    def _():
        rim_to_prev().start()

    @pl.when(has_next)
    def _():
        rim_to_next().start()

    @pl.when(jnp.logical_not(has_prev))
    def _():
        rimr[0] = jnp.zeros((HALF, 2 * D), BF16)

    @pl.when(jnp.logical_not(has_next))
    def _():
        rimr[1] = jnp.zeros((HALF, 2 * D), BF16)

    scatter_advance(part_b, 1)
    transposed(s["rt"], n1, HALF)

    @pl.when(has_prev)
    def _():
        rim_to_next().wait_recv()

    @pl.when(has_next)
    def _():
        rim_to_prev().wait_recv()

    @pl.when(has_prev)
    def _():
        rim_to_prev().wait_send()

    @pl.when(has_next)
    def _():
        rim_to_next().wait_send()

    for side, row in ((0, HALF), (1, R)):
        rows = slice(row, row + HALF)
        for j in range(z.pairs):
            lk = slice(j * 128, (j + 1) * 128)
            lv = slice(D + j * 128, D + (j + 1) * 128)
            dk = edge[side, :, lk] + rimr[side, :, lk].astype(F32)
            dv = edge[side, :, lv] + rimr[side, :, lv].astype(F32)
            dk = dk * cos_t[rows, :] - partner_lanes(dk) * sin_t[rows, :]
            qkv[rows, D + j * 128:D + (j + 1) * 128] = dk.astype(BF16)
            qkv[rows, 2 * D + j * 128:2 * D + (j + 1) * 128] = dv.astype(BF16)

    tst = n2

    def input_grad(rb, carry):
        rows = pl.ds(pl.multiple_of(rb * MB, 16), MB)
        ext = pl.ds(pl.multiple_of(rb * MB + HALF, 16), MB)
        e = dot(qkv[ext, :], wqkv[...], 1, 1)
        hat, rstd = normed(xin[ext, :].astype(F32))
        gsum[0:1, :] = gsum[0:1, :] + jnp.sum(e * hat, axis=0, keepdims=True)
        tst[rows, :] = (resg[rows, :] + norm_back(hat, rstd, e, grow[0:1, :])).astype(BF16)
        token_send(tst, tg, rb, "t")
        return carry

    lax.fori_loop(0, z.blocks, input_grad, 0)

    gcol[...] = jnp.concatenate([gsum[...], jnp.zeros((120, D), F32)], axis=0).T

    def grads_a(t, carry):
        r = pl.multiple_of(t * TM, 16)
        g = [dot(s["rt"][pl.ds(r, TM), :], qkv[HALF:HALF + R, k * D:(k + 1) * D], 1, 0) for k in range(3)]
        gains = gcol[pl.ds(r, TM), 0:GAIN_LANES]
        for nn in range(N):
            pieces = [gains] + [v[:, nn * QN:(nn + 1) * QN] for v in g]
            if z.O0:
                pieces.append(owx[pl.ds(r, TM), nn * z.O0:(nn + 1) * z.O0])
            store_part(part_a, nn, t, jnp.concatenate(pieces, axis=1))
        return carry

    lax.fori_loop(0, D // TM, grads_a, 0)
    scatter_advance(part_a, 0)
    scatter_advance(part_b, 2)
    for k in range(2, N):
        token_forward(out, "o", k)
    token_end(ost, out, "o")

    far = N - 1 - place

    def far_rows():
        return pltpu.make_async_copy(tokens.at[pl.ds(pl.multiple_of(far * R, 16), R)], xin.at[pl.ds(HALF, R)], s["l_tok"].at[0])

    def far_low():
        return pltpu.make_async_copy(tokens.at[pl.ds(T - R - HALF, HALF)], xin.at[pl.ds(0, HALF)], s["l_tok"].at[1])

    def far_high():
        return pltpu.make_async_copy(tokens.at[pl.ds(R, HALF)], xin.at[pl.ds(HALF + R, HALF)], s["l_tok"].at[2])

    def far_feed(rb, carry):
        r = pl.multiple_of(rb * MB, 16)
        rows = pl.ds(r, MB)
        x = xin[pl.ds(pl.multiple_of(rb * MB + HALF, 16), MB), :].astype(F32)
        residual = x + dot(att[rows, :], wot[...], 1, 1)
        n2v = (normed(residual)[0] * grow[1:2, :]).astype(BF16)
        total_out = residual
        for f in range(0, F, FC):
            gate = dot(n2v, wg[:, f:f + FC], 1, 0)
            upv = dot(n2v, wu[:, f:f + FC], 1, 0)
            act = gate * (0.5 * (1.0 + jnp.tanh(GELU_A * (gate * (1.0 + GELU_B * (gate * gate))))))
            total_out = total_out + dot((act * upv).astype(BF16), wgo[:, f:f + FC], 1, 1)
        ost[rows, :] = total_out.astype(BF16)
        return carry

    def far_out():
        return pltpu.make_async_copy(ost, out.at[pl.ds(pl.multiple_of(far * R, 16), R)], s["ol"].at[0])

    def far_project():
        far_rows().start()

        @pl.when(first)
        def _():
            far_low().start()
            xin[HALF + R:, :] = halo[1]

        @pl.when(last)
        def _():
            far_high().start()
            xin[0:HALF, :] = halo[0]

        tables(far)
        far_rows().wait()

        @pl.when(first)
        def _():
            far_low().wait()

        @pl.when(last)
        def _():
            far_high().wait()

        make_qkv()

    def far_finish():
        lax.fori_loop(0, z.blocks, far_feed, 0)
        far_out().start()
        far_out().wait()

    def at_ends(work):
        if N > 2:
            pl.when(at_end)(work)

    at_ends(far_project)
    scatter_advance(part_a, 1)
    token_forward(tg, "t", 1)
    at_ends(lambda: attend_part(0, half_pairs))
    for st in range(3, z.bits + 2):
        scatter_advance(part_b, st)
    at_ends(lambda: attend_part(half_pairs, z.pairs))
    scatter_advance(part_a, 2)
    scatter_advance(part_b, z.bits + 2)
    if N > 2:
        token_forward(tg, "t", 2)
    at_ends(far_finish)
    for st in range(3, z.bits + 2):
        scatter_advance(part_a, st)
    for st in range(z.bits + 3, last_stage):
        scatter_advance(part_b, st)
    for st in range(z.bits + 2, last_stage):
        scatter_advance(part_a, st)
    for k in range(3, N):
        token_forward(tg, "t", k)

    for c in pending:
        c.wait_send()
    for c in range(C):
        rz_sent(c)
    token_end(tst, tg, "t")


def run_layer(z, *args):
    shapes, names = [], []

    def vmem(name, shape, dtype):
        names.append(name)
        shapes.append(pltpu.VMEM(shape, dtype))

    def sems(name, *shape):
        names.append(name)
        shapes.append(pltpu.SemaphoreType.DMA(shape))

    W, N, D, F, R, E, C = z.W, z.N, z.D, z.F, z.R, z.E, z.C
    for c, (lo, up) in enumerate(z.cuts):
        vmem(f"wb{c}", (N, W // 2, 2, z.RS, up - lo), BF16)
        vmem(f"r0{c}", (N, W // 2, z.RS, up - lo), BF16)
        vmem(f"r1{c}", (2, W // 2 - 1, N // 2, z.RS, up - lo), BF16)
        vmem(f"rz{c}", (2, N - 1, z.RS, up - lo), BF16)
    vmem("xin", (E, D), BF16)
    vmem("halo", (2, HALF, D), BF16)
    vmem("n1", (E, D), BF16)
    vmem("qkv", (E, 3 * D), BF16)
    vmem("wqkv", (D, 3 * D), BF16)
    vmem("wot", (D, D), BF16)
    for name in ("wg", "wu", "wgo"):
        vmem(name, (D, F), BF16)
    vmem("gcol", (D, 128), F32)
    vmem("grow", (8, D), F32)
    vmem("gsum", (8, D), F32)
    vmem("owx", (D, round_up(max(N * z.O0, 1), 128)), F32)
    vmem("cos", (E, 128), F32)
    vmem("sin", (E, 128), F32)
    vmem("bias", (z.NB, SPAN, BLOCK), F32)
    vmem("stat", (z.pairs * z.NB, 8, 2 * BLOCK), F32)
    vmem("pk", (z.RS, z.lanes), BF16)
    for name in ("att", "ost", "n2", "resr", "datt", "cot"):
        vmem(name, (R, D), BF16)
    for name in ("n2t", "ct", "rt"):
        vmem(name, (D, R), BF16)
    vmem("resg", (R, D), F32)
    for name in ("hid", "dgate", "dup"):
        vmem(name, (R, F), BF16)
    vmem("dkv", (2, E, 128), F32)
    vmem("edge", (2, HALF, 2 * D), F32)
    vmem("rim", (2, HALF, 2 * D), BF16)
    vmem("rimr", (2, HALF, 2 * D), BF16)
    sems("l_own", C)
    sems("l_tok", 4)
    for name in ("zs", "zr"):
        sems(name, C, N - 1)
    for name in ("g2s", "g2r"):
        sems(name, C, 2, N - 1)
    for name in ("ss", "sr", "g1s", "g1r"):
        sems(name, C, 2, W // 2 - 1)
    for name in ("ds", "dr"):
        sems(name, C, 2, W // 2)
    for name in ("g0s", "g0r"):
        sems(name, C)
    for name in ("hs", "hr", "rs", "rr"):
        sems(name, 2)
    for name in ("ol", "tl"):
        sems(name, z.blocks)
    for name in ("os", "or", "ts", "tr"):
        sems(name, z.blocks, 2, N - 1)
    hbm = pl.BlockSpec(memory_space=pl.ANY)
    vm = pl.BlockSpec(memory_space=pltpu.VMEM)
    return pl.pallas_call(
        functools.partial(layer_kernel, z, names),
        out_shape=(
            jax.ShapeDtypeStruct((z.T, D), BF16),
            jax.ShapeDtypeStruct((z.T, D), BF16),
            jax.ShapeDtypeStruct((z.RS, z.lanes), F32),
        ),
        in_specs=[pl.BlockSpec(memory_space=pltpu.SMEM), hbm, hbm] + [vm] * 7,
        out_specs=(hbm, hbm, vm),
        scratch_shapes=shapes,
        compiler_params=pltpu.CompilerParams(collective_id=0, has_side_effects=True, vmem_limit_bytes=VMEM_BYTES),
    )(*args)


VMEM_BYTES = 64 * 1024 * 1024 - 1024 * 64


def finish_kernel(z, tg, out, gp, o_out, o_tg, o_in, o_ow, o_gu, o_dn, o_one, o_two, low, full, same, s_in, s_out, s_same_in, s_same_out):
    rows = FINISH_ROWS
    steps = z.T // rows

    def part(i):
        return pl.ds(i * rows, rows)

    loads = [pltpu.make_async_copy(tg.at[part(i)], low.at[part(i)], s_in.at[i]) for i in range(steps)]
    same_loads = [pltpu.make_async_copy(out.at[part(i)], same.at[part(i)], s_same_in.at[i]) for i in range(steps)]
    stores = [pltpu.make_async_copy(full.at[part(i)], o_tg.at[part(i)], s_out.at[i]) for i in range(steps)]
    same_stores = [pltpu.make_async_copy(same.at[part(i)], o_out.at[part(i)], s_same_out.at[i]) for i in range(steps)]
    for i in range(steps):
        loads[i].start()
    for c in same_loads:
        c.start()
    for i in range(steps):
        loads[i].wait()
        full[part(i), :] = low[part(i), :].astype(F32)
        stores[i].start()
    for i in range(steps):
        same_loads[i].wait()
        same_stores[i].start()
    unpack_grads(z, gp, o_in, o_ow, o_gu, o_dn, o_one, o_two)
    for c in stores + same_stores:
        c.wait()


def unpack_grads(z, gp, o_in, o_ow, o_gu, o_dn, o_one, o_two):
    SH, QN, FN = z.SH, z.QN, z.FN
    heads = QN // HEAD_DIM
    value = gp[...][:SH]

    def flipped(x):
        a, b = x.shape
        a2, b2 = round_up(a, 128), round_up(b, 128)
        if b2 > b:
            x = jnp.concatenate([x, jnp.zeros((a, b2 - b), F32)], axis=1)
        if a2 > a:
            x = jnp.concatenate([x, jnp.zeros((a2 - a, b2), F32)], axis=0)
        return x.T[:b, :a]

    at = GAIN_LANES
    o_in[...] = jnp.concatenate(
        [value[:, at + k * QN + a * HEAD_DIM:at + k * QN + (a + 1) * HEAD_DIM] for a in range(heads) for k in range(3)], axis=1)
    at += 3 * QN
    o_ow[...] = flipped(value[:, at:at + QN])
    at += QN
    for k in range(2):
        o_gu[:, k, :] = value[:, at + k * FN:at + (k + 1) * FN]
    at += 2 * FN
    o_dn[...] = flipped(value[:, at:at + FN])
    rows = flipped(value[:, :128])
    o_one[...] = rows[0:1, :]
    o_two[...] = rows[1:2, :]


def finish(z, tg, out, gp):
    rows = FINISH_ROWS
    hbm = pl.BlockSpec(memory_space=pl.ANY)
    vm = pl.BlockSpec(memory_space=pltpu.VMEM)
    return pl.pallas_call(
        functools.partial(finish_kernel, z),
        out_shape=(
            jax.ShapeDtypeStruct((z.T, z.D), BF16),
            jax.ShapeDtypeStruct((z.T, z.D), F32),
            jax.ShapeDtypeStruct((z.SH, 3 * z.QN), F32),
            jax.ShapeDtypeStruct((z.QN, z.SH), F32),
            jax.ShapeDtypeStruct((z.SH, 2, z.FN), F32),
            jax.ShapeDtypeStruct((z.FN, z.SH), F32),
            jax.ShapeDtypeStruct((1, z.SH), F32),
            jax.ShapeDtypeStruct((1, z.SH), F32),
        ),
        in_specs=[hbm, hbm, vm],
        out_specs=(hbm, hbm) + (vm,) * 6,
        scratch_shapes=[
            pltpu.VMEM((z.T, z.D), BF16),
            pltpu.VMEM((z.T, z.D), F32),
            pltpu.VMEM((z.T, z.D), BF16),
            pltpu.SemaphoreType.DMA((z.T // rows,)),
            pltpu.SemaphoreType.DMA((z.T // rows,)),
            pltpu.SemaphoreType.DMA((z.T // rows,)),
            pltpu.SemaphoreType.DMA((z.T // rows,)),
        ],
        compiler_params=pltpu.CompilerParams(vmem_limit_bytes=VMEM_BYTES),
    )(tg, out, gp)


def per_device(tokens, lengths, masked, attention_in, attention_out, geglu_in, geglu_out, gain_attention, gain_feedforward, out_grad):
    wide, narrow = lax.axis_size("wide"), lax.axis_size("narrow")
    z = Sizes(wide, narrow, tokens.shape[0], tokens.shape[1], attention_out.shape[0] * narrow, geglu_out.shape[0] * narrow, lengths.shape[0])
    gains = [g.reshape(1, z.SH) for g in (gain_attention, gain_feedforward)]
    out, tg, gp = run_layer(
        z, lengths, tokens, out_grad, masked.reshape(-1, 128), attention_in, attention_out, geglu_in, geglu_out, *gains)
    out, tg, g_in, g_out, g_gu, g_down, one, two = finish(z, tg, out, gp)
    return (out, tg, g_in, g_out, g_gu, g_down, one.reshape(z.SH), two.reshape(z.SH))


def solution(mesh):
    return jax.shard_map(
        per_device,
        mesh=mesh,
        in_specs=(P("wide", None), P(), P("wide"), P("wide", "narrow"), P("narrow", "wide"), P("wide", None, "narrow"),
                  P("narrow", "wide"), P("wide"), P("wide"), P("wide", None)),
        out_specs=(P("wide", None), P("wide", None), P("wide", "narrow"), P("narrow", "wide"), P("wide", None, "narrow"),
                   P("narrow", "wide"), P("wide"), P("wide")),
        check_vma=False,
    )
```

```python
import functools
import itertools
import math

import jax
import jax.numpy as jnp
from jax import lax
from jax.experimental import pallas as pl
from jax.experimental.pallas import tpu as pltpu
from jax.sharding import PartitionSpec as P

MESH = pl.DeviceIdType.MESH
HEAD_DIM = 64
WINDOW = 128
HALF = WINDOW // 2
BLOCK = 128
FINISH_ROWS = 256
SPAN = BLOCK + WINDOW
GAIN_LANES = 32
EPSILON = 1e-05
THETA = 10000.0
NEG_LARGE = -1e30
F32 = jnp.float32
BF16 = jnp.bfloat16
GELU_A = math.sqrt(2.0 / math.pi)
GELU_B = 0.044715


def round_up(value, unit):
    return -(-value // unit) * unit


def dot(a, b, ca, cb):
    return lax.dot_general(a, b, (((ca,), (cb,)), ((), ())), preferred_element_type=F32)


class Sizes:
    def __init__(self, wide, narrow, tok_rows, width, heads_width, hidden, docs):
        self.W, self.N, self.T, self.D, self.F, self.docs = wide, narrow, tok_rows, width, hidden, docs
        self.R = tok_rows // narrow
        self.E = self.R + WINDOW
        self.NB = self.R // BLOCK
        self.pairs = width // 128
        self.G = next(g for g in (4 if self.R <= 512 else 2, 2, 1) if self.NB % g == 0)
        self.SH = width // wide
        self.RS = round_up(self.SH, 16)
        self.UG = next(g for g in (1, 2, 4, 8) if g * 2 * self.SH % 16 == 0)
        self.QN, self.FN = heads_width // narrow, hidden // narrow
        self.bits = (wide // 2).bit_length() - 1
        first = GAIN_LANES + 3 * self.QN
        self.real = first + self.QN + 3 * self.FN
        self.LA = round_up(first, 128)
        self.lanes = round_up(self.real, 128)
        self.O0 = self.LA - first
        cut_a = (self.LA // 256) * 128
        tiles = (self.lanes - self.LA) // 128
        end_one = self.LA + (3 * tiles // 8) * 128
        end_two = end_one + (tiles // 4) * 128
        self.cuts = [(0, cut_a), (cut_a, self.LA), (self.LA, end_one), (end_one, end_two), (end_two, self.lanes)]
        self.C = len(self.cuts)
        self.CA = 2
        self.keep = self.R <= 512 and self.SH == self.RS
        self.CZ = self.C - 1
        self.MB = min(self.R, 256)
        self.blocks = self.R // self.MB
        self.FC = 384 if hidden % 384 == 0 else hidden
        self.HT = max(1, 192 // (2 * self.SH))
        self.TM = self.HT * 2 * self.SH


def combos(bit_list):
    out = []
    for mask in range(1 << len(bit_list)):
        out.append([b for i, b in enumerate(bit_list) if mask >> i & 1])
    return out


def layer_kernel(z, names, lengths, tokens, grads_in, masked, w_in, w_out, w_gu, w_down, gain_one, gain_two, out, tg, gp, *scratch):
    s = dict(zip(names, scratch))
    W, N, T, D, F, R, E, NB = z.W, z.N, z.T, z.D, z.F, z.R, z.E, z.NB
    C, SH, RS, N2 = z.C, z.SH, z.RS, z.N // 2
    wb = [s[f"wb{c}"] for c in range(C)]
    pk, cot = s["pk"], s["cot"]
    r0 = [s[f"r0{c}"] for c in range(C)]
    r1 = [s[f"r1{c}"] for c in range(C)]
    rz = [s[f"rz{c}"] for c in range(C)]
    w, n = lax.axis_index("wide"), lax.axis_index("narrow")
    core, hi = lax.rem(w, 2), lax.div(w, 2)
    place = n + core * (N - 1 - 2 * n)
    ahead = 1 - 2 * core
    first, last = place == 0, place == N - 1
    has_prev = jnp.logical_or(place > 0, w > 0)
    has_next = jnp.logical_or(place < N - 1, w < W - 1)
    prev_dev = (jnp.where(first, w - 1, w), jnp.where(first, n, n - ahead))
    next_dev = (jnp.where(last, w + 1, w), jnp.where(last, n, n + ahead))
    at_end = jnp.logical_or(first, last)
    low_block = jnp.logical_and(at_end, w > 0)
    high_block = jnp.logical_and(at_end, w < W - 1)
    sib_dev = (w + 1 - 2 * core, n)

    def around(k):
        return lax.rem(n + k + N, N)

    def flip(value, bit_list):
        for b in bit_list:
            value = value + (1 - 2 * lax.rem(lax.div(hi, 1 << b), 2)) * (1 << b)
        return value

    def bit_dev(b):
        return (2 * flip(hi, [b]) + core, n)

    pending = []

    def copy_to(src, dst, send, recv, dev):
        return pltpu.make_async_remote_copy(src_ref=src, dst_ref=dst, send_sem=send, recv_sem=recv, device_id=dev, device_id_type=MESH)

    def send(src, dst, send_sem, recv_sem, dev):
        c = copy_to(src, dst, send_sem, recv_sem, dev)
        c.start()
        pending.append(c)

    def arrived(dst, send_sem, recv_sem, dev):
        copy_to(dst, dst, send_sem, recv_sem, dev).wait_recv()

    barrier = pltpu.get_barrier_semaphore()
    partners = [(w, around(k)) for k in range(1, N)] + [bit_dev(b) for b in range(z.bits)] + [sib_dev]
    for dev in partners:
        pl.semaphore_signal(barrier, inc=1, device_id=dev, device_id_type=MESH)

    @pl.when(low_block)
    def _():
        pl.semaphore_signal(barrier, inc=1, device_id=(w - 1, n), device_id_type=MESH)

    @pl.when(high_block)
    def _():
        pl.semaphore_signal(barrier, inc=1, device_id=(w + 1, n), device_id_type=MESH)


    def flipped(x):
        a, b = x.shape
        a2, b2 = round_up(a, 128), round_up(b, 128)
        if b2 > b:
            x = jnp.concatenate([x, jnp.zeros((a, b2 - b), F32)], axis=1)
        if a2 > a:
            x = jnp.concatenate([x, jnp.zeros((a2 - a, b2), F32)], axis=0)
        return x.T[:b, :a]

    def pack(lo, up, pieces):
        have = sum(p.shape[1] for p in pieces)
        if up - lo > have:
            pieces = pieces + [jnp.zeros((SH, up - lo - have), F32)]
        value = jnp.concatenate(pieces, axis=1)
        if RS > SH:
            value = jnp.concatenate([value, jnp.zeros((RS - SH, up - lo), F32)], axis=0)
        pk[:, lo:up] = value.astype(BF16)

    QN, FN = z.QN, z.FN
    heads = QN // HEAD_DIM
    raw_in, out_t = w_in[...], flipped(w_out[...])
    gain_rows = jnp.concatenate([gain_one[...], gain_two[...], jnp.zeros((6, SH), F32)], axis=0)
    gain_cols = jnp.concatenate([flipped(gain_rows), jnp.zeros((SH, GAIN_LANES - 8), F32)], axis=1)
    pack(0, z.LA, [gain_cols] + [raw_in[:, (3 * a + k) * HEAD_DIM:(3 * a + k + 1) * HEAD_DIM] for k in range(3) for a in range(heads)] + [out_t[:, :z.O0]])
    pl.semaphore_wait(barrier, len(partners) + low_block.astype(jnp.int32) + high_block.astype(jnp.int32))

    half_refs = [pl.ds(h * N2, N2) for h in range(2)]
    gather_order = [list(range(z.bits))[::-1], list(range(z.bits))]

    def z_start(c):
        lo, up = z.cuts[c]
        src = pk.at[:, lo:up]
        pltpu.make_async_copy(src, wb[c].at[n, hi, core], s["l_own"].at[c]).start()
        for k in range(1, N):
            send(src, wb[c].at[n, hi, core], s["zs"].at[c, k - 1], s["zr"].at[c, k - 1], (w, around(k)))

    def z_wait(c):
        lo, up = z.cuts[c]
        pltpu.make_async_copy(pk.at[:, lo:up], wb[c].at[n, hi, core], s["l_own"].at[c]).wait()
        for k in range(1, N):
            arrived(wb[c].at[around(-k), hi, core], s["zs"].at[c, k - 1], s["zr"].at[c, k - 1], (w, around(-k)))

    def s_start(c, t):
        for h in range(2):
            b = gather_order[h][t]
            for i, combo in enumerate(combos(gather_order[h][:t])):
                ref = wb[c].at[half_refs[h], flip(hi, combo), core]
                slot = (1 << t) - 1 + i
                send(ref, ref, s["ss"].at[c, h, slot], s["sr"].at[c, h, slot], bit_dev(b))

    def s_wait(c, t):
        for h in range(2):
            b = gather_order[h][t]
            for i, combo in enumerate(combos(gather_order[h][:t])):
                ref = wb[c].at[half_refs[h], flip(hi, combo + [b]), core]
                slot = (1 << t) - 1 + i
                arrived(ref, s["ss"].at[c, h, slot], s["sr"].at[c, h, slot], bit_dev(b))

    def d_start(c, late):
        for h in range(2):
            everyone = combos(gather_order[h])
            for i, combo in enumerate(everyone):
                if (i >= len(everyone) // 2) == late:
                    ref = wb[c].at[half_refs[h], flip(hi, combo), core]
                    send(ref, ref, s["ds"].at[c, h, i], s["dr"].at[c, h, i], sib_dev)

    def d_wait(c):
        for h in range(2):
            for i, combo in enumerate(combos(gather_order[h])):
                arrived(wb[c].at[half_refs[h], flip(hi, combo), 1 - core], s["ds"].at[c, h, i], s["dr"].at[c, h, i], sib_dev)

    stages = z.bits + 2

    def gather_event(c, st):
        if st == 0:
            z_wait(c)
            if c + 1 < z.CZ:
                z_start(c + 1)
        elif st <= z.bits:
            s_wait(c, st - 1)
        else:
            d_wait(c)
        if st < z.bits:
            s_start(c, st)
        if st == z.bits - 1:
            d_start(c, False)
        if st == z.bits:
            d_start(c, True)

    L = C - 1
    l_lanes = z.cuts[L][1] - z.cuts[L][0]
    half_lanes = [slice(0, round_up(l_lanes // 2, 128)), slice(round_up(l_lanes // 2, 128), l_lanes)]

    def behind(side):
        return n if side == 0 else N - 1 - n

    def l_own():
        return pltpu.make_async_copy(pk.at[:, z.cuts[L][0]:], wb[L].at[n, hi, core], s["l_own"].at[L])

    def l_start(t):
        for h in range(2):
            b = gather_order[h][t]
            for i, combo in enumerate(combos(gather_order[h][:t])):
                ref = wb[L].at[n, flip(hi, combo), core, :, half_lanes[h]]
                slot = (1 << t) - 1 + i
                send(ref, ref, s["ss"].at[L, h, slot], s["sr"].at[L, h, slot], bit_dev(b))

    def l_wait(t):
        for h in range(2):
            b = gather_order[h][t]
            for i, combo in enumerate(combos(gather_order[h][:t])):
                ref = wb[L].at[n, flip(hi, combo + [b]), core, :, half_lanes[h]]
                slot = (1 << t) - 1 + i
                arrived(ref, s["ss"].at[L, h, slot], s["sr"].at[L, h, slot], bit_dev(b))

    def hop_copy(side, k):
        step = 1 - 2 * side
        ref = wb[L].at[n - step * k, :, core]
        return copy_to(ref, ref, s["lzs"].at[side, k], s["lzr"].at[side, k], (w, n + step))

    def core_copy(side, k, whose):
        ref = wb[L].at[n - (1 - 2 * side) * k, :, whose]
        return copy_to(ref, ref, s["lds"].at[side, k], s["ldr"].at[side, k], sib_dev)

    def l_own_group():
        core_copy(0, 0, core).start()
        for side in range(2):
            @pl.when(behind(side) < N - 1)
            def _():
                hop_copy(side, 0).start()

    def l_hop(k):
        for side in range(2):
            step = 1 - 2 * side

            @pl.when(behind(side) > k)
            def _():
                arrived(wb[L].at[n - step * (k + 1), :, core], s["lzs"].at[side, k], s["lzr"].at[side, k], (w, n - step))
                core_copy(side, k + 1, core).start()

            if k + 1 < N - 1:
                @pl.when(jnp.logical_and(behind(side) > k, behind(side) < N - 1))
                def _():
                    hop_copy(side, k + 1).start()

    def l_done():
        core_copy(0, 0, 1 - core).wait_recv()
        core_copy(0, 0, core).wait_send()
        for side in range(2):
            for k in range(N - 1):
                @pl.when(behind(side) > k)
                def _():
                    core_copy(side, k + 1, 1 - core).wait_recv()
                    core_copy(side, k + 1, core).wait_send()

                @pl.when(jnp.logical_and(behind(side) >= k, behind(side) < N - 1))
                def _():
                    hop_copy(side, k).wait_send()

    steps = [[(t - st, st) for st in reversed(range(stages)) if 0 <= t - st < z.CZ] for t in range(z.CZ + stages - 1)]
    a_step = z.CA - 1 + stages - 1
    before_a = [[e for e in step if e[0] < z.CA or t < a_step - 1] for t, step in enumerate(steps[:a_step + 1])]
    after_a = [[e for e in step if e not in (before_a[t] if t <= a_step else [])] for t, step in enumerate(steps)]

    def gather_events(events):
        for c, st in events:
            gather_event(c, st)

    z_start(0)
    raw_gate, raw_up, raw_down = w_gu[:, 0, :], w_gu[:, 1, :], flipped(w_down[...])
    pack(z.LA, z.lanes, [out_t[:, z.O0:]] + [raw_gate, raw_up, raw_down])
    l_own().start()
    l_own().wait()
    l_start(0)

    xin = s["xin"]
    own = pltpu.make_async_copy(tokens.at[pl.ds(pl.multiple_of(place * R, 16), R)], xin.at[pl.ds(HALF, R)], s["l_tok"].at[0])
    own.start()
    own_cot = pltpu.make_async_copy(grads_in.at[pl.ds(pl.multiple_of(place * R, 16), R)], cot, s["l_tok"].at[3])
    own_cot.start()

    def low_copy():
        return pltpu.make_async_copy(tokens.at[pl.ds(pl.multiple_of(place * R - HALF, 16), HALF)], xin.at[pl.ds(0, HALF)], s["l_tok"].at[1])

    def high_copy():
        return pltpu.make_async_copy(tokens.at[pl.ds(pl.multiple_of(place * R + R, 16), HALF)], xin.at[pl.ds(HALF + R, HALF)], s["l_tok"].at[2])

    halo = s["halo"]

    def halo_to_next():
        return copy_to(tokens.at[pl.ds(T - HALF, HALF)], halo.at[0], s["hs"].at[0], s["hr"].at[0], (w + 1, n))

    def halo_to_prev():
        return copy_to(tokens.at[pl.ds(0, HALF)], halo.at[1], s["hs"].at[1], s["hr"].at[1], (w - 1, n))

    @pl.when(place > 0)
    def _():
        low_copy().start()

    @pl.when(place < N - 1)
    def _():
        high_copy().start()

    @pl.when(high_block)
    def _():
        halo_to_next().start()

    @pl.when(low_block)
    def _():
        halo_to_prev().start()

    @pl.when(w == 0)
    def _():
        halo[0] = jnp.zeros((HALF, D), BF16)

    @pl.when(w == W - 1)
    def _():
        halo[1] = jnp.zeros((HALF, D), BF16)

    ends, total = [], jnp.int32(0)
    for d in range(z.docs):
        total = total + lengths[d]
        ends.append(total)
    cos_t, sin_t, bias_t = s["cos"], s["sin"], s["bias"]
    lane = lax.broadcasted_iota(jnp.int32, (BLOCK, 128), 1)
    low_half = lax.rem(lane, HEAD_DIM) < HEAD_DIM // 2

    freq_lane = lax.rem(lax.broadcasted_iota(jnp.int32, (1, 128), 1), HEAD_DIM // 2)
    freq = jnp.zeros((1, 128), F32)
    for d in range(HEAD_DIM // 2):
        freq = jnp.where(freq_lane == d, F32(THETA ** (-2.0 * d / HEAD_DIM)), freq)

    def tables(spot):
        base = w * T + spot * R
        lax.fori_loop(0, E // BLOCK, functools.partial(table_rows, base), 0)
        lax.fori_loop(0, NB, functools.partial(bias_rows, base), 0)

    def table_rows(base, i, carry):
        r = pl.multiple_of(i * BLOCK, BLOCK)
        t = base - HALF + r + lax.broadcasted_iota(jnp.int32, (BLOCK, 128), 0)
        start = jnp.zeros((BLOCK, 128), jnp.int32)
        for d in range(z.docs):
            start = start + jnp.where(t >= ends[d], lengths[d], 0)
        angle = (t - start).astype(F32) * freq
        cos_t[pl.ds(r, BLOCK), :] = jnp.cos(angle)
        sine = jnp.sin(angle)
        sin_t[pl.ds(r, BLOCK), :] = jnp.where(low_half, -sine, sine)
        return carry

    def bias_rows(base, b, carry):
        tk = base - HALF + b * BLOCK + lax.broadcasted_iota(jnp.int32, (SPAN, BLOCK), 0)
        tq = base + b * BLOCK + lax.broadcasted_iota(jnp.int32, (SPAN, BLOCK), 1)
        dk = jnp.where(tk < 0, -1, 0)
        dq = jnp.zeros((SPAN, BLOCK), jnp.int32)
        for d in range(z.docs):
            dk = dk + jnp.where(tk >= ends[d], 1, 0)
            dq = dq + jnp.where(tq >= ends[d], 1, 0)
        near = jnp.abs(tk - tq) <= HALF
        bias_t[b] = jnp.where(jnp.logical_and(dk == dq, near), 0.0, NEG_LARGE).astype(F32)
        return carry

    for t in range(z.bits):
        l_wait(t)
        if t + 1 < z.bits:
            l_start(t + 1)
    gather_events(before_a[0])
    tables(place)
    gather_events(before_a[1])
    l_own_group()

    own.wait()

    @pl.when(place > 0)
    def _():
        low_copy().wait()

    @pl.when(place < N - 1)
    def _():
        high_copy().wait()

    @pl.when(low_block)
    def _():
        halo_to_next().wait_recv()
        halo_to_prev().wait_send()

    @pl.when(high_block)
    def _():
        halo_to_prev().wait_recv()
        halo_to_next().wait_send()

    @pl.when(first)
    def _():
        xin[0:HALF, :] = halo[0]

    @pl.when(last)
    def _():
        xin[HALF + R:, :] = halo[1]

    gather_events(before_a[2])
    own_cot.wait()

    def mask_rows(b, carry):
        rows = pl.ds(pl.multiple_of(b * BLOCK, BLOCK), BLOCK)
        keep = jnp.where(masked[pl.ds(place * NB + b, 1), :] == 1, 1.0, 0.0).astype(F32)
        keep = jnp.broadcast_to(keep, (BLOCK, BLOCK)).T.astype(BF16)
        cot[rows, :] = cot[rows, :] * jnp.concatenate([keep] * (D // BLOCK), axis=1)
        return carry

    lax.fori_loop(0, NB, mask_rows, 0)

    def transposed(name, src, row0):
        if not z.keep:
            return
        dst = s[name]

        def body(i, carry):
            at = pl.multiple_of(i * 128, 128)
            dst[pl.ds(at, 128), :] = src[row0:row0 + R, pl.ds(at, 128)].astype(F32).T.astype(BF16)
            return carry

        lax.fori_loop(0, D // 128, body, 0)

    transposed("ct", cot, 0)

    for t in range(3, a_step):
        gather_events(before_a[t])
    l_hop(0)
    gather_events(before_a[a_step])

    wqkv, wot, wg, wu, wgo = s["wqkv"], s["wot"], s["wg"], s["wu"], s["wgo"]
    gcol, grow, gsum = s["gcol"], s["grow"], s["gsum"]

    UG = z.UG
    UR = UG * 2 * SH

    def section(nn, i, lo, up):
        found = []
        for c, (a, b) in enumerate(z.cuts):
            x, y = max(lo, a), min(up, b)
            if x >= y:
                continue
            x0, y0 = (x - a) // 128 * 128, round_up(y - a, 128)
            both = [wb[c][nn, i * UG + a2, k, :, x0:y0] for a2 in range(UG) for k in range(2)]
            if SH % 16 == 0:
                v = jnp.concatenate([q[:SH] for q in both], axis=0)
            else:
                v = jnp.concatenate([q.astype(F32)[:SH] for q in both], axis=0).astype(BF16)
            found.append(v[:, x - a - x0:y - a - x0])
        return found[0] if len(found) == 1 else jnp.concatenate(found, axis=1)

    def place_columns(ref, r, at, sections):
        width = sum(v.shape[1] for v in sections)
        ref[pl.ds(r, UR), at:at + width] = jnp.concatenate(sections, axis=1)

    def unpack_a(i, carry):
        r = pl.multiple_of(i * UR, 16)
        parts = [section(nn, i, 0, z.LA) for nn in range(N)]
        for k in range(3):
            at = GAIN_LANES + k * QN
            place_columns(wqkv, r, k * D, [v[:, at:at + QN] for v in parts])
        gcol[pl.ds(r, UR), :] = parts[0][:, 0:128].astype(F32)
        return carry

    lax.fori_loop(0, W // 2 // UG, unpack_a, 0)
    grow[...] = gcol[...].T[0:8, :]
    gsum[...] = jnp.zeros((8, D), F32)

    def normed(x):
        centred = x - jnp.mean(x, axis=-1, keepdims=True)
        rstd = lax.rsqrt(jnp.mean(centred * centred, axis=-1, keepdims=True) + EPSILON)
        return centred * rstd, rstd

    n1, qkv = s["n1"], s["qkv"]

    def norm_rows(i, carry):
        r = pl.multiple_of(i * BLOCK, BLOCK)
        hat, _ = normed(xin[pl.ds(r, BLOCK), :].astype(F32))
        n1[pl.ds(r, BLOCK), :] = (hat * grow[0:1, :]).astype(BF16)
        return carry

    def partner_lanes(x):
        lanes = lax.broadcasted_iota(jnp.int32, x.shape, 1)
        return jnp.where(lax.rem(lanes, HEAD_DIM) < HEAD_DIM // 2, pltpu.roll(x, 128 - HEAD_DIM // 2, 1), pltpu.roll(x, HEAD_DIM // 2, 1))

    def project_turned(ct, carry):
        at = pl.multiple_of(ct * 256, 128)
        y = dot(n1[...], wqkv[:, pl.ds(at, 256)], 1, 0)
        scale = jnp.where(ct < D // 256, F32(1.0 / math.sqrt(HEAD_DIM)), F32(1.0))
        for k in range(2):
            part_y = y[:, k * 128:(k + 1) * 128]
            part_y = (part_y * cos_t[...] + partner_lanes(part_y) * sin_t[...]) * scale
            qkv[:, pl.ds(pl.multiple_of(at + k * 128, 128), 128)] = part_y.astype(BF16)
        return carry

    def project(ct, carry):
        at = pl.multiple_of(2 * D + ct * 256, 128)
        qkv[:, pl.ds(at, 256)] = dot(n1[...], wqkv[:, pl.ds(at, 256)], 1, 0).astype(BF16)
        return carry

    def make_qkv():
        lax.fori_loop(0, E // BLOCK, norm_rows, 0)
        lax.fori_loop(0, 2 * D // 256, project_turned, 0)
        lax.fori_loop(0, D // 256, project, 0)

    for t in range(a_step):
        gather_events(after_a[t])
    if N > 2:
        l_hop(1)
    make_qkv()
    gather_events(after_a[a_step])

    att, stat = s["att"], s.get("stat")
    lane_row = lax.broadcasted_iota(jnp.int32, (BLOCK, 128), 1)
    keep_one = jnp.where(lane_row < HEAD_DIM, 1.0, 0.0).astype(BF16)
    keep_two = jnp.where(lane_row < HEAD_DIM, 0.0, 1.0).astype(BF16)

    def stacked(x):
        return jnp.concatenate([x * keep_one, x * keep_two], axis=0)

    def unstacked(x):
        return jnp.concatenate([x[:HEAD_DIM, :BLOCK], x[HEAD_DIM:, BLOCK:]], axis=0).T

    def unit_refs(j, b):
        lanes = [pl.ds(pl.multiple_of(k * D + j * 128, 128), 128) for k in range(3)]
        return lanes, pl.ds(pl.multiple_of(b * BLOCK, BLOCK), SPAN), pl.ds(pl.multiple_of(b * BLOCK + HALF, 16), BLOCK)

    def unit_scores(j, b):
        (lq, lk, lv), keys, queries = unit_refs(j, b)
        qs = stacked(qkv[queries, lq])
        kp, vp = qkv[keys, lk], qkv[keys, lv]
        pen = bias_t[b]
        return qs, kp, vp, dot(kp, qs, 1, 1) + jnp.concatenate([pen, pen], axis=1)

    G = z.G

    def attend(v, carry):
        j, g = lax.div(v, NB // G), lax.rem(v, NB // G)
        for i in range(G):
            b = g * G + i
            u = j * NB + b
            _, _, vp, scores = unit_scores(j, b)
            top = jnp.max(scores, axis=0, keepdims=True)
            weights = jnp.exp(scores - top)
            inv = 1.0 / jnp.sum(weights, axis=0, keepdims=True)
            probs = weights * inv
            if z.keep:
                s["kept"][u] = probs
            else:
                stat[u, 0:1, :] = top
                stat[u, 1:2, :] = inv
            got = unstacked(dot(vp, probs.astype(BF16), 0, 0))
            att[pl.ds(pl.multiple_of(b * BLOCK, BLOCK), BLOCK), pl.ds(pl.multiple_of(j * 128, 128), 128)] = got.astype(BF16)
        return carry

    def attend_part(lo, up):
        lax.fori_loop(lo * (NB // G), up * (NB // G), attend, 0)

    half_pairs = z.pairs // 2
    third = z.pairs // 3
    attend_part(0, third)
    for k in range(2, N - 1):
        l_hop(k)
    attend_part(third, 2 * third)
    gather_events(after_a[a_step + 1])
    attend_part(2 * third, z.pairs)
    for t in range(a_step + 2, len(steps)):
        gather_events(after_a[t])

    slices_at = GAIN_LANES + 4 * QN

    def unpack_first(i, carry):
        r = pl.multiple_of(i * UR, 16)
        lo = GAIN_LANES + 3 * QN
        parts = [section(nn, i, lo, slices_at + FN) for nn in range(N)]
        place_columns(wot, r, 0, [v[:, :QN] for v in parts])
        place_columns(wg, r, 0, [v[:, QN:] for v in parts])
        return carry

    def unpack_second(i, carry):
        r = pl.multiple_of(i * UR, 16)
        parts = [section(nn, i, slices_at + FN, slices_at + 3 * FN) for nn in range(N)]
        place_columns(wu, r, 0, [v[:, :FN] for v in parts])
        place_columns(wgo, r, 0, [v[:, FN:] for v in parts])
        return carry

    lax.fori_loop(0, W // 2 // UG, unpack_first, 0)
    l_done()
    lax.fori_loop(0, W // 2 // UG, unpack_second, 0)

    ost, n2, res, resg = s["ost"], s["n2"], s["resr"], s["resg"]
    hid, dgate, dup, datt = s["hid"], s["dgate"], s["dup"], s["datt"]
    MB, FC = z.MB, z.FC

    def norm_back(hat, rstd, e, gain):
        eg = e * gain
        return rstd * (eg - jnp.mean(eg, axis=-1, keepdims=True) - hat * jnp.mean(eg * hat, axis=-1, keepdims=True))

    def line_rows(dest, m, rb):
        theirs = m + core * (N - 1 - 2 * m)
        return dest.at[pl.ds(pl.multiple_of(theirs * R + rb * MB, 16), MB)]

    def line_copy(dest, rb, key, side, k, stage=None):
        step = 1 - 2 * side
        ref = line_rows(dest, n - step * k, rb)
        src = ref if stage is None else stage.at[pl.ds(pl.multiple_of(rb * MB, 16), MB)]
        return copy_to(src, ref, s[key + "s"].at[rb, side, k], s[key + "r"].at[rb, side, k], (w, n + step))

    def own_copy(stage, dest, rb, key):
        return pltpu.make_async_copy(stage.at[pl.ds(pl.multiple_of(rb * MB, 16), MB)], line_rows(dest, n, rb), s[key + "l"].at[rb])

    def token_send(stage, dest, rb, key):
        own_copy(stage, dest, rb, key).start()
        for side in range(2):
            @pl.when(behind(side) < N - 1)
            def _():
                line_copy(dest, rb, key, side, 0, stage).start()

    hops = {"o": N - 2 if N > 2 else N - 1, "t": N - 1}

    def token_forward(dest, key, k):
        if k > hops[key]:
            return

        def body(rb, carry):
            for side in range(2):
                step = 1 - 2 * side

                @pl.when(behind(side) >= k)
                def _():
                    arrived(line_rows(dest, n - step * k, rb), s[key + "s"].at[rb, side, k - 1], s[key + "r"].at[rb, side, k - 1], (w, n - step))

                if k < hops[key]:
                    @pl.when(jnp.logical_and(behind(side) >= k, behind(side) < N - 1))
                    def _():
                        line_copy(dest, rb, key, side, k).start()
            return carry

        lax.fori_loop(0, z.blocks, body, 0)

    def token_sent(stage, dest, key, lo, up):
        def body(rb, carry):
            if lo == 0:
                own_copy(stage, dest, rb, key).wait()
            for side in range(2):
                for k in range(lo, up):
                    @pl.when(jnp.logical_and(behind(side) >= k, behind(side) < N - 1))
                    def _():
                        line_copy(dest, rb, key, side, k).wait_send()
            return carry

        lax.fori_loop(0, z.blocks, body, 0)

    def feed(rb, carry):
        r = pl.multiple_of(rb * MB, 16)
        rows = pl.ds(r, MB)
        x = xin[pl.ds(pl.multiple_of(rb * MB + HALF, 16), MB), :].astype(F32)
        residual = x + dot(att[rows, :], wot[...], 1, 1)
        hat, rstd = normed(residual)
        gain = grow[1:2, :]
        n2v = (hat * gain).astype(BF16)
        n2[rows, :] = n2v
        cotv = cot[rows, :]
        total_out, e = residual, None
        for f in range(0, F, FC):
            gate = dot(n2v, wg[:, f:f + FC], 1, 0)
            upv = dot(n2v, wu[:, f:f + FC], 1, 0)
            dh = dot(cotv, wgo[:, f:f + FC], 1, 0)
            sq = gate * gate
            th = jnp.tanh(GELU_A * (gate * (1.0 + GELU_B * sq)))
            half = 0.5 * (1.0 + th)
            act = gate * half
            slope = half + (0.5 * GELU_A) * gate * (1.0 - th * th) * (1.0 + (3.0 * GELU_B) * sq)
            hv = (act * upv).astype(BF16)
            dgv = (dh * upv * slope).astype(BF16)
            duv = (dh * act).astype(BF16)
            hid[rows, f:f + FC] = hv
            dgate[rows, f:f + FC] = dgv
            dup[rows, f:f + FC] = duv
            total_out = total_out + dot(hv, wgo[:, f:f + FC], 1, 1)
            more = dot(dgv, wg[:, f:f + FC], 1, 1) + dot(duv, wu[:, f:f + FC], 1, 1)
            e = more if e is None else e + more
        ost[rows, :] = total_out.astype(BF16)
        token_send(ost, out, rb, "o")
        gsum[1:2, :] = gsum[1:2, :] + jnp.sum(e * hat, axis=0, keepdims=True)
        grad = cotv.astype(F32) + norm_back(hat, rstd, e, gain)
        resg[rows, :] = grad
        low = grad.astype(BF16)
        res[rows, :] = low
        datt[rows, :] = dot(low, wot[...], 1, 0).astype(BF16)
        return carry

    lax.fori_loop(0, z.blocks, feed, 0)

    for c in pending:
        c.wait_send()
    pending.clear()

    def store_rows(c, nn, i, k, value):
        if RS > SH:
            value = jnp.concatenate([value, jnp.zeros((RS - SH, value.shape[1]), F32)], axis=0)
        wb[c][nn, i, k] = value.astype(BF16)

    HT, TM = z.HT, z.TM
    owx = s["owx"]

    def store_part(chunks, nn, t, value):
        lo = z.cuts[chunks[0]][0]
        for c in chunks:
            a, b = z.cuts[c]
            for i in range(HT):
                for k in range(2):
                    at = (2 * i + k) * SH
                    store_rows(c, nn, t * HT + i, k, value[at:at + SH, a - lo:b - lo])

    def turned_dot(name, src, row0, t, rhs):
        if z.keep:
            return dot(s[name][pl.ds(pl.multiple_of(t * TM, 16), TM), :], rhs, 1, 0)
        return dot(src[row0:row0 + R, t * TM:(t + 1) * TM], rhs, 0, 0)

    def tiles(body):
        if z.keep:
            lax.fori_loop(0, D // TM, body, 0)
        else:
            for t in range(D // TM):
                body(t, 0)

    def grads_b(t, carry):
        r = pl.multiple_of(t * TM, 16)
        gg = turned_dot("n2t", n2, 0, t, dgate[...])
        gu = turned_dot("n2t", n2, 0, t, dup[...])
        go = turned_dot("ct", cot, 0, t, hid[...])
        gw = turned_dot("rt", res, 0, t, att[...])
        if z.O0:
            firsts = [gw[:, nn * QN:nn * QN + z.O0] for nn in range(N)]
            spare = owx.shape[1] - N * z.O0
            if spare:
                firsts.append(jnp.zeros((TM, spare), F32))
            owx[pl.ds(r, TM), :] = jnp.concatenate(firsts, axis=1)
        for nn in range(N):
            pieces = [gw[:, nn * QN + z.O0:(nn + 1) * QN]] + [v[:, nn * FN:(nn + 1) * FN] for v in (gg, gu, go)]
            if z.lanes > z.real:
                pieces.append(jnp.zeros((TM, z.lanes - z.real), F32))
            store_part(list(range(z.CA, C)), nn, t, jnp.concatenate(pieces, axis=1))
        return carry

    scatter_order = [list(range(z.bits)), list(range(z.bits))[::-1]]

    def slot_base(t):
        return sum(1 << (z.bits - 1 - u) for u in range(t))

    def r0_start(c):
        send(wb[c].at[:, :, 1 - core], r0[c], s["g0s"].at[c], s["g0r"].at[c], sib_dev)

    def r0_finish(c):
        arrived(r0[c], s["g0s"].at[c], s["g0r"].at[c], sib_dev)

        def body(i, carry):
            for nn in range(N):
                wb[c][nn, i, core] = (wb[c][nn, i, core].astype(F32) + r0[c][nn, i].astype(F32)).astype(BF16)
            return carry

        lax.fori_loop(0, W // 2, body, 0)

    def r1_start(c, t):
        for h in range(2):
            b = scatter_order[h][t]
            for i, combo in enumerate(combos(scatter_order[h][t + 1:])):
                slot = slot_base(t) + i
                send(wb[c].at[half_refs[h], flip(hi, combo + [b]), core], r1[c].at[h, slot], s["g1s"].at[c, h, slot], s["g1r"].at[c, h, slot], bit_dev(b))

    def r1_finish(c, t):
        for h in range(2):
            b = scatter_order[h][t]
            for i, combo in enumerate(combos(scatter_order[h][t + 1:])):
                slot = slot_base(t) + i
                arrived(r1[c].at[h, slot], s["g1s"].at[c, h, slot], s["g1r"].at[c, h, slot], bit_dev(b))
                hv = flip(hi, combo)
                for nn in range(N2):
                    at = h * N2 + nn
                    wb[c][at, hv, core] = (wb[c][at, hv, core].astype(F32) + r1[c][h, slot, nn].astype(F32)).astype(BF16)

    def rz_copy(c, side, d):
        step = 1 - 2 * side
        return copy_to(wb[c].at[n + step * (1 + d), hi, core], rz[c].at[side, d], s["g2s"].at[c, side, d], s["g2r"].at[c, side, d], (w, n + step))

    def rz_round(c, r):
        for side in range(2):
            step = 1 - 2 * side

            @pl.when(behind(side) == r)
            def _():
                for d in reversed(range(N - r)):
                    if r > 0:
                        arrived(rz[c].at[side, d], s["g2s"].at[c, side, d], s["g2r"].at[c, side, d], (w, n - step))
                        if d > 0:
                            m = n + step * d
                            wb[c][m, hi, core] = (wb[c][m, hi, core].astype(F32) + rz[c][side, d].astype(F32)).astype(BF16)
                    if d > 0:
                        rz_copy(c, side, d - 1).start()

    def rz_sent(c):
        for side in range(2):
            for r in range(N - 1):
                @pl.when(behind(side) == r)
                def _():
                    for d in range(N - 1 - r):
                        rz_copy(c, side, d).wait_send()

    def rz_finish(c):
        lo, up = z.cuts[c]
        gp[:, lo:up] = wb[c][n, hi, core].astype(F32)
        for side in range(2):
            @pl.when(behind(side) > 0)
            def _():
                gp[:, lo:up] = gp[:, lo:up] + rz[c][side, 0].astype(F32)

    last_stage = z.bits + 1 + N

    def scatter_advance(chunks, st):
        for c in chunks:
            if st == 0:
                r0_start(c)
            elif st <= z.bits + 1:
                if st == 1:
                    r0_finish(c)
                else:
                    r1_finish(c, st - 2)
                if st <= z.bits:
                    r1_start(c, st - 1)
                else:
                    rz_round(c, 0)
            else:
                rz_round(c, st - z.bits - 1)
                if st == last_stage - 1:
                    rz_finish(c)

    part_a, part_b = list(range(z.CA)), list(range(z.CA, C))
    transposed("n2t", n2, 0)
    transposed("rt", res, 0)
    tiles(grads_b)

    scatter_advance(part_b, 0)

    dkv, edge, rim, rimr = s["dkv"], s["edge"], s["rim"], s["rimr"]
    dk_ref, dv_ref = dkv.at[0], dkv.at[1]

    def attend_back(j, carry):
        dkv[:, 0:BLOCK, :] = jnp.zeros((2, BLOCK, 128), F32)

        def group(g, inner):
            tails = None
            for i in range(G):
                b = g * G + i
                u = j * NB + b
                (lq, lk, lv), keys, queries = unit_refs(j, b)
                if z.keep:
                    qs, kp, vp = stacked(qkv[queries, lq]), qkv[keys, lk], qkv[keys, lv]
                    probs = s["kept"][u]
                else:
                    qs, kp, vp, scores = unit_scores(j, b)
                    probs = jnp.exp(scores - stat[u, 0:1, :]) * stat[u, 1:2, :]
                gs = stacked(datt[pl.ds(pl.multiple_of(b * BLOCK, BLOCK), BLOCK), pl.ds(pl.multiple_of(j * 128, 128), 128)])
                prob_grad = dot(vp, gs, 1, 1)
                row_dot = jnp.sum(probs * prob_grad, axis=0, keepdims=True)
                score_grad = (probs * (prob_grad - row_dot)).astype(BF16)
                parts = (dot(score_grad, qs, 1, 0), dot(probs.astype(BF16), gs, 1, 0))
                dq = unstacked(dot(kp, score_grad, 0, 0)) * F32(1.0 / math.sqrt(HEAD_DIM))
                dq = dq * cos_t[queries, :] - partner_lanes(dq) * sin_t[queries, :]
                qkv[queries, lq] = dq.astype(BF16)
                here = pl.ds(pl.multiple_of(b * BLOCK, BLOCK), BLOCK)
                for k in range(2):
                    before = dkv[k, here, :] if tails is None else tails[k]
                    dkv[k, here, :] = before + parts[k][:BLOCK]
                tails = [x[BLOCK:] for x in parts]
            after = pl.ds(pl.multiple_of(g * G * BLOCK + G * BLOCK, BLOCK), BLOCK)
            for k in range(2):
                dkv[k, after, :] = tails[k]
            return inner

        lax.fori_loop(0, NB // G, group, 0)
        (_, lk, lv), _, _ = unit_refs(j, 0)
        lj = pl.ds(pl.multiple_of(j * 128, 128), 128)
        for k, ref in enumerate((dk_ref, dv_ref)):
            wide_lanes = pl.ds(pl.multiple_of(k * D + j * 128, 128), 128)
            rim[0, :, wide_lanes] = ref[0:HALF, :].astype(BF16)
            rim[1, :, wide_lanes] = ref[E - HALF:, :].astype(BF16)
            edge[0, :, wide_lanes] = ref[HALF:WINDOW, :]
            edge[1, :, wide_lanes] = ref[R:R + HALF, :]
        mid = slice(HALF, HALF + R)
        dk = dk_ref[mid, :]
        qkv[mid, lk] = (dk * cos_t[mid, :] - partner_lanes(dk) * sin_t[mid, :]).astype(BF16)
        qkv[mid, lv] = dv_ref[mid, :].astype(BF16)
        return carry

    lax.fori_loop(0, third, attend_back, 0)
    token_forward(out, "o", 1)
    lax.fori_loop(third, 2 * third, attend_back, 0)
    scatter_advance(part_b, 1)
    lax.fori_loop(2 * third, z.pairs, attend_back, 0)

    def rim_to_prev():
        return copy_to(rim.at[0], rimr.at[1], s["rs"].at[0], s["rr"].at[1], prev_dev)

    def rim_to_next():
        return copy_to(rim.at[1], rimr.at[0], s["rs"].at[1], s["rr"].at[0], next_dev)

    @pl.when(has_prev)
    def _():
        rim_to_prev().start()

    @pl.when(has_next)
    def _():
        rim_to_next().start()

    @pl.when(jnp.logical_not(has_prev))
    def _():
        rimr[0] = jnp.zeros((HALF, 2 * D), BF16)

    @pl.when(jnp.logical_not(has_next))
    def _():
        rimr[1] = jnp.zeros((HALF, 2 * D), BF16)

    transposed("rt", n1, HALF)

    @pl.when(has_prev)
    def _():
        rim_to_next().wait_recv()

    @pl.when(has_next)
    def _():
        rim_to_prev().wait_recv()

    @pl.when(has_prev)
    def _():
        rim_to_prev().wait_send()

    @pl.when(has_next)
    def _():
        rim_to_next().wait_send()

    for side, row in ((0, HALF), (1, R)):
        rows = slice(row, row + HALF)
        for j in range(z.pairs):
            lk = slice(j * 128, (j + 1) * 128)
            lv = slice(D + j * 128, D + (j + 1) * 128)
            dk = edge[side, :, lk] + rimr[side, :, lk].astype(F32)
            dv = edge[side, :, lv] + rimr[side, :, lv].astype(F32)
            dk = dk * cos_t[rows, :] - partner_lanes(dk) * sin_t[rows, :]
            qkv[rows, D + j * 128:D + (j + 1) * 128] = dk.astype(BF16)
            qkv[rows, 2 * D + j * 128:2 * D + (j + 1) * 128] = dv.astype(BF16)

    tst = n2

    def input_grad(rb, carry):
        rows = pl.ds(pl.multiple_of(rb * MB, 16), MB)
        ext = pl.ds(pl.multiple_of(rb * MB + HALF, 16), MB)
        e = dot(qkv[ext, :], wqkv[...], 1, 1)
        hat, rstd = normed(xin[ext, :].astype(F32))
        gsum[0:1, :] = gsum[0:1, :] + jnp.sum(e * hat, axis=0, keepdims=True)
        tst[rows, :] = (resg[rows, :] + norm_back(hat, rstd, e, grow[0:1, :])).astype(BF16)
        token_send(tst, tg, rb, "t")
        return carry

    lax.fori_loop(0, z.blocks, input_grad, 0)

    gcol[...] = jnp.concatenate([gsum[...], jnp.zeros((120, D), F32)], axis=0).T

    def grads_a(t, carry):
        r = pl.multiple_of(t * TM, 16)
        g = [turned_dot("rt", n1, HALF, t, qkv[HALF:HALF + R, k * D:(k + 1) * D]) for k in range(3)]
        gains = gcol[pl.ds(r, TM), 0:GAIN_LANES]
        for nn in range(N):
            pieces = [gains] + [v[:, nn * QN:(nn + 1) * QN] for v in g]
            if z.O0:
                pieces.append(owx[pl.ds(r, TM), nn * z.O0:(nn + 1) * z.O0])
            store_part(part_a, nn, t, jnp.concatenate(pieces, axis=1))
        return carry

    tiles(grads_a)
    scatter_advance(part_a, 0)
    scatter_advance(part_b, 2)
    token_sent(ost, out, "o", 0, 1)

    far = N - 1 - place

    def far_rows():
        return pltpu.make_async_copy(tokens.at[pl.ds(pl.multiple_of(far * R, 16), R)], xin.at[pl.ds(HALF, R)], s["l_tok"].at[0])

    def far_low():
        return pltpu.make_async_copy(tokens.at[pl.ds(T - R - HALF, HALF)], xin.at[pl.ds(0, HALF)], s["l_tok"].at[1])

    def far_high():
        return pltpu.make_async_copy(tokens.at[pl.ds(R, HALF)], xin.at[pl.ds(HALF + R, HALF)], s["l_tok"].at[2])

    def far_feed(rb, carry):
        r = pl.multiple_of(rb * MB, 16)
        rows = pl.ds(r, MB)
        x = xin[pl.ds(pl.multiple_of(rb * MB + HALF, 16), MB), :].astype(F32)
        residual = x + dot(att[rows, :], wot[...], 1, 1)
        n2v = (normed(residual)[0] * grow[1:2, :]).astype(BF16)
        total_out = residual
        for f in range(0, F, FC):
            gate = dot(n2v, wg[:, f:f + FC], 1, 0)
            upv = dot(n2v, wu[:, f:f + FC], 1, 0)
            act = gate * (0.5 * (1.0 + jnp.tanh(GELU_A * (gate * (1.0 + GELU_B * (gate * gate))))))
            total_out = total_out + dot((act * upv).astype(BF16), wgo[:, f:f + FC], 1, 1)
        ost[rows, :] = total_out.astype(BF16)
        return carry

    def far_out():
        return pltpu.make_async_copy(ost, out.at[pl.ds(pl.multiple_of(far * R, 16), R)], s["ol"].at[0])

    def far_project():
        far_rows().start()

        @pl.when(first)
        def _():
            far_low().start()
            xin[HALF + R:, :] = halo[1]

        @pl.when(last)
        def _():
            far_high().start()
            xin[0:HALF, :] = halo[0]

        tables(far)
        far_rows().wait()

        @pl.when(first)
        def _():
            far_low().wait()

        @pl.when(last)
        def _():
            far_high().wait()

        make_qkv()

    def far_finish():
        lax.fori_loop(0, z.blocks, far_feed, 0)
        far_out().start()
        far_out().wait()

    def at_ends(work):
        if N > 2:
            pl.when(at_end)(work)

    at_ends(far_project)
    scatter_advance(part_a, 1)
    token_forward(tg, "t", 1)
    for st in range(3, z.bits + 2):
        scatter_advance(part_b, st)
    at_ends(functools.partial(attend_part, 0, half_pairs))
    at_ends(functools.partial(attend_part, half_pairs, z.pairs))
    scatter_advance(part_a, 2)
    at_ends(far_finish)
    for st in range(3, z.bits + 2):
        scatter_advance(part_a, st)
    for k in range(2, N):
        token_forward(out, "o", k)
    if N > 2:
        token_forward(tg, "t", 2)
    for st in range(z.bits + 2, last_stage):
        scatter_advance(part_b, st)
        scatter_advance(part_a, st)
    for k in range(3, N):
        token_forward(tg, "t", k)

    for c in pending:
        c.wait_send()
    for c in range(C):
        rz_sent(c)
    token_sent(ost, out, "o", 1, hops["o"])
    token_sent(tst, tg, "t", 0, hops["t"])


def run_layer(z, *args):
    shapes, names = [], []

    def vmem(name, shape, dtype):
        names.append(name)
        shapes.append(pltpu.VMEM(shape, dtype))

    def sems(name, *shape):
        names.append(name)
        shapes.append(pltpu.SemaphoreType.DMA(shape))

    W, N, D, F, R, E, C = z.W, z.N, z.D, z.F, z.R, z.E, z.C
    for c, (lo, up) in enumerate(z.cuts):
        vmem(f"wb{c}", (N, W // 2, 2, z.RS, up - lo), BF16)
        vmem(f"r0{c}", (N, W // 2, z.RS, up - lo), BF16)
        vmem(f"r1{c}", (2, W // 2 - 1, N // 2, z.RS, up - lo), BF16)
        vmem(f"rz{c}", (2, N - 1, z.RS, up - lo), BF16)
    vmem("xin", (E, D), BF16)
    vmem("halo", (2, HALF, D), BF16)
    vmem("n1", (E, D), BF16)
    vmem("qkv", (E, 3 * D), BF16)
    vmem("wqkv", (D, 3 * D), BF16)
    vmem("wot", (D, D), BF16)
    for name in ("wg", "wu", "wgo"):
        vmem(name, (D, F), BF16)
    vmem("gcol", (D, 128), F32)
    vmem("grow", (8, D), F32)
    vmem("gsum", (8, D), F32)
    vmem("owx", (D, round_up(max(N * z.O0, 1), 128)), F32)
    vmem("cos", (E, 128), F32)
    vmem("sin", (E, 128), F32)
    vmem("bias", (z.NB, SPAN, BLOCK), F32)
    if z.keep:
        vmem("kept", (z.pairs * z.NB, SPAN, 2 * BLOCK), F32)
    else:
        vmem("stat", (z.pairs * z.NB, 8, 2 * BLOCK), F32)
    vmem("pk", (z.RS, z.lanes), BF16)
    for name in ("att", "ost", "n2", "resr", "datt", "cot"):
        vmem(name, (R, D), BF16)
    if z.keep:
        for name in ("n2t", "ct", "rt"):
            vmem(name, (D, R), BF16)
    vmem("resg", (R, D), F32)
    for name in ("hid", "dgate", "dup"):
        vmem(name, (R, F), BF16)
    vmem("dkv", (2, E, 128), F32)
    vmem("edge", (2, HALF, 2 * D), F32)
    vmem("rim", (2, HALF, 2 * D), BF16)
    vmem("rimr", (2, HALF, 2 * D), BF16)
    sems("l_own", C)
    sems("l_tok", 4)
    for name in ("zs", "zr"):
        sems(name, C, N - 1)
    for name in ("g2s", "g2r"):
        sems(name, C, 2, N - 1)
    for name in ("ss", "sr", "g1s", "g1r"):
        sems(name, C, 2, W // 2 - 1)
    for name in ("ds", "dr"):
        sems(name, C, 2, W // 2)
    for name in ("g0s", "g0r"):
        sems(name, C)
    for name in ("hs", "hr", "rs", "rr"):
        sems(name, 2)
    for name in ("lzs", "lzr"):
        sems(name, 2, N - 1)
    for name in ("lds", "ldr"):
        sems(name, 2, N)
    for name in ("ol", "tl"):
        sems(name, z.blocks)
    for name in ("os", "or", "ts", "tr"):
        sems(name, z.blocks, 2, N - 1)
    hbm = pl.BlockSpec(memory_space=pl.ANY)
    vm = pl.BlockSpec(memory_space=pltpu.VMEM)
    return pl.pallas_call(
        functools.partial(layer_kernel, z, names),
        out_shape=(
            jax.ShapeDtypeStruct((z.T, D), BF16),
            jax.ShapeDtypeStruct((z.T, D), BF16),
            jax.ShapeDtypeStruct((z.RS, z.lanes), F32),
        ),
        in_specs=[pl.BlockSpec(memory_space=pltpu.SMEM), hbm, hbm] + [vm] * 7,
        out_specs=(hbm, hbm, vm),
        scratch_shapes=shapes,
        compiler_params=pltpu.CompilerParams(collective_id=0, has_side_effects=True, vmem_limit_bytes=VMEM_BYTES),
    )(*args)


VMEM_BYTES = 64 * 1024 * 1024 - 1024 * 64


def finish_kernel(z, tg, out, gp, o_out, o_tg, o_in, o_ow, o_gu, o_dn, o_one, o_two, low, full, same, s_in, s_out, s_same_in, s_same_out):
    rows = FINISH_ROWS
    steps = z.T // rows

    def part(i):
        return pl.ds(i * rows, rows)

    loads = [pltpu.make_async_copy(tg.at[part(i)], low.at[part(i)], s_in.at[i]) for i in range(steps)]
    same_loads = [pltpu.make_async_copy(out.at[part(i)], same.at[part(i)], s_same_in.at[i]) for i in range(steps)]
    stores = [pltpu.make_async_copy(full.at[part(i)], o_tg.at[part(i)], s_out.at[i]) for i in range(steps)]
    same_stores = [pltpu.make_async_copy(same.at[part(i)], o_out.at[part(i)], s_same_out.at[i]) for i in range(steps)]
    for i in range(steps):
        loads[i].start()
        same_loads[i].start()
    for i in range(steps):
        loads[i].wait()
        full[part(i), :] = low[part(i), :].astype(F32)
        stores[i].start()
        same_loads[i].wait()
        same_stores[i].start()
    unpack_grads(z, gp, o_in, o_ow, o_gu, o_dn, o_one, o_two)
    for c in stores + same_stores:
        c.wait()


def unpack_grads(z, gp, o_in, o_ow, o_gu, o_dn, o_one, o_two):
    SH, QN, FN = z.SH, z.QN, z.FN
    heads = QN // HEAD_DIM
    value = gp[...][:SH]

    def flipped(x):
        a, b = x.shape
        a2, b2 = round_up(a, 128), round_up(b, 128)
        if b2 > b:
            x = jnp.concatenate([x, jnp.zeros((a, b2 - b), F32)], axis=1)
        if a2 > a:
            x = jnp.concatenate([x, jnp.zeros((a2 - a, b2), F32)], axis=0)
        return x.T[:b, :a]

    at = GAIN_LANES
    o_in[...] = jnp.concatenate(
        [value[:, at + k * QN + a * HEAD_DIM:at + k * QN + (a + 1) * HEAD_DIM] for a in range(heads) for k in range(3)], axis=1)
    at += 3 * QN
    o_ow[...] = flipped(value[:, at:at + QN])
    at += QN
    for k in range(2):
        o_gu[:, k, :] = value[:, at + k * FN:at + (k + 1) * FN]
    at += 2 * FN
    o_dn[...] = flipped(value[:, at:at + FN])
    rows = flipped(value[:, :128])
    o_one[...] = rows[0:1, :]
    o_two[...] = rows[1:2, :]


def finish(z, tg, out, gp):
    rows = FINISH_ROWS
    hbm = pl.BlockSpec(memory_space=pl.ANY)
    vm = pl.BlockSpec(memory_space=pltpu.VMEM)
    return pl.pallas_call(
        functools.partial(finish_kernel, z),
        out_shape=(
            jax.ShapeDtypeStruct((z.T, z.D), BF16),
            jax.ShapeDtypeStruct((z.T, z.D), F32),
            jax.ShapeDtypeStruct((z.SH, 3 * z.QN), F32),
            jax.ShapeDtypeStruct((z.QN, z.SH), F32),
            jax.ShapeDtypeStruct((z.SH, 2, z.FN), F32),
            jax.ShapeDtypeStruct((z.FN, z.SH), F32),
            jax.ShapeDtypeStruct((1, z.SH), F32),
            jax.ShapeDtypeStruct((1, z.SH), F32),
        ),
        in_specs=[hbm, hbm, vm],
        out_specs=(hbm, hbm) + (vm,) * 6,
        scratch_shapes=[
            pltpu.VMEM((z.T, z.D), BF16),
            pltpu.VMEM((z.T, z.D), F32),
            pltpu.VMEM((z.T, z.D), BF16),
            pltpu.SemaphoreType.DMA((z.T // rows,)),
            pltpu.SemaphoreType.DMA((z.T // rows,)),
            pltpu.SemaphoreType.DMA((z.T // rows,)),
            pltpu.SemaphoreType.DMA((z.T // rows,)),
        ],
        compiler_params=pltpu.CompilerParams(vmem_limit_bytes=VMEM_BYTES),
    )(tg, out, gp)


def per_device(tokens, lengths, masked, attention_in, attention_out, geglu_in, geglu_out, gain_attention, gain_feedforward, out_grad):
    wide, narrow = lax.axis_size("wide"), lax.axis_size("narrow")
    z = Sizes(wide, narrow, tokens.shape[0], tokens.shape[1], attention_out.shape[0] * narrow, geglu_out.shape[0] * narrow, lengths.shape[0])
    gains = [g.reshape(1, z.SH) for g in (gain_attention, gain_feedforward)]
    out, tg, gp = run_layer(
        z, lengths, tokens, out_grad, masked.reshape(-1, 128), attention_in, attention_out, geglu_in, geglu_out, *gains)
    out, tg, g_in, g_out, g_gu, g_down, one, two = finish(z, tg, out, gp)
    return (out, tg, g_in, g_out, g_gu, g_down, one.reshape(z.SH), two.reshape(z.SH))


def solution(mesh):
    return jax.shard_map(
        per_device,
        mesh=mesh,
        in_specs=(P("wide", None), P(), P("wide"), P("wide", "narrow"), P("narrow", "wide"), P("wide", None, "narrow"),
                  P("narrow", "wide"), P("wide"), P("wide"), P("wide", None)),
        out_specs=(P("wide", None), P("wide", None), P("wide", "narrow"), P("narrow", "wide"), P("wide", None, "narrow"),
                   P("narrow", "wide"), P("wide"), P("wide")),
        check_vma=False,
    )
```

```python
import functools
import itertools
import math

import jax
import jax.numpy as jnp
from jax import lax
from jax.experimental import pallas as pl
from jax.experimental.pallas import tpu as pltpu
from jax.sharding import PartitionSpec as P

MESH = pl.DeviceIdType.MESH
HEAD_DIM = 64
WINDOW = 128
HALF = WINDOW // 2
BLOCK = 128
FINISH_ROWS = 256
SPAN = BLOCK + WINDOW
GAIN_LANES = 32
EPSILON = 1e-05
THETA = 10000.0
NEG_LARGE = -1e30
F32 = jnp.float32
BF16 = jnp.bfloat16
GELU_A = math.sqrt(2.0 / math.pi)
GELU_B = 0.044715


def round_up(value, unit):
    return -(-value // unit) * unit


def dot(a, b, ca, cb):
    return lax.dot_general(a, b, (((ca,), (cb,)), ((), ())), preferred_element_type=F32)


class Sizes:
    def __init__(self, wide, narrow, tok_rows, width, heads_width, hidden, docs):
        self.W, self.N, self.T, self.D, self.F, self.docs = wide, narrow, tok_rows, width, hidden, docs
        self.R = tok_rows // narrow
        self.E = self.R + WINDOW
        self.NB = self.R // BLOCK
        self.pairs = width // 128
        self.G = next(g for g in (4 if self.R <= 512 else 2, 2, 1) if self.NB % g == 0)
        self.SH = width // wide
        self.RS = round_up(self.SH, 16)
        self.UG = next(g for g in (1, 2, 4, 8) if g * 2 * self.SH % 16 == 0)
        self.QN, self.FN = heads_width // narrow, hidden // narrow
        self.bits = (wide // 2).bit_length() - 1
        first = GAIN_LANES + 3 * self.QN
        self.real = first + self.QN + 3 * self.FN
        self.LA = round_up(first, 128)
        self.lanes = round_up(self.real, 128)
        self.O0 = self.LA - first
        cut_a = (self.LA // 256) * 128
        tiles = (self.lanes - self.LA) // 128
        end_one = self.LA + (3 * tiles // 8) * 128
        end_two = end_one + (tiles // 4) * 128
        self.cuts = [(0, cut_a), (cut_a, self.LA), (self.LA, end_one), (end_one, end_two), (end_two, self.lanes)]
        self.C = len(self.cuts)
        self.CA = 2
        self.keep = self.R <= 512 and self.SH == self.RS
        self.CZ = self.C - 1
        self.MB = min(self.R, 256)
        self.blocks = self.R // self.MB
        self.FC = 384 if hidden % 384 == 0 else hidden
        self.HT = max(1, 192 // (2 * self.SH))
        self.TM = self.HT * 2 * self.SH


def combos(bit_list):
    out = []
    for mask in range(1 << len(bit_list)):
        out.append([b for i, b in enumerate(bit_list) if mask >> i & 1])
    return out


def layer_kernel(z, names, lengths, tokens, grads_in, masked, w_in, w_out, w_gu, w_down, gain_one, gain_two, out, tg, gp, *scratch):
    s = dict(zip(names, scratch))
    W, N, T, D, F, R, E, NB = z.W, z.N, z.T, z.D, z.F, z.R, z.E, z.NB
    C, SH, RS, N2 = z.C, z.SH, z.RS, z.N // 2
    wb = [s[f"wb{c}"] for c in range(C)]
    pk, cot = s["pk"], s["cot"]
    r0 = [s[f"r0{c}"] for c in range(C)]
    r1 = [s[f"r1{c}"] for c in range(C)]
    rz = [s[f"rz{c}"] for c in range(C)]
    w, n = lax.axis_index("wide"), lax.axis_index("narrow")
    core, hi = lax.rem(w, 2), lax.div(w, 2)
    place = n + core * (N - 1 - 2 * n)
    ahead = 1 - 2 * core
    first, last = place == 0, place == N - 1
    has_prev = jnp.logical_or(place > 0, w > 0)
    has_next = jnp.logical_or(place < N - 1, w < W - 1)
    prev_dev = (jnp.where(first, w - 1, w), jnp.where(first, n, n - ahead))
    next_dev = (jnp.where(last, w + 1, w), jnp.where(last, n, n + ahead))
    at_end = jnp.logical_or(first, last)
    low_block = jnp.logical_and(at_end, w > 0)
    high_block = jnp.logical_and(at_end, w < W - 1)
    sib_dev = (w + 1 - 2 * core, n)

    def around(k):
        return lax.rem(n + k + N, N)

    def flip(value, bit_list):
        for b in bit_list:
            value = value + (1 - 2 * lax.rem(lax.div(hi, 1 << b), 2)) * (1 << b)
        return value

    def bit_dev(b):
        return (2 * flip(hi, [b]) + core, n)

    pending = []

    def copy_to(src, dst, send, recv, dev):
        return pltpu.make_async_remote_copy(src_ref=src, dst_ref=dst, send_sem=send, recv_sem=recv, device_id=dev, device_id_type=MESH)

    def send(src, dst, send_sem, recv_sem, dev):
        c = copy_to(src, dst, send_sem, recv_sem, dev)
        c.start()
        pending.append(c)

    def arrived(dst, send_sem, recv_sem, dev):
        copy_to(dst, dst, send_sem, recv_sem, dev).wait_recv()

    barrier = pltpu.get_barrier_semaphore()
    partners = [(w, around(k)) for k in range(1, N)] + [bit_dev(b) for b in range(z.bits)] + [sib_dev]
    for dev in partners:
        pl.semaphore_signal(barrier, inc=1, device_id=dev, device_id_type=MESH)

    @pl.when(low_block)
    def _():
        pl.semaphore_signal(barrier, inc=1, device_id=(w - 1, n), device_id_type=MESH)

    @pl.when(high_block)
    def _():
        pl.semaphore_signal(barrier, inc=1, device_id=(w + 1, n), device_id_type=MESH)


    def flipped(x):
        a, b = x.shape
        a2, b2 = round_up(a, 128), round_up(b, 128)
        if b2 > b:
            x = jnp.concatenate([x, jnp.zeros((a, b2 - b), F32)], axis=1)
        if a2 > a:
            x = jnp.concatenate([x, jnp.zeros((a2 - a, b2), F32)], axis=0)
        return x.T[:b, :a]

    def pack(lo, up, pieces):
        have = sum(p.shape[1] for p in pieces)
        if up - lo > have:
            pieces = pieces + [jnp.zeros((SH, up - lo - have), F32)]
        value = jnp.concatenate(pieces, axis=1)
        if RS > SH:
            value = jnp.concatenate([value, jnp.zeros((RS - SH, up - lo), F32)], axis=0)
        pk[:, lo:up] = value.astype(BF16)

    QN, FN = z.QN, z.FN
    heads = QN // HEAD_DIM
    raw_in, out_t = w_in[...], flipped(w_out[...])
    gain_rows = jnp.concatenate([gain_one[...], gain_two[...], jnp.zeros((6, SH), F32)], axis=0)
    gain_cols = jnp.concatenate([flipped(gain_rows), jnp.zeros((SH, GAIN_LANES - 8), F32)], axis=1)
    pack(0, z.LA, [gain_cols] + [raw_in[:, (3 * a + k) * HEAD_DIM:(3 * a + k + 1) * HEAD_DIM] for k in range(3) for a in range(heads)] + [out_t[:, :z.O0]])
    pl.semaphore_wait(barrier, len(partners) + low_block.astype(jnp.int32) + high_block.astype(jnp.int32))

    half_refs = [pl.ds(h * N2, N2) for h in range(2)]
    gather_order = [list(range(z.bits))[::-1], list(range(z.bits))]

    def z_start(c):
        lo, up = z.cuts[c]
        src = pk.at[:, lo:up]
        pltpu.make_async_copy(src, wb[c].at[n, hi, core], s["l_own"].at[c]).start()
        for k in range(1, N):
            send(src, wb[c].at[n, hi, core], s["zs"].at[c, k - 1], s["zr"].at[c, k - 1], (w, around(k)))

    def z_wait(c):
        lo, up = z.cuts[c]
        pltpu.make_async_copy(pk.at[:, lo:up], wb[c].at[n, hi, core], s["l_own"].at[c]).wait()
        for k in range(1, N):
            arrived(wb[c].at[around(-k), hi, core], s["zs"].at[c, k - 1], s["zr"].at[c, k - 1], (w, around(-k)))

    def s_start(c, t):
        for h in range(2):
            b = gather_order[h][t]
            for i, combo in enumerate(combos(gather_order[h][:t])):
                ref = wb[c].at[half_refs[h], flip(hi, combo), core]
                slot = (1 << t) - 1 + i
                send(ref, ref, s["ss"].at[c, h, slot], s["sr"].at[c, h, slot], bit_dev(b))

    def s_wait(c, t):
        for h in range(2):
            b = gather_order[h][t]
            for i, combo in enumerate(combos(gather_order[h][:t])):
                ref = wb[c].at[half_refs[h], flip(hi, combo + [b]), core]
                slot = (1 << t) - 1 + i
                arrived(ref, s["ss"].at[c, h, slot], s["sr"].at[c, h, slot], bit_dev(b))

    def d_start(c, late):
        for h in range(2):
            everyone = combos(gather_order[h])
            for i, combo in enumerate(everyone):
                if (i >= len(everyone) // 2) == late:
                    ref = wb[c].at[half_refs[h], flip(hi, combo), core]
                    send(ref, ref, s["ds"].at[c, h, i], s["dr"].at[c, h, i], sib_dev)

    def d_wait(c):
        for h in range(2):
            for i, combo in enumerate(combos(gather_order[h])):
                arrived(wb[c].at[half_refs[h], flip(hi, combo), 1 - core], s["ds"].at[c, h, i], s["dr"].at[c, h, i], sib_dev)

    stages = z.bits + 2

    def gather_event(c, st):
        if st == 0:
            z_wait(c)
            if c + 1 < z.CZ:
                z_start(c + 1)
        elif st <= z.bits:
            s_wait(c, st - 1)
        else:
            d_wait(c)
        if st < z.bits:
            s_start(c, st)
        if st == z.bits - 1:
            d_start(c, False)
        if st == z.bits:
            d_start(c, True)

    L = C - 1
    l_lanes = z.cuts[L][1] - z.cuts[L][0]
    half_lanes = [slice(0, round_up(l_lanes // 2, 128)), slice(round_up(l_lanes // 2, 128), l_lanes)]

    def behind(side):
        return n if side == 0 else N - 1 - n

    def l_own():
        return pltpu.make_async_copy(pk.at[:, z.cuts[L][0]:], wb[L].at[n, hi, core], s["l_own"].at[L])

    def l_start(t):
        for h in range(2):
            b = gather_order[h][t]
            for i, combo in enumerate(combos(gather_order[h][:t])):
                ref = wb[L].at[n, flip(hi, combo), core, :, half_lanes[h]]
                slot = (1 << t) - 1 + i
                send(ref, ref, s["ss"].at[L, h, slot], s["sr"].at[L, h, slot], bit_dev(b))

    def l_wait(t):
        for h in range(2):
            b = gather_order[h][t]
            for i, combo in enumerate(combos(gather_order[h][:t])):
                ref = wb[L].at[n, flip(hi, combo + [b]), core, :, half_lanes[h]]
                slot = (1 << t) - 1 + i
                arrived(ref, s["ss"].at[L, h, slot], s["sr"].at[L, h, slot], bit_dev(b))

    def hop_copy(side, k):
        step = 1 - 2 * side
        ref = wb[L].at[n - step * k, :, core]
        return copy_to(ref, ref, s["lzs"].at[side, k], s["lzr"].at[side, k], (w, n + step))

    def core_copy(side, k, whose):
        ref = wb[L].at[n - (1 - 2 * side) * k, :, whose]
        return copy_to(ref, ref, s["lds"].at[side, k], s["ldr"].at[side, k], sib_dev)

    def l_own_group():
        core_copy(0, 0, core).start()
        for side in range(2):
            @pl.when(behind(side) < N - 1)
            def _():
                hop_copy(side, 0).start()

    def l_hop(k):
        for side in range(2):
            step = 1 - 2 * side

            @pl.when(behind(side) > k)
            def _():
                arrived(wb[L].at[n - step * (k + 1), :, core], s["lzs"].at[side, k], s["lzr"].at[side, k], (w, n - step))
                core_copy(side, k + 1, core).start()

            if k + 1 < N - 1:
                @pl.when(jnp.logical_and(behind(side) > k, behind(side) < N - 1))
                def _():
                    hop_copy(side, k + 1).start()

    def l_done():
        core_copy(0, 0, 1 - core).wait_recv()
        core_copy(0, 0, core).wait_send()
        for side in range(2):
            for k in range(N - 1):
                @pl.when(behind(side) > k)
                def _():
                    core_copy(side, k + 1, 1 - core).wait_recv()
                    core_copy(side, k + 1, core).wait_send()

                @pl.when(jnp.logical_and(behind(side) >= k, behind(side) < N - 1))
                def _():
                    hop_copy(side, k).wait_send()

    steps = [[(t - st, st) for st in reversed(range(stages)) if 0 <= t - st < z.CZ] for t in range(z.CZ + stages - 1)]
    a_step = z.CA - 1 + stages - 1
    before_a = [[e for e in step if e[0] < z.CA or t < a_step - 1] for t, step in enumerate(steps[:a_step + 1])]
    after_a = [[e for e in step if e not in (before_a[t] if t <= a_step else [])] for t, step in enumerate(steps)]

    def gather_events(events):
        for c, st in events:
            gather_event(c, st)

    z_start(0)
    raw_gate, raw_up, raw_down = w_gu[:, 0, :], w_gu[:, 1, :], flipped(w_down[...])
    pack(z.LA, z.lanes, [out_t[:, z.O0:]] + [raw_gate, raw_up, raw_down])
    l_own().start()
    l_own().wait()
    l_start(0)

    xin = s["xin"]
    own = pltpu.make_async_copy(tokens.at[pl.ds(pl.multiple_of(place * R, 16), R)], xin.at[pl.ds(HALF, R)], s["l_tok"].at[0])
    own.start()
    own_cot = pltpu.make_async_copy(grads_in.at[pl.ds(pl.multiple_of(place * R, 16), R)], cot, s["l_tok"].at[3])
    own_cot.start()

    def low_copy():
        return pltpu.make_async_copy(tokens.at[pl.ds(pl.multiple_of(place * R - HALF, 16), HALF)], xin.at[pl.ds(0, HALF)], s["l_tok"].at[1])

    def high_copy():
        return pltpu.make_async_copy(tokens.at[pl.ds(pl.multiple_of(place * R + R, 16), HALF)], xin.at[pl.ds(HALF + R, HALF)], s["l_tok"].at[2])

    halo = s["halo"]

    def halo_to_next():
        return copy_to(tokens.at[pl.ds(T - HALF, HALF)], halo.at[0], s["hs"].at[0], s["hr"].at[0], (w + 1, n))

    def halo_to_prev():
        return copy_to(tokens.at[pl.ds(0, HALF)], halo.at[1], s["hs"].at[1], s["hr"].at[1], (w - 1, n))

    @pl.when(place > 0)
    def _():
        low_copy().start()

    @pl.when(place < N - 1)
    def _():
        high_copy().start()

    @pl.when(high_block)
    def _():
        halo_to_next().start()

    @pl.when(low_block)
    def _():
        halo_to_prev().start()

    @pl.when(w == 0)
    def _():
        halo[0] = jnp.zeros((HALF, D), BF16)

    @pl.when(w == W - 1)
    def _():
        halo[1] = jnp.zeros((HALF, D), BF16)

    ends, total = [], jnp.int32(0)
    for d in range(z.docs):
        total = total + lengths[d]
        ends.append(total)
    cos_t, sin_t, bias_t = s["cos"], s["sin"], s["bias"]
    lane = lax.broadcasted_iota(jnp.int32, (BLOCK, 128), 1)
    low_half = lax.rem(lane, HEAD_DIM) < HEAD_DIM // 2

    freq_lane = lax.rem(lax.broadcasted_iota(jnp.int32, (1, 128), 1), HEAD_DIM // 2)
    freq = jnp.zeros((1, 128), F32)
    for d in range(HEAD_DIM // 2):
        freq = jnp.where(freq_lane == d, F32(THETA ** (-2.0 * d / HEAD_DIM)), freq)

    def tables(spot):
        base = w * T + spot * R
        lax.fori_loop(0, E // BLOCK, functools.partial(table_rows, base), 0)
        lax.fori_loop(0, NB, functools.partial(bias_rows, base), 0)

    def table_rows(base, i, carry):
        r = pl.multiple_of(i * BLOCK, BLOCK)
        t = base - HALF + r + lax.broadcasted_iota(jnp.int32, (BLOCK, 128), 0)
        start = jnp.zeros((BLOCK, 128), jnp.int32)
        for d in range(z.docs):
            start = start + jnp.where(t >= ends[d], lengths[d], 0)
        angle = (t - start).astype(F32) * freq
        cos_t[pl.ds(r, BLOCK), :] = jnp.cos(angle)
        sine = jnp.sin(angle)
        sin_t[pl.ds(r, BLOCK), :] = jnp.where(low_half, -sine, sine)
        return carry

    def bias_rows(base, b, carry):
        tk = base - HALF + b * BLOCK + lax.broadcasted_iota(jnp.int32, (SPAN, BLOCK), 0)
        tq = base + b * BLOCK + lax.broadcasted_iota(jnp.int32, (SPAN, BLOCK), 1)
        dk = jnp.where(tk < 0, -1, 0)
        dq = jnp.zeros((SPAN, BLOCK), jnp.int32)
        for d in range(z.docs):
            dk = dk + jnp.where(tk >= ends[d], 1, 0)
            dq = dq + jnp.where(tq >= ends[d], 1, 0)
        near = jnp.abs(tk - tq) <= HALF
        bias_t[b] = jnp.where(jnp.logical_and(dk == dq, near), 0.0, NEG_LARGE).astype(F32)
        return carry

    for t in range(z.bits):
        l_wait(t)
        if t + 1 < z.bits:
            l_start(t + 1)
    gather_events(before_a[0])
    tables(place)
    gather_events(before_a[1])
    l_own_group()

    own.wait()

    @pl.when(place > 0)
    def _():
        low_copy().wait()

    @pl.when(place < N - 1)
    def _():
        high_copy().wait()

    @pl.when(low_block)
    def _():
        halo_to_next().wait_recv()
        halo_to_prev().wait_send()

    @pl.when(high_block)
    def _():
        halo_to_prev().wait_recv()
        halo_to_next().wait_send()

    @pl.when(first)
    def _():
        xin[0:HALF, :] = halo[0]

    @pl.when(last)
    def _():
        xin[HALF + R:, :] = halo[1]

    gather_events(before_a[2])
    own_cot.wait()

    def mask_rows(b, carry):
        rows = pl.ds(pl.multiple_of(b * BLOCK, BLOCK), BLOCK)
        keep = jnp.where(masked[pl.ds(place * NB + b, 1), :] == 1, 1.0, 0.0).astype(F32)
        keep = jnp.broadcast_to(keep, (BLOCK, BLOCK)).T.astype(BF16)
        cot[rows, :] = cot[rows, :] * jnp.concatenate([keep] * (D // BLOCK), axis=1)
        return carry

    lax.fori_loop(0, NB, mask_rows, 0)

    def transposed(name, src, row0):
        if not z.keep:
            return
        dst = s[name]

        def body(i, carry):
            at = pl.multiple_of(i * 128, 128)
            dst[pl.ds(at, 128), :] = src[row0:row0 + R, pl.ds(at, 128)].astype(F32).T.astype(BF16)
            return carry

        lax.fori_loop(0, D // 128, body, 0)

    transposed("ct", cot, 0)

    wqkv, wot, wg, wu, wgo = s["wqkv"], s["wot"], s["wg"], s["wu"], s["wgo"]
    gcol, grow, gsum = s["gcol"], s["grow"], s["gsum"]

    UG = z.UG
    UR = UG * 2 * SH

    def section(nn, i, lo, up):
        found = []
        for c, (a, b) in enumerate(z.cuts):
            x, y = max(lo, a), min(up, b)
            if x >= y:
                continue
            x0, y0 = (x - a) // 128 * 128, round_up(y - a, 128)
            both = [wb[c][nn, i * UG + a2, k, :, x0:y0] for a2 in range(UG) for k in range(2)]
            if SH % 16 == 0:
                v = jnp.concatenate([q[:SH] for q in both], axis=0)
            else:
                v = jnp.concatenate([q.astype(F32)[:SH] for q in both], axis=0).astype(BF16)
            found.append(v[:, x - a - x0:y - a - x0])
        return found[0] if len(found) == 1 else jnp.concatenate(found, axis=1)

    def place_columns(ref, r, at, sections):
        width = sum(v.shape[1] for v in sections)
        ref[pl.ds(r, UR), at:at + width] = jnp.concatenate(sections, axis=1)

    def unpack_query(i, carry):
        r = pl.multiple_of(i * UR, 16)
        parts = [section(nn, i, 0, GAIN_LANES + QN) for nn in range(N)]
        place_columns(wqkv, r, 0, [v[:, GAIN_LANES:] for v in parts])
        gcol[pl.ds(r, UR), :] = jnp.concatenate([parts[0][:, :GAIN_LANES].astype(F32), jnp.zeros((UR, 128 - GAIN_LANES), F32)], axis=1)
        return carry

    def unpack_a(i, carry):
        r = pl.multiple_of(i * UR, 16)
        parts = [section(nn, i, GAIN_LANES + QN, GAIN_LANES + 3 * QN) for nn in range(N)]
        for k in range(2):
            place_columns(wqkv, r, (k + 1) * D, [v[:, k * QN:(k + 1) * QN] for v in parts])
        return carry

    def normed(x):
        centred = x - jnp.mean(x, axis=-1, keepdims=True)
        rstd = lax.rsqrt(jnp.mean(centred * centred, axis=-1, keepdims=True) + EPSILON)
        return centred * rstd, rstd

    n1, qkv = s["n1"], s["qkv"]

    def norm_rows(i, carry):
        r = pl.multiple_of(i * BLOCK, BLOCK)
        hat, _ = normed(xin[pl.ds(r, BLOCK), :].astype(F32))
        n1[pl.ds(r, BLOCK), :] = (hat * grow[0:1, :]).astype(BF16)
        return carry

    def partner_lanes(x):
        lanes = lax.broadcasted_iota(jnp.int32, x.shape, 1)
        return jnp.where(lax.rem(lanes, HEAD_DIM) < HEAD_DIM // 2, pltpu.roll(x, 128 - HEAD_DIM // 2, 1), pltpu.roll(x, HEAD_DIM // 2, 1))

    def project_turned(ct, carry):
        at = pl.multiple_of(ct * 256, 128)
        y = dot(n1[...], wqkv[:, pl.ds(at, 256)], 1, 0)
        scale = jnp.where(ct < D // 256, F32(1.0 / math.sqrt(HEAD_DIM)), F32(1.0))
        for k in range(2):
            part_y = y[:, k * 128:(k + 1) * 128]
            part_y = (part_y * cos_t[...] + partner_lanes(part_y) * sin_t[...]) * scale
            qkv[:, pl.ds(pl.multiple_of(at + k * 128, 128), 128)] = part_y.astype(BF16)
        return carry

    def project(ct, carry):
        at = pl.multiple_of(2 * D + ct * 256, 128)
        qkv[:, pl.ds(at, 256)] = dot(n1[...], wqkv[:, pl.ds(at, 256)], 1, 0).astype(BF16)
        return carry

    gsum[...] = jnp.zeros((8, D), F32)

    def make_query():
        lax.fori_loop(0, E // BLOCK, norm_rows, 0)
        lax.fori_loop(0, D // 256, project_turned, 0)

    def make_key_value():
        lax.fori_loop(D // 256, 2 * D // 256, project_turned, 0)
        lax.fori_loop(0, D // 256, project, 0)

    def make_qkv():
        make_query()
        make_key_value()

    def begin_query():
        lax.fori_loop(0, W // 2 // UG, unpack_query, 0)
        grow[...] = gcol[...].T[0:8, :]
        make_query()

    early = z.cuts[0][1] >= GAIN_LANES + QN
    for t in range(3, a_step):
        for e in before_a[t]:
            gather_events([e])
            if early and e == (0, stages - 1):
                begin_query()
    l_hop(0)
    gather_events(before_a[a_step])
    if not early:
        begin_query()
    lax.fori_loop(0, W // 2 // UG, unpack_a, 0)
    for t in range(a_step):
        gather_events(after_a[t])
    if N > 2:
        l_hop(1)
    make_key_value()
    gather_events(after_a[a_step])

    att, stat = s["att"], s.get("stat")
    lane_row = lax.broadcasted_iota(jnp.int32, (BLOCK, 128), 1)
    keep_one = jnp.where(lane_row < HEAD_DIM, 1.0, 0.0).astype(BF16)
    keep_two = jnp.where(lane_row < HEAD_DIM, 0.0, 1.0).astype(BF16)

    def stacked(x):
        return jnp.concatenate([x * keep_one, x * keep_two], axis=0)

    def unstacked(x):
        return jnp.concatenate([x[:HEAD_DIM, :BLOCK], x[HEAD_DIM:, BLOCK:]], axis=0).T

    def unit_refs(j, b):
        lanes = [pl.ds(pl.multiple_of(k * D + j * 128, 128), 128) for k in range(3)]
        return lanes, pl.ds(pl.multiple_of(b * BLOCK, BLOCK), SPAN), pl.ds(pl.multiple_of(b * BLOCK + HALF, 16), BLOCK)

    def unit_scores(j, b):
        (lq, lk, lv), keys, queries = unit_refs(j, b)
        qs = stacked(qkv[queries, lq])
        kp, vp = qkv[keys, lk], qkv[keys, lv]
        pen = bias_t[b]
        return qs, kp, vp, dot(kp, qs, 1, 1) + jnp.concatenate([pen, pen], axis=1)

    G = z.G

    def attend(v, carry):
        j, g = lax.div(v, NB // G), lax.rem(v, NB // G)
        for i in range(G):
            b = g * G + i
            u = j * NB + b
            _, _, vp, scores = unit_scores(j, b)
            top = jnp.max(scores, axis=0, keepdims=True)
            weights = jnp.exp(scores - top)
            inv = 1.0 / jnp.sum(weights, axis=0, keepdims=True)
            probs = weights * inv
            if z.keep:
                s["kept"][u] = probs
            else:
                stat[u, 0:1, :] = top
                stat[u, 1:2, :] = inv
            got = unstacked(dot(vp, probs.astype(BF16), 0, 0))
            att[pl.ds(pl.multiple_of(b * BLOCK, BLOCK), BLOCK), pl.ds(pl.multiple_of(j * 128, 128), 128)] = got.astype(BF16)
        return carry

    def attend_part(lo, up):
        lax.fori_loop(lo * (NB // G), up * (NB // G), attend, 0)

    half_pairs = z.pairs // 2
    third = z.pairs // 3
    attend_part(0, third)
    for k in range(2, N - 1):
        l_hop(k)
    attend_part(third, 2 * third)
    gather_events(after_a[a_step + 1])
    attend_part(2 * third, z.pairs)
    for t in range(a_step + 2, len(steps)):
        gather_events(after_a[t])

    slices_at = GAIN_LANES + 4 * QN

    def unpack_first(i, carry):
        r = pl.multiple_of(i * UR, 16)
        lo = GAIN_LANES + 3 * QN
        parts = [section(nn, i, lo, slices_at + FN) for nn in range(N)]
        place_columns(wot, r, 0, [v[:, :QN] for v in parts])
        place_columns(wg, r, 0, [v[:, QN:] for v in parts])
        return carry

    def unpack_second(i, carry):
        r = pl.multiple_of(i * UR, 16)
        parts = [section(nn, i, slices_at + FN, slices_at + 3 * FN) for nn in range(N)]
        place_columns(wu, r, 0, [v[:, :FN] for v in parts])
        place_columns(wgo, r, 0, [v[:, FN:] for v in parts])
        return carry

    lax.fori_loop(0, W // 2 // UG, unpack_first, 0)
    l_done()
    lax.fori_loop(0, W // 2 // UG, unpack_second, 0)

    ost, n2, res, resg = s["ost"], s["n2"], s["resr"], s["resg"]
    hid, dgate, dup, datt = s["hid"], s["dgate"], s["dup"], s["datt"]
    MB, FC = z.MB, z.FC

    def norm_back(hat, rstd, e, gain):
        eg = e * gain
        return rstd * (eg - jnp.mean(eg, axis=-1, keepdims=True) - hat * jnp.mean(eg * hat, axis=-1, keepdims=True))

    def line_rows(dest, m, rb):
        theirs = m + core * (N - 1 - 2 * m)
        return dest.at[pl.ds(pl.multiple_of(theirs * R + rb * MB, 16), MB)]

    def line_copy(dest, rb, key, side, k, stage=None):
        step = 1 - 2 * side
        ref = line_rows(dest, n - step * k, rb)
        src = ref if stage is None else stage.at[pl.ds(pl.multiple_of(rb * MB, 16), MB)]
        return copy_to(src, ref, s[key + "s"].at[rb, side, k], s[key + "r"].at[rb, side, k], (w, n + step))

    def own_copy(stage, dest, rb, key):
        return pltpu.make_async_copy(stage.at[pl.ds(pl.multiple_of(rb * MB, 16), MB)], line_rows(dest, n, rb), s[key + "l"].at[rb])

    def token_send(stage, dest, rb, key):
        own_copy(stage, dest, rb, key).start()
        for side in range(2):
            @pl.when(behind(side) < N - 1)
            def _():
                line_copy(dest, rb, key, side, 0, stage).start()

    hops = {"o": N - 2 if N > 2 else N - 1, "t": N - 1}

    def token_forward(dest, key, k):
        if k > hops[key]:
            return

        def body(rb, carry):
            for side in range(2):
                step = 1 - 2 * side

                @pl.when(behind(side) >= k)
                def _():
                    arrived(line_rows(dest, n - step * k, rb), s[key + "s"].at[rb, side, k - 1], s[key + "r"].at[rb, side, k - 1], (w, n - step))

                if k < hops[key]:
                    @pl.when(jnp.logical_and(behind(side) >= k, behind(side) < N - 1))
                    def _():
                        line_copy(dest, rb, key, side, k).start()
            return carry

        lax.fori_loop(0, z.blocks, body, 0)

    def token_sent(stage, dest, key, lo, up):
        def body(rb, carry):
            if lo == 0:
                own_copy(stage, dest, rb, key).wait()
            for side in range(2):
                for k in range(lo, up):
                    @pl.when(jnp.logical_and(behind(side) >= k, behind(side) < N - 1))
                    def _():
                        line_copy(dest, rb, key, side, k).wait_send()
            return carry

        lax.fori_loop(0, z.blocks, body, 0)

    def feed(rb, carry):
        r = pl.multiple_of(rb * MB, 16)
        rows = pl.ds(r, MB)
        x = xin[pl.ds(pl.multiple_of(rb * MB + HALF, 16), MB), :].astype(F32)
        residual = x + dot(att[rows, :], wot[...], 1, 1)
        hat, rstd = normed(residual)
        gain = grow[1:2, :]
        n2v = (hat * gain).astype(BF16)
        n2[rows, :] = n2v
        cotv = cot[rows, :]
        total_out, e = residual, None
        for f in range(0, F, FC):
            gate = dot(n2v, wg[:, f:f + FC], 1, 0)
            upv = dot(n2v, wu[:, f:f + FC], 1, 0)
            dh = dot(cotv, wgo[:, f:f + FC], 1, 0)
            sq = gate * gate
            th = jnp.tanh(GELU_A * (gate * (1.0 + GELU_B * sq)))
            half = 0.5 * (1.0 + th)
            act = gate * half
            slope = half + (0.5 * GELU_A) * gate * (1.0 - th * th) * (1.0 + (3.0 * GELU_B) * sq)
            hv = (act * upv).astype(BF16)
            dgv = (dh * upv * slope).astype(BF16)
            duv = (dh * act).astype(BF16)
            hid[rows, f:f + FC] = hv
            dgate[rows, f:f + FC] = dgv
            dup[rows, f:f + FC] = duv
            total_out = total_out + dot(hv, wgo[:, f:f + FC], 1, 1)
            more = dot(dgv, wg[:, f:f + FC], 1, 1) + dot(duv, wu[:, f:f + FC], 1, 1)
            e = more if e is None else e + more
        ost[rows, :] = total_out.astype(BF16)
        token_send(ost, out, rb, "o")
        gsum[1:2, :] = gsum[1:2, :] + jnp.sum(e * hat, axis=0, keepdims=True)
        grad = cotv.astype(F32) + norm_back(hat, rstd, e, gain)
        resg[rows, :] = grad
        low = grad.astype(BF16)
        res[rows, :] = low
        datt[rows, :] = dot(low, wot[...], 1, 0).astype(BF16)
        return carry

    lax.fori_loop(0, z.blocks, feed, 0)

    for c in pending:
        c.wait_send()
    pending.clear()

    def store_rows(c, nn, i, k, value):
        if RS > SH:
            value = jnp.concatenate([value, jnp.zeros((RS - SH, value.shape[1]), F32)], axis=0)
        wb[c][nn, i, k] = value.astype(BF16)

    HT, TM = z.HT, z.TM
    owx = s["owx"]

    def store_part(chunks, nn, t, value):
        lo = z.cuts[chunks[0]][0]
        for c in chunks:
            a, b = z.cuts[c]
            for i in range(HT):
                for k in range(2):
                    at = (2 * i + k) * SH
                    store_rows(c, nn, t * HT + i, k, value[at:at + SH, a - lo:b - lo])

    def turned_dot(name, src, row0, t, rhs):
        if z.keep:
            return dot(s[name][pl.ds(pl.multiple_of(t * TM, 16), TM), :], rhs, 1, 0)
        return dot(src[row0:row0 + R, t * TM:(t + 1) * TM], rhs, 0, 0)

    def tiles(body):
        if z.keep:
            lax.fori_loop(0, D // TM, body, 0)
        else:
            for t in range(D // TM):
                body(t, 0)

    def grads_b(t, carry):
        r = pl.multiple_of(t * TM, 16)
        gg = turned_dot("n2t", n2, 0, t, dgate[...])
        gu = turned_dot("n2t", n2, 0, t, dup[...])
        go = turned_dot("ct", cot, 0, t, hid[...])
        gw = turned_dot("rt", res, 0, t, att[...])
        if z.O0:
            firsts = [gw[:, nn * QN:nn * QN + z.O0] for nn in range(N)]
            spare = owx.shape[1] - N * z.O0
            if spare:
                firsts.append(jnp.zeros((TM, spare), F32))
            owx[pl.ds(r, TM), :] = jnp.concatenate(firsts, axis=1)
        for nn in range(N):
            pieces = [gw[:, nn * QN + z.O0:(nn + 1) * QN]] + [v[:, nn * FN:(nn + 1) * FN] for v in (gg, gu, go)]
            if z.lanes > z.real:
                pieces.append(jnp.zeros((TM, z.lanes - z.real), F32))
            store_part(list(range(z.CA, C)), nn, t, jnp.concatenate(pieces, axis=1))
        return carry

    scatter_order = [list(range(z.bits)), list(range(z.bits))[::-1]]

    def slot_base(t):
        return sum(1 << (z.bits - 1 - u) for u in range(t))

    def r0_start(c):
        send(wb[c].at[:, :, 1 - core], r0[c], s["g0s"].at[c], s["g0r"].at[c], sib_dev)

    def r0_finish(c):
        arrived(r0[c], s["g0s"].at[c], s["g0r"].at[c], sib_dev)

        def body(i, carry):
            for nn in range(N):
                wb[c][nn, i, core] = (wb[c][nn, i, core].astype(F32) + r0[c][nn, i].astype(F32)).astype(BF16)
            return carry

        lax.fori_loop(0, W // 2, body, 0)

    def r1_start(c, t):
        for h in range(2):
            b = scatter_order[h][t]
            for i, combo in enumerate(combos(scatter_order[h][t + 1:])):
                slot = slot_base(t) + i
                send(wb[c].at[half_refs[h], flip(hi, combo + [b]), core], r1[c].at[h, slot], s["g1s"].at[c, h, slot], s["g1r"].at[c, h, slot], bit_dev(b))

    def r1_finish(c, t):
        for h in range(2):
            b = scatter_order[h][t]
            for i, combo in enumerate(combos(scatter_order[h][t + 1:])):
                slot = slot_base(t) + i
                arrived(r1[c].at[h, slot], s["g1s"].at[c, h, slot], s["g1r"].at[c, h, slot], bit_dev(b))
                hv = flip(hi, combo)
                for nn in range(N2):
                    at = h * N2 + nn
                    wb[c][at, hv, core] = (wb[c][at, hv, core].astype(F32) + r1[c][h, slot, nn].astype(F32)).astype(BF16)

    def rz_copy(c, side, d):
        step = 1 - 2 * side
        return copy_to(wb[c].at[n + step * (1 + d), hi, core], rz[c].at[side, d], s["g2s"].at[c, side, d], s["g2r"].at[c, side, d], (w, n + step))

    def rz_round(c, r):
        for side in range(2):
            step = 1 - 2 * side

            @pl.when(behind(side) == r)
            def _():
                for d in reversed(range(N - r)):
                    if r > 0:
                        arrived(rz[c].at[side, d], s["g2s"].at[c, side, d], s["g2r"].at[c, side, d], (w, n - step))
                        if d > 0:
                            m = n + step * d
                            wb[c][m, hi, core] = (wb[c][m, hi, core].astype(F32) + rz[c][side, d].astype(F32)).astype(BF16)
                    if d > 0:
                        rz_copy(c, side, d - 1).start()

    def rz_sent(c):
        for side in range(2):
            for r in range(N - 1):
                @pl.when(behind(side) == r)
                def _():
                    for d in range(N - 1 - r):
                        rz_copy(c, side, d).wait_send()

    def rz_finish(c):
        lo, up = z.cuts[c]
        gp[:, lo:up] = wb[c][n, hi, core].astype(F32)
        for side in range(2):
            @pl.when(behind(side) > 0)
            def _():
                gp[:, lo:up] = gp[:, lo:up] + rz[c][side, 0].astype(F32)

    last_stage = z.bits + 1 + N

    def scatter_advance(chunks, st):
        for c in chunks:
            if st == 0:
                r0_start(c)
            elif st <= z.bits + 1:
                if st == 1:
                    r0_finish(c)
                else:
                    r1_finish(c, st - 2)
                if st <= z.bits:
                    r1_start(c, st - 1)
                else:
                    rz_round(c, 0)
            else:
                rz_round(c, st - z.bits - 1)
                if st == last_stage - 1:
                    rz_finish(c)

    part_a, part_b = list(range(z.CA)), list(range(z.CA, C))
    transposed("n2t", n2, 0)
    transposed("rt", res, 0)
    tiles(grads_b)

    scatter_advance(part_b, 0)

    dkv, edge, rim, rimr = s["dkv"], s["edge"], s["rim"], s["rimr"]
    dk_ref, dv_ref = dkv.at[0], dkv.at[1]

    def attend_back(j, carry):
        dkv[:, 0:BLOCK, :] = jnp.zeros((2, BLOCK, 128), F32)

        def group(g, inner):
            tails = None
            for i in range(G):
                b = g * G + i
                u = j * NB + b
                (lq, lk, lv), keys, queries = unit_refs(j, b)
                if z.keep:
                    qs, kp, vp = stacked(qkv[queries, lq]), qkv[keys, lk], qkv[keys, lv]
                    probs = s["kept"][u]
                else:
                    qs, kp, vp, scores = unit_scores(j, b)
                    probs = jnp.exp(scores - stat[u, 0:1, :]) * stat[u, 1:2, :]
                gs = stacked(datt[pl.ds(pl.multiple_of(b * BLOCK, BLOCK), BLOCK), pl.ds(pl.multiple_of(j * 128, 128), 128)])
                prob_grad = dot(vp, gs, 1, 1)
                row_dot = jnp.sum(probs * prob_grad, axis=0, keepdims=True)
                score_grad = (probs * (prob_grad - row_dot)).astype(BF16)
                parts = (dot(score_grad, qs, 1, 0), dot(probs.astype(BF16), gs, 1, 0))
                dq = unstacked(dot(kp, score_grad, 0, 0)) * F32(1.0 / math.sqrt(HEAD_DIM))
                dq = dq * cos_t[queries, :] - partner_lanes(dq) * sin_t[queries, :]
                qkv[queries, lq] = dq.astype(BF16)
                here = pl.ds(pl.multiple_of(b * BLOCK, BLOCK), BLOCK)
                for k in range(2):
                    before = dkv[k, here, :] if tails is None else tails[k]
                    dkv[k, here, :] = before + parts[k][:BLOCK]
                tails = [x[BLOCK:] for x in parts]
            after = pl.ds(pl.multiple_of(g * G * BLOCK + G * BLOCK, BLOCK), BLOCK)
            for k in range(2):
                dkv[k, after, :] = tails[k]
            return inner

        lax.fori_loop(0, NB // G, group, 0)
        (_, lk, lv), _, _ = unit_refs(j, 0)
        lj = pl.ds(pl.multiple_of(j * 128, 128), 128)
        for k, ref in enumerate((dk_ref, dv_ref)):
            wide_lanes = pl.ds(pl.multiple_of(k * D + j * 128, 128), 128)
            rim[0, :, wide_lanes] = ref[0:HALF, :].astype(BF16)
            rim[1, :, wide_lanes] = ref[E - HALF:, :].astype(BF16)
            edge[0, :, wide_lanes] = ref[HALF:WINDOW, :]
            edge[1, :, wide_lanes] = ref[R:R + HALF, :]
        mid = slice(HALF, HALF + R)
        dk = dk_ref[mid, :]
        qkv[mid, lk] = (dk * cos_t[mid, :] - partner_lanes(dk) * sin_t[mid, :]).astype(BF16)
        qkv[mid, lv] = dv_ref[mid, :].astype(BF16)
        return carry

    lax.fori_loop(0, third, attend_back, 0)
    token_forward(out, "o", 1)
    lax.fori_loop(third, 2 * third, attend_back, 0)
    scatter_advance(part_b, 1)
    lax.fori_loop(2 * third, z.pairs, attend_back, 0)

    def rim_to_prev():
        return copy_to(rim.at[0], rimr.at[1], s["rs"].at[0], s["rr"].at[1], prev_dev)

    def rim_to_next():
        return copy_to(rim.at[1], rimr.at[0], s["rs"].at[1], s["rr"].at[0], next_dev)

    @pl.when(has_prev)
    def _():
        rim_to_prev().start()

    @pl.when(has_next)
    def _():
        rim_to_next().start()

    @pl.when(jnp.logical_not(has_prev))
    def _():
        rimr[0] = jnp.zeros((HALF, 2 * D), BF16)

    @pl.when(jnp.logical_not(has_next))
    def _():
        rimr[1] = jnp.zeros((HALF, 2 * D), BF16)

    transposed("rt", n1, HALF)

    @pl.when(has_prev)
    def _():
        rim_to_next().wait_recv()

    @pl.when(has_next)
    def _():
        rim_to_prev().wait_recv()

    @pl.when(has_prev)
    def _():
        rim_to_prev().wait_send()

    @pl.when(has_next)
    def _():
        rim_to_next().wait_send()

    for side, row in ((0, HALF), (1, R)):
        rows = slice(row, row + HALF)
        for j in range(z.pairs):
            lk = slice(j * 128, (j + 1) * 128)
            lv = slice(D + j * 128, D + (j + 1) * 128)
            dk = edge[side, :, lk] + rimr[side, :, lk].astype(F32)
            dv = edge[side, :, lv] + rimr[side, :, lv].astype(F32)
            dk = dk * cos_t[rows, :] - partner_lanes(dk) * sin_t[rows, :]
            qkv[rows, D + j * 128:D + (j + 1) * 128] = dk.astype(BF16)
            qkv[rows, 2 * D + j * 128:2 * D + (j + 1) * 128] = dv.astype(BF16)

    tst = n2

    def input_grad(rb, carry):
        rows = pl.ds(pl.multiple_of(rb * MB, 16), MB)
        ext = pl.ds(pl.multiple_of(rb * MB + HALF, 16), MB)
        e = dot(qkv[ext, :], wqkv[...], 1, 1)
        hat, rstd = normed(xin[ext, :].astype(F32))
        gsum[0:1, :] = gsum[0:1, :] + jnp.sum(e * hat, axis=0, keepdims=True)
        tst[rows, :] = (resg[rows, :] + norm_back(hat, rstd, e, grow[0:1, :])).astype(BF16)
        token_send(tst, tg, rb, "t")
        return carry

    lax.fori_loop(0, z.blocks, input_grad, 0)

    gcol[...] = jnp.concatenate([gsum[...], jnp.zeros((120, D), F32)], axis=0).T

    def grads_a(t, carry):
        r = pl.multiple_of(t * TM, 16)
        g = [turned_dot("rt", n1, HALF, t, qkv[HALF:HALF + R, k * D:(k + 1) * D]) for k in range(3)]
        gains = gcol[pl.ds(r, TM), 0:GAIN_LANES]
        for nn in range(N):
            pieces = [gains] + [v[:, nn * QN:(nn + 1) * QN] for v in g]
            if z.O0:
                pieces.append(owx[pl.ds(r, TM), nn * z.O0:(nn + 1) * z.O0])
            store_part(part_a, nn, t, jnp.concatenate(pieces, axis=1))
        return carry

    tiles(grads_a)
    scatter_advance(part_a, 0)
    scatter_advance(part_b, 2)
    token_sent(ost, out, "o", 0, 1)

    far = N - 1 - place

    def far_rows():
        return pltpu.make_async_copy(tokens.at[pl.ds(pl.multiple_of(far * R, 16), R)], xin.at[pl.ds(HALF, R)], s["l_tok"].at[0])

    def far_low():
        return pltpu.make_async_copy(tokens.at[pl.ds(T - R - HALF, HALF)], xin.at[pl.ds(0, HALF)], s["l_tok"].at[1])

    def far_high():
        return pltpu.make_async_copy(tokens.at[pl.ds(R, HALF)], xin.at[pl.ds(HALF + R, HALF)], s["l_tok"].at[2])

    def far_feed(rb, carry):
        r = pl.multiple_of(rb * MB, 16)
        rows = pl.ds(r, MB)
        x = xin[pl.ds(pl.multiple_of(rb * MB + HALF, 16), MB), :].astype(F32)
        residual = x + dot(att[rows, :], wot[...], 1, 1)
        n2v = (normed(residual)[0] * grow[1:2, :]).astype(BF16)
        total_out = residual
        for f in range(0, F, FC):
            gate = dot(n2v, wg[:, f:f + FC], 1, 0)
            upv = dot(n2v, wu[:, f:f + FC], 1, 0)
            act = gate * (0.5 * (1.0 + jnp.tanh(GELU_A * (gate * (1.0 + GELU_B * (gate * gate))))))
            total_out = total_out + dot((act * upv).astype(BF16), wgo[:, f:f + FC], 1, 1)
        ost[rows, :] = total_out.astype(BF16)
        return carry

    def far_out():
        return pltpu.make_async_copy(ost, out.at[pl.ds(pl.multiple_of(far * R, 16), R)], s["ol"].at[0])

    def far_project():
        far_rows().start()

        @pl.when(first)
        def _():
            far_low().start()
            xin[HALF + R:, :] = halo[1]

        @pl.when(last)
        def _():
            far_high().start()
            xin[0:HALF, :] = halo[0]

        tables(far)
        far_rows().wait()

        @pl.when(first)
        def _():
            far_low().wait()

        @pl.when(last)
        def _():
            far_high().wait()

        make_qkv()

    def far_finish():
        lax.fori_loop(0, z.blocks, far_feed, 0)
        far_out().start()
        far_out().wait()

    def at_ends(work):
        if N > 2:
            pl.when(at_end)(work)

    at_ends(far_project)
    scatter_advance(part_a, 1)
    token_forward(tg, "t", 1)
    for st in range(3, z.bits + 2):
        scatter_advance(part_b, st)
    at_ends(functools.partial(attend_part, 0, half_pairs))
    at_ends(functools.partial(attend_part, half_pairs, z.pairs))
    scatter_advance(part_a, 2)
    at_ends(far_finish)
    for st in range(3, z.bits + 2):
        scatter_advance(part_a, st)
    for k in range(2, N):
        token_forward(out, "o", k)
    if N > 2:
        token_forward(tg, "t", 2)
    for st in range(z.bits + 2, last_stage):
        scatter_advance(part_b, st)
        scatter_advance(part_a, st)
    for k in range(3, N):
        token_forward(tg, "t", k)

    for c in pending:
        c.wait_send()
    for c in range(C):
        rz_sent(c)
    token_sent(ost, out, "o", 1, hops["o"])
    token_sent(tst, tg, "t", 0, hops["t"])


def run_layer(z, *args):
    shapes, names = [], []

    def vmem(name, shape, dtype):
        names.append(name)
        shapes.append(pltpu.VMEM(shape, dtype))

    def sems(name, *shape):
        names.append(name)
        shapes.append(pltpu.SemaphoreType.DMA(shape))

    W, N, D, F, R, E, C = z.W, z.N, z.D, z.F, z.R, z.E, z.C
    for c, (lo, up) in enumerate(z.cuts):
        vmem(f"wb{c}", (N, W // 2, 2, z.RS, up - lo), BF16)
        vmem(f"r0{c}", (N, W // 2, z.RS, up - lo), BF16)
        vmem(f"r1{c}", (2, W // 2 - 1, N // 2, z.RS, up - lo), BF16)
        vmem(f"rz{c}", (2, N - 1, z.RS, up - lo), BF16)
    vmem("xin", (E, D), BF16)
    vmem("halo", (2, HALF, D), BF16)
    vmem("n1", (E, D), BF16)
    vmem("qkv", (E, 3 * D), BF16)
    vmem("wqkv", (D, 3 * D), BF16)
    vmem("wot", (D, D), BF16)
    for name in ("wg", "wu", "wgo"):
        vmem(name, (D, F), BF16)
    vmem("gcol", (D, 128), F32)
    vmem("grow", (8, D), F32)
    vmem("gsum", (8, D), F32)
    vmem("owx", (D, round_up(max(N * z.O0, 1), 128)), F32)
    vmem("cos", (E, 128), F32)
    vmem("sin", (E, 128), F32)
    vmem("bias", (z.NB, SPAN, BLOCK), F32)
    if z.keep:
        vmem("kept", (z.pairs * z.NB, SPAN, 2 * BLOCK), F32)
    else:
        vmem("stat", (z.pairs * z.NB, 8, 2 * BLOCK), F32)
    vmem("pk", (z.RS, z.lanes), BF16)
    for name in ("att", "ost", "n2", "resr", "datt", "cot"):
        vmem(name, (R, D), BF16)
    if z.keep:
        for name in ("n2t", "ct", "rt"):
            vmem(name, (D, R), BF16)
    vmem("resg", (R, D), F32)
    for name in ("hid", "dgate", "dup"):
        vmem(name, (R, F), BF16)
    vmem("dkv", (2, E, 128), F32)
    vmem("edge", (2, HALF, 2 * D), F32)
    vmem("rim", (2, HALF, 2 * D), BF16)
    vmem("rimr", (2, HALF, 2 * D), BF16)
    sems("l_own", C)
    sems("l_tok", 4)
    for name in ("zs", "zr"):
        sems(name, C, N - 1)
    for name in ("g2s", "g2r"):
        sems(name, C, 2, N - 1)
    for name in ("ss", "sr", "g1s", "g1r"):
        sems(name, C, 2, W // 2 - 1)
    for name in ("ds", "dr"):
        sems(name, C, 2, W // 2)
    for name in ("g0s", "g0r"):
        sems(name, C)
    for name in ("hs", "hr", "rs", "rr"):
        sems(name, 2)
    for name in ("lzs", "lzr"):
        sems(name, 2, N - 1)
    for name in ("lds", "ldr"):
        sems(name, 2, N)
    for name in ("ol", "tl"):
        sems(name, z.blocks)
    for name in ("os", "or", "ts", "tr"):
        sems(name, z.blocks, 2, N - 1)
    hbm = pl.BlockSpec(memory_space=pl.ANY)
    vm = pl.BlockSpec(memory_space=pltpu.VMEM)
    return pl.pallas_call(
        functools.partial(layer_kernel, z, names),
        out_shape=(
            jax.ShapeDtypeStruct((z.T, D), BF16),
            jax.ShapeDtypeStruct((z.T, D), BF16),
            jax.ShapeDtypeStruct((z.RS, z.lanes), F32),
        ),
        in_specs=[pl.BlockSpec(memory_space=pltpu.SMEM), hbm, hbm] + [vm] * 7,
        out_specs=(hbm, hbm, vm),
        scratch_shapes=shapes,
        compiler_params=pltpu.CompilerParams(collective_id=0, has_side_effects=True, vmem_limit_bytes=VMEM_BYTES),
    )(*args)


VMEM_BYTES = 64 * 1024 * 1024 - 1024 * 64


def finish_kernel(z, tg, out, gp, o_out, o_tg, o_in, o_ow, o_gu, o_dn, o_one, o_two, low, full, same, s_in, s_out, s_same_in, s_same_out):
    rows = FINISH_ROWS
    steps = z.T // rows

    def part(i):
        return pl.ds(i * rows, rows)

    loads = [pltpu.make_async_copy(tg.at[part(i)], low.at[part(i)], s_in.at[i]) for i in range(steps)]
    same_loads = [pltpu.make_async_copy(out.at[part(i)], same.at[part(i)], s_same_in.at[i]) for i in range(steps)]
    stores = [pltpu.make_async_copy(full.at[part(i)], o_tg.at[part(i)], s_out.at[i]) for i in range(steps)]
    same_stores = [pltpu.make_async_copy(same.at[part(i)], o_out.at[part(i)], s_same_out.at[i]) for i in range(steps)]
    for i in range(steps):
        loads[i].start()
        same_loads[i].start()
    for i in range(steps):
        loads[i].wait()
        full[part(i), :] = low[part(i), :].astype(F32)
        stores[i].start()
        same_loads[i].wait()
        same_stores[i].start()
    unpack_grads(z, gp, o_in, o_ow, o_gu, o_dn, o_one, o_two)
    for c in stores + same_stores:
        c.wait()


def unpack_grads(z, gp, o_in, o_ow, o_gu, o_dn, o_one, o_two):
    SH, QN, FN = z.SH, z.QN, z.FN
    heads = QN // HEAD_DIM
    value = gp[...][:SH]

    def flipped(x):
        a, b = x.shape
        a2, b2 = round_up(a, 128), round_up(b, 128)
        if b2 > b:
            x = jnp.concatenate([x, jnp.zeros((a, b2 - b), F32)], axis=1)
        if a2 > a:
            x = jnp.concatenate([x, jnp.zeros((a2 - a, b2), F32)], axis=0)
        return x.T[:b, :a]

    at = GAIN_LANES
    o_in[...] = jnp.concatenate(
        [value[:, at + k * QN + a * HEAD_DIM:at + k * QN + (a + 1) * HEAD_DIM] for a in range(heads) for k in range(3)], axis=1)
    at += 3 * QN
    o_ow[...] = flipped(value[:, at:at + QN])
    at += QN
    for k in range(2):
        o_gu[:, k, :] = value[:, at + k * FN:at + (k + 1) * FN]
    at += 2 * FN
    o_dn[...] = flipped(value[:, at:at + FN])
    rows = flipped(value[:, :128])
    o_one[...] = rows[0:1, :]
    o_two[...] = rows[1:2, :]


def finish(z, tg, out, gp):
    rows = FINISH_ROWS
    hbm = pl.BlockSpec(memory_space=pl.ANY)
    vm = pl.BlockSpec(memory_space=pltpu.VMEM)
    return pl.pallas_call(
        functools.partial(finish_kernel, z),
        out_shape=(
            jax.ShapeDtypeStruct((z.T, z.D), BF16),
            jax.ShapeDtypeStruct((z.T, z.D), F32),
            jax.ShapeDtypeStruct((z.SH, 3 * z.QN), F32),
            jax.ShapeDtypeStruct((z.QN, z.SH), F32),
            jax.ShapeDtypeStruct((z.SH, 2, z.FN), F32),
            jax.ShapeDtypeStruct((z.FN, z.SH), F32),
            jax.ShapeDtypeStruct((1, z.SH), F32),
            jax.ShapeDtypeStruct((1, z.SH), F32),
        ),
        in_specs=[hbm, hbm, vm],
        out_specs=(hbm, hbm) + (vm,) * 6,
        scratch_shapes=[
            pltpu.VMEM((z.T, z.D), BF16),
            pltpu.VMEM((z.T, z.D), F32),
            pltpu.VMEM((z.T, z.D), BF16),
            pltpu.SemaphoreType.DMA((z.T // rows,)),
            pltpu.SemaphoreType.DMA((z.T // rows,)),
            pltpu.SemaphoreType.DMA((z.T // rows,)),
            pltpu.SemaphoreType.DMA((z.T // rows,)),
        ],
        compiler_params=pltpu.CompilerParams(vmem_limit_bytes=VMEM_BYTES),
    )(tg, out, gp)


def per_device(tokens, lengths, masked, attention_in, attention_out, geglu_in, geglu_out, gain_attention, gain_feedforward, out_grad):
    wide, narrow = lax.axis_size("wide"), lax.axis_size("narrow")
    z = Sizes(wide, narrow, tokens.shape[0], tokens.shape[1], attention_out.shape[0] * narrow, geglu_out.shape[0] * narrow, lengths.shape[0])
    gains = [g.reshape(1, z.SH) for g in (gain_attention, gain_feedforward)]
    out, tg, gp = run_layer(
        z, lengths, tokens, out_grad, masked.reshape(-1, 128), attention_in, attention_out, geglu_in, geglu_out, *gains)
    out, tg, g_in, g_out, g_gu, g_down, one, two = finish(z, tg, out, gp)
    return (out, tg, g_in, g_out, g_gu, g_down, one.reshape(z.SH), two.reshape(z.SH))


def solution(mesh):
    return jax.shard_map(
        per_device,
        mesh=mesh,
        in_specs=(P("wide", None), P(), P("wide"), P("wide", "narrow"), P("narrow", "wide"), P("wide", None, "narrow"),
                  P("narrow", "wide"), P("wide"), P("wide"), P("wide", None)),
        out_specs=(P("wide", None), P("wide", None), P("wide", "narrow"), P("narrow", "wide"), P("wide", None, "narrow"),
                   P("narrow", "wide"), P("wide"), P("wide")),
        check_vma=False,
    )
```
